32 devices in a mesh: ctx: 16 (over z, y, x), fsdp: 2 (over core).
Axes of the slice: x: 2, y: 2, z: 4, core: 2. Of those that a mesh axis runs over, the one named last changes fastest.
Arguments:
- tokens_in: bfloat16 [4096, 2304], P(('ctx', 'fsdp')), may hold values from -6 to 6
- block_table: int32 [128], replicated, may hold values from 0 to 127, as said below
- w_query: float32 [2304, 2048], P(('ctx', 'fsdp')), may hold values from -0.21875 to 0.21875
- w_key: float32 [2304, 1024], P(('ctx', 'fsdp')), may hold values from -0.21875 to 0.21875
- w_value: float32 [2304, 1024], P(('ctx', 'fsdp')), may hold values from -0.125 to 0.125
- w_output: float32 [2048, 2304], P(None, ('ctx', 'fsdp')), may hold values from -0.125 to 0.125
- w_gate: float32 [2304, 9216], P(None, ('ctx', 'fsdp')), may hold values from -0.125 to 0.125
- w_up: float32 [2304, 9216], P(None, ('ctx', 'fsdp')), may hold values from -0.125 to 0.125
- w_down: float32 [9216, 2304], P(('ctx', 'fsdp')), may hold values from -0.0625 to 0.0625
- gain_attn_in: float32 [2304], P(('ctx', 'fsdp')), may hold values from 0.5 to 1.5
- gain_attn_out: float32 [2304], P(('ctx', 'fsdp')), may hold values from 0.5 to 1.5
- gain_ffn_in: float32 [2304], P(('ctx', 'fsdp')), may hold values from 0.5 to 1.5
- gain_ffn_out: float32 [2304], P(('ctx', 'fsdp')), may hold values from 0.5 to 1.5
- cotangent: bfloat16 [4096, 2304], P(('ctx', 'fsdp')), may hold values from -6 to 6
Outputs:
- layer_out: bfloat16 [4096, 2304], P(('ctx', 'fsdp'))
- grad_in: bfloat16 [4096, 2304], P(('ctx', 'fsdp'))
- grad_query: float32 [2304, 2048], P(('ctx', 'fsdp'))
- grad_key: float32 [2304, 1024], P(('ctx', 'fsdp'))
- grad_value: float32 [2304, 1024], P(('ctx', 'fsdp'))
- grad_output: float32 [2048, 2304], P(None, ('ctx', 'fsdp'))
- grad_gate: float32 [2304, 9216], P(None, ('ctx', 'fsdp'))
- grad_up: float32 [2304, 9216], P(None, ('ctx', 'fsdp'))
- grad_down: float32 [9216, 2304], P(('ctx', 'fsdp'))
- grad_gain_attn_in: float32 [2304], P(('ctx', 'fsdp'))
- grad_gain_attn_out: float32 [2304], P(('ctx', 'fsdp'))
- grad_gain_ffn_in: float32 [2304], P(('ctx', 'fsdp'))
- grad_gain_ffn_out: float32 [2304], P(('ctx', 'fsdp'))
The draws below stay inside these ranges and needn't reach their ends.
Inputs may be any that keep to these rules, and one draw needn't show every extreme that they name: `block_table`: A permutation of the 128 natural blocks of 32 tokens (block b holds natural tokens b * 32 to b * 32 + 31). Device i along ctx+fsdp holds stored blocks 4 i to 4 i + 3: a block p of the prompt's first half, the prompt's block 63 - p, then the blocks c + k and c + 2 * 8 - 1 - k of one continuation whose first block is c, with k < 8. Each aligned group of 8 devices along ctx+fsdp (devices 0 to 7, 8 to 15, and so on) holds all blocks of one continuation.
All inputs are finite; a program needn't handle non-finite values.
Results may differ from the reference program's by a relative error of at most 0.028.
Values may be sent and summed in bfloat16 or wider, within the bound.
A program may use at most 640 MiB of HBM per device.

```python
import math
import jax
import jax.numpy as jnp
from jax import lax

D = 2304
HQ = 8
KVH = 4
HD = 256
FF = 9216
BLK = 32
CONT_LEN = 512
PROMPT = 2048
TOKENS = 4096
NBLK = 128


def draw_block_table(key, part):
    key = jax.random.fold_in(key, 7)
    first_key, second_key, third_key = jax.random.split(key, 3)
    devices = NBLK // 4
    mate_count = CONT_LEN // (2 * BLK)
    cont_count = devices // mate_count
    prompt_blocks = jax.random.permutation(first_key, devices).astype(jnp.int32)
    mirrored = 2 * devices - 1 - prompt_blocks
    cont_order = jax.random.permutation(second_key, cont_count).astype(jnp.int32)
    pair_keys = jax.random.split(third_key, cont_count)
    pair_order = jax.vmap(lambda single: jax.random.permutation(single, mate_count))(pair_keys).astype(jnp.int32)
    first_block = 2 * devices + cont_order[:, None] * (2 * mate_count)
    early = (first_block + pair_order).reshape(-1)
    late = (first_block + 2 * mate_count - 1 - pair_order).reshape(-1)
    table = jnp.stack([prompt_blocks, mirrored, early, late], axis=1)
    return table.reshape(-1).astype(jnp.int32)


def spiked(array, key, source, target, parts, factor):
    def block_of(dim):
        return (jnp.arange(array.shape[dim]) // (array.shape[dim] // parts)).reshape((-1,) + (1,) * (array.ndim - 1 - dim))

    one_side = jax.random.permutation(key, parts)[block_of(target)]
    other_side = (block_of(target) + parts // 2) % parts
    return jnp.where((block_of(source) == one_side) | (block_of(source) == other_side), factor * array, array)


def shard_levels(own_key, extent, shards, least, top_value):
    def one(dim, blocks):
        steps = jax.random.uniform(jax.random.fold_in(jax.random.fold_in(own_key, 6), dim), (blocks,), jnp.float32, least / len(shards), top_value / len(shards))
        return jnp.repeat(jnp.exp(steps), extent[dim] // blocks).reshape((-1,) + (1,) * (len(extent) - dim - 1))

    loudness = one(*shards[0])
    for cut in shards[1:]:
        loudness = loudness * one(*cut)
    return loudness


def noise(rng, extent, width, limit, pieces=(), kind=jnp.bfloat16):
    drawn = width * jax.random.normal(rng, extent, jnp.float32)
    if pieces:
        drawn = drawn * shard_levels(rng, extent, pieces, -0.22, 0.18)
    return jnp.clip(drawn, -limit, limit).astype(kind)


def noise_with(key, dims, deviation, bound, cuts, heavy, held_as=jnp.bfloat16):
    array = deviation * jax.random.normal(key, dims, jnp.float32)
    if cuts:
        array = array * shard_levels(key, dims, cuts, -0.22, 0.18)
    return jnp.clip(spiked(array, jax.random.fold_in(key, 3), *heavy), -bound, bound).astype(held_as)


def setup_inputs(seed: int = 0) -> dict:
    splits = jax.random.split(jax.random.key(seed), 15)
    tokens_in = noise_with(splits[0], (TOKENS, D), 1.0, 6.0, ((0, 32),), (0, 1, 32, 2.75))
    block_table = draw_block_table(jax.random.fold_in(splits[14], 71), 0)
    w_query = noise(splits[2], (D, HQ * HD), (D // 3) ** -0.5, 0.21875, ((0, 32),), jnp.float32)
    w_key = noise(splits[3], (D, KVH * HD), (D // 3) ** -0.5, 0.21875, ((0, 32),), jnp.float32)
    w_value = noise(splits[4], (D, KVH * HD), D ** -0.5, 0.125, ((0, 32),), jnp.float32)
    w_output = noise(splits[5], (HQ * HD, D), (HQ * HD) ** -0.5, 0.125, ((1, 32),), jnp.float32)
    w_gate = noise(splits[6], (D, FF), D ** -0.5, 0.125, ((1, 32),), jnp.float32)
    w_up = noise(splits[7], (D, FF), D ** -0.5, 0.125, ((1, 32),), jnp.float32)
    w_down = noise(splits[8], (FF, D), FF ** -0.5, 0.0625, ((0, 32),), jnp.float32)
    gain_attn_in = jnp.clip(1.0 + 0.1 * jax.random.normal(splits[9], (D,), jnp.float32), 0.5, 1.5)
    gain_attn_out = jnp.clip(1.0 + 0.1 * jax.random.normal(splits[10], (D,), jnp.float32), 0.5, 1.5)
    gain_ffn_in = jnp.clip(1.0 + 0.1 * jax.random.normal(splits[11], (D,), jnp.float32), 0.5, 1.5)
    gain_ffn_out = jnp.clip(1.0 + 0.1 * jax.random.normal(splits[12], (D,), jnp.float32), 0.5, 1.5)
    cotangent = noise_with(splits[13], (TOKENS, D), 1.0, 6.0, ((0, 32),), (0, 1, 32, 2.75))
    return {"tokens_in": tokens_in, "block_table": block_table, "w_query": w_query, "w_key": w_key, "w_value": w_value, "w_output": w_output, "w_gate": w_gate, "w_up": w_up, "w_down": w_down, "gain_attn_in": gain_attn_in, "gain_attn_out": gain_attn_out, "gain_ffn_in": gain_ffn_in, "gain_ffn_out": gain_ffn_out, "cotangent": cotangent}


NORM_EPS = 1e-06
SOFT_CAP = 50.0
MASKED = -1e+30

@jax.custom_vjp
def low(v):
    return lax.optimization_barrier(v.astype(jnp.bfloat16)).astype(jnp.float32)

@jax.custom_vjp
def low_back(v):
    return v

def low_keep(v):
    return (low(v), None)

def low_pass(kept, grad):
    return (grad,)

def back_keep(v):
    return (v, None)

def back_low(kept, grad):
    return (low(grad),)
low.defvjp(low_keep, low_pass)
low_back.defvjp(back_keep, back_low)

def matmul(left_side, right_side):
    return jnp.dot(left_side, right_side, precision=lax.Precision.HIGHEST, preferred_element_type=jnp.float32)

def normalize(values):
    return values * lax.rsqrt(lax.optimization_barrier(jnp.mean(values * values, axis=-1, keepdims=True)) + NORM_EPS)

def row_meta(blocks, prompt):
    offsets = jnp.arange(BLK, dtype=jnp.int32)
    natural = (blocks[:, None].astype(jnp.int32) * BLK + offsets[None, :]).reshape(-1)
    group_span = 2 * prompt
    inner_index = natural % group_span
    group_id = natural // group_span
    in_continuation = inner_index >= prompt
    segment = jnp.where(in_continuation, 1 + (inner_index - prompt) // CONT_LEN, 0)
    position = jnp.where(in_continuation, prompt + (inner_index - prompt) % CONT_LEN, inner_index)
    stride = prompt // CONT_LEN + 1
    return (position.astype(jnp.int32), (group_id * stride + segment).astype(jnp.int32), (group_id * stride).astype(jnp.int32))

def rope_tables(position):
    frequency = 10000.0 ** (-(jnp.arange(HD // 2, dtype=jnp.float32) * 2.0 / HD))
    angles = position.astype(jnp.float32)[:, None] * frequency[None, :]
    return (jnp.cos(angles), jnp.sin(angles))

def rotate(values, cosine, sine_table):
    half_width = values.shape[-1] // 2
    first_half, second_half = (values[..., :half_width], values[..., half_width:])
    cosine, sine_table = (cosine[:, None, :], sine_table[:, None, :])
    return jnp.concatenate([first_half * cosine - second_half * sine_table, second_half * cosine + first_half * sine_table], axis=-1)

def visible(query_pos, query_doc, query_base, key_pos, key_doc):
    earlier = key_pos[None, :] <= query_pos[:, None]
    shared = (key_doc[None, :] == query_doc[:, None]) | (key_doc[None, :] == query_base[:, None])
    return earlier & shared

def attend_group(group_items):
    queries, keys, values, position, document, base = group_items
    length = queries.shape[0]
    block_rows = math.gcd(length, 512)
    count_blocks = length // block_rows
    score_scale = HD ** (-0.5)

    def one_block(block_items):
        query_block, query_pos, query_doc, query_base = block_items
        scores = low_back(jnp.einsum('rgjd,kgd->rgjk', query_block, keys, precision=lax.Precision.HIGHEST, preferred_element_type=jnp.float32))
        capped = SOFT_CAP * jnp.tanh(scores * (score_scale / SOFT_CAP))
        allowed = visible(query_pos, query_doc, query_base, position, document)[:, None, None, :]
        capped = jnp.where(allowed, capped, MASKED)
        shifted = jnp.exp(capped - lax.optimization_barrier(jnp.max(capped, axis=-1, keepdims=True)))
        weights_soft = shifted / lax.optimization_barrier(jnp.sum(shifted, axis=-1, keepdims=True))
        return jnp.einsum('rgjk,kgd->rgjd', low(weights_soft), values, precision=lax.Precision.HIGHEST, preferred_element_type=jnp.float32)

    def in_blocks(whole_array):
        return whole_array.reshape((count_blocks, block_rows) + whole_array.shape[1:])
    result = lax.map(jax.checkpoint(one_block), (in_blocks(queries), in_blocks(position), in_blocks(document), in_blocks(base)))
    return result.reshape(queries.shape)

def reference(tokens_in, block_table, w_query, w_key, w_value, w_output, w_gate, w_up, w_down, gain_attn_in, gain_attn_out, gain_ffn_in, gain_ffn_out, cotangent):
    position, document, base = row_meta(jnp.arange(NBLK, dtype=jnp.int32), PROMPT)
    cosine, sine_table = rope_tables(position)
    groups = HQ // KVH

    def forward(inputs, wq_master, wk_master, wv_master, wo_master, wg_master, wu_master, wd_master, gain_one, gain_two, gain_three, gain_four):
        row_count = inputs.shape[0]
        normed_x = low(normalize(inputs) * low(gain_one))
        query_raw = low_back(matmul(normed_x, low(wq_master))).reshape(row_count, HQ, HD)
        queries = low(rotate(query_raw, cosine, sine_table)).reshape(row_count, KVH, groups, HD)
        key_raw = low_back(matmul(normed_x, low(wk_master))).reshape(row_count, KVH, HD)
        keys = low(rotate(key_raw, cosine, sine_table)).reshape(row_count, KVH, HD)
        values = low(low_back(matmul(normed_x, low(wv_master)))).reshape(row_count, KVH, HD)
        attended = attend_group((queries, keys, values, position, document, base))
        attended = low(low_back(attended.reshape(row_count, HQ * HD)))
        branch = low_back(matmul(attended, low(wo_master)))
        hidden = inputs + normalize(branch) * low(gain_two)
        normed_h = low(normalize(hidden) * low(gain_three))
        gate = low_back(matmul(normed_h, low(wg_master)))
        upper = low_back(matmul(normed_h, low(wu_master)))
        activated = low(jax.nn.gelu(gate, approximate=True) * upper)
        ffn_out = low_back(matmul(activated, low(wd_master)))
        return hidden + normalize(ffn_out) * low(gain_four)

    def natural_order(stored):
        blocks = stored.reshape(NBLK, BLK, stored.shape[-1])
        return jnp.zeros_like(blocks).at[block_table.astype(jnp.int32)].set(blocks).reshape(TOKENS, stored.shape[-1])

    def stored_order(natural):
        return natural.reshape(NBLK, BLK, natural.shape[-1])[block_table.astype(jnp.int32)].reshape(TOKENS, natural.shape[-1])
    inputs = natural_order(tokens_in).astype(jnp.float32)
    upstream = natural_order(cotangent).astype(jnp.float32)
    layer, pull = jax.vjp(forward, inputs, w_query, w_key, w_value, w_output, w_gate, w_up, w_down, gain_attn_in, gain_attn_out, gain_ffn_in, gain_ffn_out)
    grads = pull(upstream)
    return (stored_order(layer).astype(jnp.bfloat16), stored_order(grads[0]).astype(jnp.bfloat16), grads[1], grads[2], grads[3], grads[4], grads[5], grads[6], grads[7], grads[8], grads[9], grads[10], grads[11])
```

```python
import functools
import math

import jax
import jax.numpy as jnp
from jax import lax
from jax.experimental import pallas as pl
from jax.experimental.pallas import tpu as pltpu
from jax.sharding import PartitionSpec as P

HD = 256
BLK = 32
CONT_LEN = 512
KBLK = 1024


SOFT_CAP = 50.0
MASKED = -1e30
MESH = pl.DeviceIdType.MESH
NT = (((1,), (1,)), ((), ()))
NN = (((1,), (0,)), ((), ()))
TN = (((0,), (0,)), ((), ()))
NORM_EPS = 1e-06
GELU_A = 0.7978845608028654
GELU_B = 0.044715


def mm(left, right, dims):
    return lax.dot_general(left, right, dims, preferred_element_type=jnp.float32)


def spans(total, width):
    return [(at, min(width, total - at)) for at in range(0, total, width)]


def ffn_kernel(
    planes,
    fs,
    n2_ref,
    h_ref,
    dy_ref,
    gain_ref,
    wa_ref,
    wb_ref,
    wc_ref,
    out_ref,
    dn2_ref,
    gsum_ref,
    dw_ref,
    w,
    n2all,
    dfall,
    gate,
    up,
    act,
    part,
    yrecv,
    zrecv,
    stage,
    w_sem,
    dw_sem,
    ag_ys,
    ag_yr,
    ag_zs,
    ag_zr,
    rs_ys,
    rs_yr,
    rs_zs,
    rs_zr,
):
    P = planes
    rows, width = n2_ref.shape
    slot = wa_ref.shape[1]
    hidden = 4 * slot
    bf = jnp.bfloat16
    me = lax.axis_index("ctx") * fs + lax.axis_index("fsdp")
    p0 = me // 8
    y0 = (me // 4) % 2

    def device(index):
        return (index // fs, index % fs)

    partner = device(me + 4 - 8 * y0)
    right = device(jnp.minimum(me + 8, 8 * P - 8 + me % 8))
    left = device(jnp.maximum(me - 8, me % 8))
    has_right = p0 < P - 1
    has_left = p0 > 0

    barrier = pltpu.get_barrier_semaphore()
    pl.semaphore_signal(barrier, inc=1, device_id=partner, device_id_type=MESH)

    @pl.when(has_right)
    def _():
        pl.semaphore_signal(barrier, inc=1, device_id=right, device_id_type=MESH)

    @pl.when(has_left)
    def _():
        pl.semaphore_signal(barrier, inc=1, device_id=left, device_id_type=MESH)

    weight_copies = []
    for piece in range(4):
        for which in range(3):
            source = (wa_ref.at[which], wb_ref.at[which], wc_ref.at[0, which], wc_ref.at[1, which])[piece]
            copy = pltpu.make_async_copy(
                source, w.at[which, pl.ds(piece * slot, slot)], w_sem.at[piece * 3 + which]
            )
            copy.start()
            weight_copies.append(copy)

    def block(p, y):
        return pl.ds(pl.multiple_of((p * 2 + y) * rows, rows), rows)

    def pair(p):
        return pl.ds(pl.multiple_of(p * 2 * rows, 2 * rows), 2 * rows)

    def at(p):
        return pl.ds(pl.multiple_of(p * rows, rows), rows)

    few = jnp.minimum(p0, P - 1 - p0)

    def order(k):
        two_sided = jnp.where(k % 2 == 1, p0 - (k + 1) // 2, p0 + (k + 1) // 2)
        one_sided = jnp.where(p0 > P - 1 - p0, p0 - (k - few), p0 + (k - few))
        return jnp.where(k <= 2 * few, two_sided, one_sided)

    pl.semaphore_wait(barrier, 1 + jnp.where(has_right, 1, 0) + jnp.where(has_left, 1, 0))

    def gather(buf, turn, compute):
        def y_copy(p, y):
            return pltpu.make_async_remote_copy(
                src_ref=buf.at[block(p, y)],
                dst_ref=buf.at[block(p, y)],
                send_sem=ag_ys.at[turn, p],
                recv_sem=ag_yr.at[turn, p],
                device_id=partner,
                device_id_type=MESH,
            )

        def z_copy(p, to, way):
            return pltpu.make_async_remote_copy(
                src_ref=buf.at[block(p, y0)],
                dst_ref=buf.at[block(p, y0)],
                send_sem=ag_zs.at[turn, way, p],
                recv_sem=ag_zr.at[turn, p],
                device_id=to,
                device_id_type=MESH,
            )

        def z_send(p):
            @pl.when(has_right & (p <= p0))
            def _():
                z_copy(p, right, 0).start()

            @pl.when(has_left & (p >= p0))
            def _():
                z_copy(p, left, 1).start()

        z_send(p0)
        y_copy(p0, y0).start()

        def step(k, carry):
            @pl.when(k < P)
            def _():
                p = order(k)
                z_copy(p, right, 0).wait_recv()
                z_send(p)
                y_copy(p, y0).start()

            q = order(k - 1)
            y_copy(q, 1 - y0).wait_recv()
            compute(q)
            return carry

        lax.fori_loop(1, P + 1, step, 0)

        def drain(p, carry):
            y_copy(p, y0).wait_send()

            @pl.when(has_right & (p <= p0))
            def _():
                z_copy(p, right, 0).wait_send()

            @pl.when(has_left & (p >= p0))
            def _():
                z_copy(p, left, 1).wait_send()

            return carry

        lax.fori_loop(0, P, drain, 0)

    def scatter(turn, beside):
        def y_copy(p):
            return pltpu.make_async_remote_copy(
                src_ref=part.at[block(p, 1 - y0)],
                dst_ref=yrecv.at[at(p)],
                send_sem=rs_ys.at[turn, p],
                recv_sem=rs_yr.at[turn, p],
                device_id=partner,
                device_id_type=MESH,
            )

        def z_copy(p, to, into):
            return pltpu.make_async_remote_copy(
                src_ref=part.at[block(p, y0)],
                dst_ref=zrecv.at[at(into)],
                send_sem=rs_zs.at[turn, p],
                recv_sem=rs_zr.at[turn, into],
                device_id=to,
                device_id_type=MESH,
            )

        def start_y(j, carry):
            y_copy(order(P - 1 - j)).start()
            return carry

        lax.fori_loop(0, P, start_y, 0)

        def step(j, carry):
            p = order(P - 1 - j)
            beside(j)
            y_copy(p).wait_recv()
            part[block(p, y0), :] = (
                part[block(p, y0), :].astype(jnp.float32) + yrecv[at(p), :].astype(jnp.float32)
            ).astype(bf)

            @pl.when((has_left & (p > p0)) | (has_right & (p < p0)))
            def _():
                z_copy(p, right, p).wait_recv()
                part[block(p, y0), :] = (
                    part[block(p, y0), :].astype(jnp.float32) + zrecv[at(p), :].astype(jnp.float32)
                ).astype(bf)

            @pl.when(p > p0)
            def _():
                z_copy(p, right, p).start()

            @pl.when(p < p0)
            def _():
                z_copy(p, left, jnp.where(p == p0 - 1, P, p)).start()

            return carry

        lax.fori_loop(0, P - 1, step, 0)
        beside(P - 1)
        y_copy(p0).wait_recv()
        dn2_ref[...] = part[block(p0, y0), :].astype(jnp.float32) + yrecv[at(p0), :].astype(
            jnp.float32
        )

        @pl.when(has_left)
        def _():
            z_copy(p0, right, p0).wait_recv()
            dn2_ref[...] += zrecv[at(p0), :].astype(jnp.float32)

        @pl.when(has_right)
        def _():
            z_copy(p0, right, P).wait_recv()
            dn2_ref[...] += zrecv[at(P), :].astype(jnp.float32)

        def drain(p, carry):
            y_copy(p).wait_send()

            @pl.when(p != p0)
            def _():
                z_copy(p, right, p).wait_send()

            return carry

        lax.fori_loop(0, P, drain, 0)

    n2all[block(p0, y0), :] = n2_ref[...]

    def forward(p):
        @pl.when(p == p0)
        def _():
            for copy in weight_copies:
                copy.wait()

        feats = n2all[pair(p), :]
        for first, wide in spans(hidden, 256):
            cols = slice(first, first + wide)
            gates = mm(feats, w[0, cols, :], NT)
            ups = mm(feats, w[1, cols, :], NT)
            bent = jnp.tanh(GELU_A * (gates + GELU_B * gates * gates * gates))
            gate[pair(p), cols] = gates.astype(bf)
            up[pair(p), cols] = ups.astype(bf)
            act[pair(p), cols] = (0.5 * gates * (1.0 + bent) * ups).astype(bf)
        for first, wide in spans(width, 768):
            cols = slice(first, first + wide)
            part[pair(p), cols] = mm(act[pair(p), :], w[2, :, cols], NN).astype(bf)

    gather(n2all, 0, forward)
    scatter(0, lambda j: None)
    ffn = dn2_ref[...]
    inverse = lax.rsqrt(jnp.mean(ffn * ffn, axis=-1, keepdims=True) + NORM_EPS)
    unit = ffn * inverse
    out_ref[...] = (h_ref[...] + unit * gain_ref[...]).astype(bf)
    upstream = dy_ref[...].astype(jnp.float32)
    gsum_ref[...] = jnp.sum(upstream * unit, axis=0, keepdims=True)
    pulled = upstream * gain_ref[...]
    dfall[block(p0, y0), :] = (
        inverse * (pulled - unit * jnp.mean(pulled * unit, axis=-1, keepdims=True))
    ).astype(bf)

    def backward(p):
        grads = dfall[pair(p), :]
        for first, wide in spans(hidden, 256):
            cols = slice(first, first + wide)
            dact = mm(grads, w[2, cols, :], NT)
            gates = gate[pair(p), cols].astype(jnp.float32)
            ups = up[pair(p), cols].astype(jnp.float32)
            square = gates * gates
            bent = jnp.tanh(GELU_A * (gates + GELU_B * gates * square))
            half = 0.5 * (1.0 + bent)
            slope = half + 0.5 * gates * (1.0 - bent * bent) * (
                GELU_A * (1.0 + 3.0 * GELU_B * square)
            )
            gate[pair(p), cols] = (dact * ups * slope).astype(bf)
            up[pair(p), cols] = (dact * gates * half).astype(bf)
        for first, wide in spans(width, 768):
            cols = slice(first, first + wide)
            part[pair(p), cols] = (
                mm(gate[pair(p), :], w[0, :, cols], NN) + mm(up[pair(p), :], w[1, :, cols], NN)
            ).astype(bf)

    gather(dfall, 1, backward)

    chunks = spans(width, 768)

    def dw_copy(which, number):
        first, wide = chunks[number]
        slot_here = (which * len(chunks) + number) % 2
        return pltpu.make_async_copy(
            stage.at[slot_here], dw_ref.at[which, :, pl.ds(first, wide)], dw_sem.at[slot_here]
        )

    def weight_grad(task):
        which, number = task // len(chunks), task % len(chunks)
        first, wide = chunks[number]
        if task >= 2:
            dw_copy((task - 2) // len(chunks), (task - 2) % len(chunks)).wait()
        left_side = (gate, up, act)[which]
        right_side = (n2all, n2all, dfall)[which]
        stage[task % 2] = mm(
            left_side[...], right_side[:, first : first + wide], TN
        ).astype(bf)
        dw_copy(which, number).start()

    tasks = 3 * len(chunks)

    def beside(j):
        if isinstance(j, int):
            for task in range(tasks):
                weight_grad(task)

    scatter(1, beside)
    for task in range(tasks - 2, tasks):
        dw_copy(task // len(chunks), task % len(chunks)).wait()


def ffn_call(mesh_shape, n2, h, dy, gain, wa, wb, wc):
    fs = mesh_shape["fsdp"]
    planes = mesh_shape["ctx"] * fs // 8
    rows, width = n2.shape
    slot = wa.shape[1]
    hidden = 4 * slot
    tokens = planes * 2 * rows
    bf, f32 = jnp.bfloat16, jnp.float32
    vmem = pl.BlockSpec(memory_space=pltpu.VMEM)
    hbm = pl.BlockSpec(memory_space=pl.ANY)
    dma = pltpu.SemaphoreType.DMA
    return pl.pallas_call(
        functools.partial(ffn_kernel, planes, fs),
        out_shape=(
            jax.ShapeDtypeStruct((rows, width), bf),
            jax.ShapeDtypeStruct((rows, width), f32),
            jax.ShapeDtypeStruct((1, width), f32),
            jax.ShapeDtypeStruct((3, hidden, width), bf),
        ),
        in_specs=[vmem, vmem, vmem, vmem, hbm, hbm, hbm],
        out_specs=(vmem, vmem, vmem, hbm),
        scratch_shapes=[
            pltpu.VMEM((3, hidden, width), bf),
            pltpu.VMEM((tokens, width), bf),
            pltpu.VMEM((tokens, width), bf),
            pltpu.VMEM((tokens, hidden), bf),
            pltpu.VMEM((tokens, hidden), bf),
            pltpu.VMEM((tokens, hidden), bf),
            pltpu.VMEM((tokens, width), bf),
            pltpu.VMEM((planes * rows, width), bf),
            pltpu.VMEM(((planes + 1) * rows, width), bf),
            pltpu.VMEM((2, hidden, 768), bf),
            dma((12,)),
            dma((2,)),
            dma((2, planes)),
            dma((2, planes)),
            dma((2, 2, planes)),
            dma((2, planes)),
            dma((2, planes)),
            dma((2, planes)),
            dma((2, planes)),
            dma((2, planes + 1)),
        ],
        compiler_params=pltpu.CompilerParams(
            collective_id=1, has_side_effects=True, vmem_limit_bytes=60 * 2**20
        ),
        name="ffn",
    )(n2, h, dy, gain, wa, wb, wc)


CONTRACT_ROWS = (((0,), (0,)), ((), ()))
CONTRACT_COLS = (((1,), (1,)), ((), ()))


def from_partner(array, axis, apart):
    return lax.ppermute(array, axis, [(i, i ^ 1 << apart) for i in range(lax.axis_size(axis))])


def normalize(values):
    inverse = lax.rsqrt(jnp.mean(values * values, axis=-1, keepdims=True) + NORM_EPS)
    return (values * inverse, inverse)


def norm_back(unit_values, inverse, grad_unit):
    return inverse * (
        grad_unit - unit_values * jnp.mean(grad_unit * unit_values, axis=-1, keepdims=True)
    )


def row_meta(blocks, prompt):
    offsets = jnp.arange(BLK, dtype=jnp.int32)
    natural = (blocks[:, None] * BLK + offsets[None, :]).reshape(-1)
    group_span = 2 * prompt
    inner_index = natural % group_span
    group_id = natural // group_span
    in_continuation = inner_index >= prompt
    segment = jnp.where(in_continuation, 1 + (inner_index - prompt) // CONT_LEN, 0)
    position = jnp.where(in_continuation, prompt + (inner_index - prompt) % CONT_LEN, inner_index)
    stride = prompt // CONT_LEN + 1
    return (position, group_id * stride + segment, group_id * stride)


def rope_tables(position):
    frequency = 10000.0 ** (-(jnp.arange(HD // 2, dtype=jnp.float32) * 2.0 / HD))
    angles = position.astype(jnp.float32)[:, None] * frequency[None, :]
    return (jnp.cos(angles), jnp.sin(angles))


def rotate(values, cosine, sine_table):
    half_width = values.shape[-1] // 2
    first_half, second_half = (values[..., :half_width], values[..., half_width:])
    cosine, sine_table = (cosine[:, None, :], sine_table[:, None, :])
    return jnp.concatenate(
        [
            first_half * cosine - second_half * sine_table,
            second_half * cosine + first_half * sine_table,
        ],
        axis=-1,
    )


def unrotate(grads, cosine, sine_table):
    half_width = grads.shape[-1] // 2
    first_half, second_half = (grads[..., :half_width], grads[..., half_width:])
    cosine, sine_table = (cosine[:, None, :], sine_table[:, None, :])
    return jnp.concatenate(
        [
            first_half * cosine + second_half * sine_table,
            second_half * cosine - first_half * sine_table,
        ],
        axis=-1,
    )


def visible(query_pos, query_doc, query_base, key_pos, key_doc):
    earlier = key_pos[None, :] <= query_pos[:, None]
    shared = (key_doc[None, :] == query_doc[:, None]) | (key_doc[None, :] == query_base[:, None])
    return earlier & shared


def gated(gate_values, up_values):
    return jax.nn.gelu(gate_values, approximate=True) * up_values


def ffn_fits(mesh_shape, rows, width, slot):
    planes = mesh_shape["ctx"] * mesh_shape["fsdp"] // 8
    tokens, hidden = planes * 2 * rows, 4 * slot
    wide_rows = 3 * hidden + 3 * tokens + (2 * planes + 1) * rows
    held = 2 * width * wide_rows + 6 * tokens * hidden + 2 * 2 * 768 * hidden
    return slot % 16 == 0 and held < 48 * 2**20


def ffn_gathered(hidden_res, normed_h, upstream, gain_four, w_gate, w_up, w_down):
    bfloat = jnp.bfloat16
    pair_weights = jnp.stack([w_gate, w_up]).astype(bfloat)
    down_local = w_down.astype(bfloat)
    gate_up = jnp.einsum(
        "rd,sdf->rsf",
        lax.all_gather(normed_h, ("ctx", "fsdp"), axis=0, tiled=True),
        pair_weights,
        preferred_element_type=jnp.float32,
    )
    activated = gated(gate_up[:, 0], gate_up[:, 1]).astype(bfloat)
    part_rows = activated
    ffn_raw = lax.psum_scatter(
        jnp.dot(part_rows, down_local, preferred_element_type=jnp.float32).astype(bfloat),
        ("ctx", "fsdp"),
        scatter_dimension=0,
        tiled=True,
    ).astype(jnp.float32)
    unit_f, inv_f = normalize(ffn_raw)
    layer_out = (hidden_res + unit_f * gain_four).astype(bfloat)
    grad_four = jnp.sum(upstream * unit_f, axis=0)
    grad_ffn = norm_back(unit_f, inv_f, upstream * gain_four).astype(bfloat)
    grad_piece = lax.all_gather(grad_ffn, ("ctx", "fsdp"), axis=0, tiled=True)
    normed_piece = lax.all_gather(normed_h, ("ctx", "fsdp"), axis=0, tiled=True)
    act_grad = lax.dot_general(
        grad_piece, down_local, CONTRACT_COLS, preferred_element_type=jnp.float32
    )
    pull_piece = jax.vjp(gated, gate_up[:, 0], gate_up[:, 1])[1]
    gate_grad, up_grad = pull_piece(act_grad)
    pair_low = jnp.stack([gate_grad, up_grad], axis=1).astype(bfloat)
    down_sum = lax.dot_general(
        activated, grad_piece, CONTRACT_ROWS, preferred_element_type=jnp.float32
    )
    pair_sum = jnp.einsum("nd,nsf->sdf", normed_piece, pair_low, preferred_element_type=jnp.float32)
    grad_gate = pair_sum[0]
    grad_up = pair_sum[1]
    part_rows = pair_low
    grad_normed_h = lax.psum_scatter(
        jnp.einsum("nsf,sdf->nd", part_rows, pair_weights, preferred_element_type=jnp.float32).astype(bfloat),
        ("ctx", "fsdp"),
        scatter_dimension=0,
        tiled=True,
    ).astype(jnp.float32)
    return (layer_out, grad_normed_h, grad_four, grad_gate, grad_up, down_sum)


def ffn_in_groups(mesh_shape, hidden_res, normed_h, cotangent, gain_four, w_gate, w_up, w_down):
    axes = ("ctx", "fsdp")
    bfloat = jnp.bfloat16
    own = jnp.stack([w_gate.T.astype(bfloat), w_up.T.astype(bfloat), w_down.astype(bfloat)])
    across = from_partner(own, axes, 1)
    beside = from_partner(jnp.stack([own, across]), axes, 0)
    layer_out, grad_normed_h, grad_four, partial = ffn_call(
        mesh_shape, normed_h, hidden_res, cotangent, gain_four[None, :], own, across, beside
    )
    partial = partial.reshape((3, 4) + own.shape[1:])
    shared = partial[:, :2].astype(jnp.float32) + from_partner(partial[:, 2:], axes, 0).astype(
        jnp.float32
    )
    summed = shared[:, 0] + from_partner(shared[:, 1].astype(bfloat), axes, 1).astype(jnp.float32)
    return (layer_out, grad_normed_h, grad_four[0], summed[0].T, summed[1].T, summed[2])


def on_device(
    mesh_shape,
    tokens_in,
    block_table,
    w_query,
    w_key,
    w_value,
    w_output,
    w_gate,
    w_up,
    w_down,
    gain_attn_in,
    gain_attn_out,
    gain_ffn_in,
    gain_ffn_out,
    cotangent,
):
    row_count, model_width = tokens_in.shape
    devices = lax.axis_size(("ctx", "fsdp"))
    slot_count = block_table.shape[0] // devices
    prompt = 2 * devices * BLK
    all_rows = row_count * devices
    device_here = lax.axis_index(("ctx", "fsdp"))
    head_count = w_query.shape[1] // HD
    kv_count = w_key.shape[1] // HD
    groups = head_count // kv_count
    score_scale = HD ** (-0.5)
    bfloat = jnp.bfloat16
    gathered = (
        lax.all_gather(w_query.astype(bfloat), ("ctx", "fsdp"), axis=0, tiled=True),
        lax.all_gather(w_key.astype(bfloat), ("ctx", "fsdp"), axis=0, tiled=True),
        lax.all_gather(w_value.astype(bfloat), ("ctx", "fsdp"), axis=0, tiled=True),
        lax.all_gather(w_output.astype(bfloat), ("ctx", "fsdp"), axis=1, tiled=True),
        lax.all_gather(gain_attn_in.astype(bfloat), ("ctx", "fsdp"), axis=0, tiled=True),
        lax.all_gather(gain_attn_out.astype(bfloat), ("ctx", "fsdp"), axis=0, tiled=True),
        lax.all_gather(gain_ffn_in.astype(bfloat), ("ctx", "fsdp"), axis=0, tiled=True),
        lax.all_gather(gain_ffn_out.astype(bfloat), ("ctx", "fsdp"), axis=0, tiled=True),
    )
    query_weight, key_weight, value_weight, output_weight = (
        gathered[0],
        gathered[1],
        gathered[2],
        gathered[3],
    )
    gain_one = gathered[4].astype(jnp.float32)
    gain_two = gathered[5].astype(jnp.float32)
    gain_three = gathered[6].astype(jnp.float32)
    gain_four = gathered[7].astype(jnp.float32)
    key_meta = row_meta(block_table, prompt)
    key_pos, key_doc = (key_meta[0], key_meta[1])
    my_blocks = lax.dynamic_slice_in_dim(block_table, device_here * slot_count, slot_count)
    query_pos, query_doc, query_base = row_meta(my_blocks, prompt)
    cosine, sine_table = rope_tables(query_pos)
    inputs = tokens_in.astype(jnp.float32)
    unit_x, inv_x = normalize(inputs)
    normed_x = (unit_x * gain_one).astype(bfloat)
    query_raw = jnp.dot(normed_x, query_weight, preferred_element_type=jnp.float32).reshape(
        row_count, head_count, HD
    )
    queries = (
        rotate(query_raw, cosine, sine_table)
        .astype(bfloat)
        .reshape(row_count, kv_count, groups, HD)
    )
    key_raw = jnp.dot(normed_x, key_weight, preferred_element_type=jnp.float32).reshape(
        row_count, kv_count, HD
    )
    keys = rotate(key_raw, cosine, sine_table).astype(bfloat)
    values = (
        jnp.dot(normed_x, value_weight, preferred_element_type=jnp.float32)
        .reshape(row_count, kv_count, HD)
        .astype(bfloat)
    )

    def key_block_meta(first_row, block_width):
        block_pos = lax.dynamic_slice_in_dim(key_pos, first_row, block_width)
        block_doc = lax.dynamic_slice_in_dim(key_doc, first_row, block_width)
        return visible(query_pos, query_doc, query_base, block_pos, block_doc)[:, None, None, :]

    def bent_scores(key_block):
        scores = jnp.einsum(
            "rgjd,kgd->rgjk", queries, key_block, preferred_element_type=jnp.float32
        )
        return jnp.tanh(scores * (score_scale / SOFT_CAP))

    start_state = (
        jnp.full((row_count, kv_count, groups), MASKED, jnp.float32),
        jnp.zeros((row_count, kv_count, groups), jnp.float32),
        jnp.zeros((row_count, kv_count, groups, HD), jnp.float32),
    )
    key_piece = lax.all_gather(keys, ("ctx", "fsdp"), axis=0, tiled=True)
    value_piece = lax.all_gather(values, ("ctx", "fsdp"), axis=0, tiled=True)
    piece_rows = key_piece.shape[0]
    block_width = math.gcd(piece_rows, KBLK)

    def attend_block_step(block_index, state):
        running_max, running_sum, running_out = state
        offset = block_index * block_width
        key_block = lax.dynamic_slice_in_dim(key_piece, offset, block_width, 0)
        value_block = lax.dynamic_slice_in_dim(value_piece, offset, block_width, 0)
        allowed = key_block_meta(offset, block_width)
        capped = jnp.where(allowed, SOFT_CAP * bent_scores(key_block), MASKED)
        fresh_max = jnp.maximum(running_max, jnp.max(capped, axis=-1))
        decay = jnp.exp(running_max - fresh_max)
        weights_soft = jnp.where(allowed, jnp.exp(capped - fresh_max[..., None]), 0.0)
        running_sum = running_sum * decay + jnp.sum(weights_soft, axis=-1)
        running_out = running_out * decay[..., None] + jnp.einsum(
            "rgjk,kgd->rgjd",
            weights_soft.astype(bfloat),
            value_block,
            preferred_element_type=jnp.float32,
        )
        return (fresh_max, running_sum, running_out)

    running_max, running_sum, running_out = lax.fori_loop(
        0, piece_rows // block_width, attend_block_step, start_state
    )
    log_total = running_max + jnp.log(running_sum)
    attended = (running_out / running_sum[..., None]).reshape(row_count, head_count * HD)
    attended_low = attended.astype(bfloat)
    branch_raw = jnp.dot(attended_low, output_weight, preferred_element_type=jnp.float32)
    unit_a, inv_a = normalize(branch_raw)
    hidden_res = inputs + unit_a * gain_two
    unit_h, inv_h = normalize(hidden_res)
    normed_h = (unit_h * gain_three).astype(bfloat)
    upstream = cotangent.astype(jnp.float32)
    if ffn_fits(mesh_shape, row_count, model_width, w_down.shape[0]):
        layer_out, grad_normed_h, grad_four, grad_gate, grad_up, down_sum = ffn_in_groups(
            mesh_shape, hidden_res, normed_h, cotangent, gain_four, w_gate, w_up, w_down
        )
    else:
        layer_out, grad_normed_h, grad_four, grad_gate, grad_up, down_sum = ffn_gathered(
            hidden_res, normed_h, upstream, gain_four, w_gate, w_up, w_down
        )
    grad_three = jnp.sum(grad_normed_h * unit_h, axis=0)
    grad_res = upstream + norm_back(unit_h, inv_h, grad_normed_h * gain_three)
    grad_two = jnp.sum(grad_res * unit_a, axis=0)
    grad_branch = norm_back(unit_a, inv_a, grad_res * gain_two).astype(bfloat)
    grad_att = lax.dot_general(
        grad_branch, output_weight, CONTRACT_COLS, preferred_element_type=jnp.float32
    ).astype(bfloat)
    grad_heads = grad_att.reshape(row_count, kv_count, groups, HD)
    row_delta = jnp.sum(
        grad_heads.astype(jnp.float32) * attended.reshape(row_count, kv_count, groups, HD), axis=-1
    )
    begin_state = (
        jnp.zeros((row_count, kv_count, groups, HD), jnp.float32),
        jnp.zeros((all_rows, kv_count, HD), jnp.float32),
        jnp.zeros((all_rows, kv_count, HD), jnp.float32),
    )
    retrace_key_piece = lax.all_gather(keys, ("ctx", "fsdp"), axis=0, tiled=True)
    retrace_value_piece = lax.all_gather(values, ("ctx", "fsdp"), axis=0, tiled=True)
    piece_rows = retrace_key_piece.shape[0]
    retrace_block_width = math.gcd(piece_rows, KBLK)

    def retrace_block_step(block_index, state):
        query_sum, key_sums, value_sums = state
        offset = block_index * retrace_block_width
        key_block = lax.dynamic_slice_in_dim(retrace_key_piece, offset, retrace_block_width, 0)
        value_block = lax.dynamic_slice_in_dim(retrace_value_piece, offset, retrace_block_width, 0)
        allowed = key_block_meta(offset, retrace_block_width)
        bent = bent_scores(key_block)
        weights_soft = jnp.where(allowed, jnp.exp(SOFT_CAP * bent - log_total[..., None]), 0.0)
        value_dots = jnp.einsum(
            "rgjd,kgd->rgjk", grad_heads, value_block, preferred_element_type=jnp.float32
        )
        score_grad = (
            weights_soft * (value_dots - row_delta[..., None]) * (1.0 - bent * bent) * score_scale
        ).astype(bfloat)
        query_sum = query_sum + jnp.einsum(
            "rgjk,kgd->rgjd", score_grad, key_block, preferred_element_type=jnp.float32
        )
        key_part = jnp.einsum(
            "rgjk,rgjd->kgd", score_grad, queries, preferred_element_type=jnp.float32
        )
        value_part = jnp.einsum(
            "rgjk,rgjd->kgd",
            weights_soft.astype(bfloat),
            grad_heads,
            preferred_element_type=jnp.float32,
        )
        key_sums = lax.dynamic_update_slice_in_dim(key_sums, key_part, offset, 0)
        value_sums = lax.dynamic_update_slice_in_dim(value_sums, value_part, offset, 0)
        return (query_sum, key_sums, value_sums)

    query_sum, key_sums, value_sums = lax.fori_loop(
        0, piece_rows // retrace_block_width, retrace_block_step, begin_state
    )
    mate_count = CONT_LEN // (2 * BLK)
    tail_shape = key_sums.shape[1:]
    key_slots = key_sums.reshape((devices, slot_count, BLK) + tail_shape)
    value_slots = value_sums.reshape((devices, slot_count, BLK) + tail_shape)
    prompt_rows = 2 * BLK * devices
    key_head, value_head = (
        lax.psum_scatter(
            key_slots[:, :2].reshape((prompt_rows,) + tail_shape),
            ("ctx", "fsdp"),
            scatter_dimension=0,
            tiled=True,
        ),
        lax.psum_scatter(
            value_slots[:, :2].reshape((prompt_rows,) + tail_shape),
            ("ctx", "fsdp"),
            scatter_dimension=0,
            tiled=True,
        ),
    )
    group_start = device_here // mate_count * mate_count
    later_both = jnp.stack(
        [
            lax.dynamic_slice_in_dim(key_slots[:, 2:], group_start, mate_count, 0),
            lax.dynamic_slice_in_dim(value_slots[:, 2:], group_start, mate_count, 0),
        ],
        axis=1,
    )
    rank_inner = device_here % mate_count
    for level in reversed(range(mate_count.bit_length() - 1)):
        half_count = later_both.shape[0] // 2
        upper_side = rank_inner >> level & 1 == 1
        lower_half = later_both[:half_count]
        upper_half = later_both[half_count:]
        kept = jnp.where(upper_side, upper_half, lower_half)
        given = jnp.where(upper_side, lower_half, upper_half)
        later_both = kept + from_partner(given.astype(jnp.bfloat16), ("ctx", "fsdp"), level).astype(
            given.dtype
        )
    key_mine = jnp.concatenate(
        [key_head, later_both[0, 0].reshape((2 * BLK,) + tail_shape)], axis=0
    )
    value_mine = jnp.concatenate(
        [value_head, later_both[0, 1].reshape((2 * BLK,) + tail_shape)], axis=0
    )
    grad_q = (
        unrotate(query_sum.reshape(row_count, head_count, HD), cosine, sine_table)
        .reshape(row_count, head_count * HD)
        .astype(bfloat)
    )
    grad_k = unrotate(key_mine, cosine, sine_table).reshape(row_count, kv_count * HD).astype(bfloat)
    grad_v = value_mine.reshape(row_count, kv_count * HD).astype(bfloat)
    grad_normed_x = lax.dot_general(
        grad_q, query_weight, CONTRACT_COLS, preferred_element_type=jnp.float32
    )
    grad_normed_x = grad_normed_x + lax.dot_general(
        grad_k, key_weight, CONTRACT_COLS, preferred_element_type=jnp.float32
    )
    grad_normed_x = grad_normed_x + lax.dot_general(
        grad_v, value_weight, CONTRACT_COLS, preferred_element_type=jnp.float32
    )
    grad_one = jnp.sum(grad_normed_x * unit_x, axis=0)
    grad_in = (grad_res + norm_back(unit_x, inv_x, grad_normed_x * gain_one)).astype(bfloat)
    projection_grads = jnp.concatenate([grad_q, grad_k, grad_v], axis=1)
    input_term = lax.dot_general(
        normed_x, projection_grads, CONTRACT_ROWS, preferred_element_type=jnp.float32
    )
    output_term = lax.dot_general(
        grad_branch, attended_low, CONTRACT_ROWS, preferred_element_type=jnp.float32
    )
    input_share, output_share, share_one, share_two, share_three, share_four = (
        lax.psum_scatter(input_term, ("ctx", "fsdp"), scatter_dimension=0, tiled=True),
        lax.psum_scatter(output_term, ("ctx", "fsdp"), scatter_dimension=0, tiled=True),
        lax.psum_scatter(grad_one, ("ctx", "fsdp"), scatter_dimension=0, tiled=True),
        lax.psum_scatter(grad_two, ("ctx", "fsdp"), scatter_dimension=0, tiled=True),
        lax.psum_scatter(grad_three, ("ctx", "fsdp"), scatter_dimension=0, tiled=True),
        lax.psum_scatter(grad_four, ("ctx", "fsdp"), scatter_dimension=0, tiled=True),
    )
    query_cols = head_count * HD
    key_cols = kv_count * HD
    grad_query = input_share[:, :query_cols]
    grad_key = input_share[:, query_cols : query_cols + key_cols]
    grad_value = input_share[:, query_cols + key_cols :]
    grad_output = output_share.T
    return (
        layer_out,
        grad_in,
        grad_query,
        grad_key,
        grad_value,
        grad_output,
        grad_gate,
        grad_up,
        down_sum,
        share_one,
        share_two,
        share_three,
        share_four,
    )


def solution(mesh):
    placed = (
        P(("ctx", "fsdp"), None),
        P(),
        P(("ctx", "fsdp"), None),
        P(("ctx", "fsdp"), None),
        P(("ctx", "fsdp"), None),
        P(None, ("ctx", "fsdp")),
        P(None, ("ctx", "fsdp")),
        P(None, ("ctx", "fsdp")),
        P(("ctx", "fsdp"), None),
        P(("ctx", "fsdp")),
        P(("ctx", "fsdp")),
        P(("ctx", "fsdp")),
        P(("ctx", "fsdp")),
        P(("ctx", "fsdp"), None),
    )
    return jax.shard_map(
        functools.partial(on_device, dict(mesh.shape)),
        mesh=mesh,
        in_specs=placed,
        out_specs=(
            P(("ctx", "fsdp"), None),
            P(("ctx", "fsdp"), None),
            P(("ctx", "fsdp"), None),
            P(("ctx", "fsdp"), None),
            P(("ctx", "fsdp"), None),
            P(None, ("ctx", "fsdp")),
            P(None, ("ctx", "fsdp")),
            P(None, ("ctx", "fsdp")),
            P(("ctx", "fsdp"), None),
            P(("ctx", "fsdp")),
            P(("ctx", "fsdp")),
            P(("ctx", "fsdp")),
            P(("ctx", "fsdp")),
        ),
        check_vma=False,
    )
```

```python
import functools
import math

import jax
import jax.numpy as jnp
from jax import lax
from jax.experimental import pallas as pl
from jax.experimental.pallas import tpu as pltpu
from jax.sharding import PartitionSpec as P

HD = 256
BLK = 32
CONT_LEN = 512
KBLK = 1024


SOFT_CAP = 50.0
MASKED = -1e30
MESH = pl.DeviceIdType.MESH
NT = (((1,), (1,)), ((), ()))
NN = (((1,), (0,)), ((), ()))
TN = (((0,), (0,)), ((), ()))
NORM_EPS = 1e-06
GELU_A = 0.7978845608028654
GELU_B = 0.044715


def mm(left, right, dims):
    return lax.dot_general(left, right, dims, preferred_element_type=jnp.float32)


def spans(total, width):
    return [(at, min(width, total - at)) for at in range(0, total, width)]


def flip(index, bit):
    return index + bit - 2 * bit * ((index // bit) % 2)


def place(fs):
    return lax.axis_index("ctx") * fs + lax.axis_index("fsdp")


def device(index, fs):
    return (index // fs, index % fs)


def remote(src, dst, send, recv, to):
    return pltpu.make_async_remote_copy(
        src_ref=src, dst_ref=dst, send_sem=send, recv_sem=recv, device_id=to, device_id_type=MESH
    )


def line_order(p0, planes):
    few = jnp.minimum(p0, planes - 1 - p0)

    def order(k):
        two_sided = jnp.where(k % 2 == 1, p0 - (k + 1) // 2, p0 + (k + 1) // 2)
        one_sided = jnp.where(p0 > planes - 1 - p0, p0 - (k - few), p0 + (k - few))
        return jnp.where(k <= 2 * few, two_sided, one_sided)

    return order


def neighbours(me, planes, fs):
    p0 = me // 8
    right = device(jnp.minimum(me + 8, 8 * planes - 8 + me % 8), fs)
    left = device(jnp.maximum(me - 8, me % 8), fs)
    return p0, right, left, p0 < planes - 1, p0 > 0


def greet(peers, right, left, has_right, has_left):
    barrier = pltpu.get_barrier_semaphore()
    for peer in peers:
        pl.semaphore_signal(barrier, inc=1, device_id=peer, device_id_type=MESH)

    @pl.when(has_right)
    def _():
        pl.semaphore_signal(barrier, inc=1, device_id=right, device_id_type=MESH)

    @pl.when(has_left)
    def _():
        pl.semaphore_signal(barrier, inc=1, device_id=left, device_id_type=MESH)

    pl.semaphore_wait(
        barrier, len(peers) + jnp.where(has_right, 1, 0) + jnp.where(has_left, 1, 0)
    )


def rows_at(index, size):
    return pl.ds(pl.multiple_of(index * size, size), size)


def line_copies(view, p0, right, left, has_right, has_left, send_sem, recv_sem):
    def copy(p, to, way):
        return remote(view(p), view(p), send_sem.at[way, p], recv_sem.at[p], to)

    def send(p):
        @pl.when(has_right & (p <= p0))
        def _():
            copy(p, right, 0).start()

        @pl.when(has_left & (p >= p0))
        def _():
            copy(p, left, 1).start()

    def arrived(p):
        copy(p, right, 0).wait_recv()

    def drain(p):
        @pl.when(has_right & (p <= p0))
        def _():
            copy(p, right, 0).wait_send()

        @pl.when(has_left & (p >= p0))
        def _():
            copy(p, left, 1).wait_send()

    return send, arrived, drain


def chain_copies(view, slot, p0, planes, right, left, has_right, has_left, send_sem, recv_sem):
    def copy(p, to, into):
        return remote(view(p), slot(into), send_sem.at[p], recv_sem.at[into], to)

    def add(into, p):
        copy(p, right, into).wait_recv()
        mine = view(p)
        mine[...] = (
            mine[...].astype(jnp.float32) + slot(into)[...].astype(jnp.float32)
        ).astype(mine.dtype)

    def onward(p):
        @pl.when((has_left & (p > p0)) | (has_right & (p < p0)))
        def _():
            add(p, p)

        @pl.when(p > p0)
        def _():
            copy(p, right, p).start()

        @pl.when(p < p0)
        def _():
            copy(p, left, jnp.where(p == p0 - 1, planes, p)).start()

    def settle():
        @pl.when(has_left)
        def _():
            add(p0, p0)

        @pl.when(has_right)
        def _():
            add(planes, p0)

    def drain(p):
        @pl.when(p != p0)
        def _():
            copy(p, right, p).wait_send()

    return onward, settle, drain


def summing_levels(planes):
    return [1] + [8 << bit for bit in range(planes.bit_length() - 1)] + [2, 4]


def unit_rows(values):
    inverse = lax.rsqrt(jnp.mean(values * values, axis=-1, keepdims=True) + NORM_EPS)
    return values * inverse, inverse


def turn(values, cosine, sine, back):
    half = values.shape[-1] // 2
    first, second = values[:, :half], values[:, half:]
    if back:
        return jnp.concatenate(
            [first * cosine + second * sine, second * cosine - first * sine], axis=-1
        )
    return jnp.concatenate([first * cosine - second * sine, second * cosine + first * sine], axis=-1)


def attend_kernel(
    planes,
    fs,
    shard,
    x_ref,
    packed_ref,
    gains_ref,
    cos_ref,
    sin_ref,
    qpos_ref,
    kpos_ref,
    ffn_ref,
    across_ref,
    branch_ref,
    w6_ref,
    feats_ref,
    queries_ref,
    kv_ref,
    low_ref,
    mix_ref,
    norm_ref,
    spread_ref,
    w6,
    wrecv,
    whole,
    total,
    part,
    yrecv,
    xrecv,
    grecv,
    xs,
    a2a_s,
    a2a_r,
    n1_s,
    n1_r,
    wz_s,
    wz_r,
    wd_s,
    wd_r,
    kz_s,
    kz_r,
    kd_s,
    kd_r,
    g_s,
    g_r,
    rs_s,
    rs_r,
    ffn_s,
    ffn_r,
    keep,
):
    P = planes
    bf, f32 = jnp.bfloat16, jnp.float32
    width = x_ref.shape[2]
    deep = 8 * shard
    me = place(fs)
    s, hd, c = me % 8, (me % 8) // 2, me % 2
    x0, y0 = hd % 2, hd // 2
    p0, right, left, has_right, has_left = neighbours(me, P, fs)
    order = line_order(p0, P)
    core = device(flip(me, 1), fs)
    xmate = device(flip(me, 2), fs)
    ymate = device(flip(me, 4), fs)
    plane = [(s + d) % 8 for d in range(1, 8)]
    others = [device(p0 * 8 + one, fs) for one in plane]
    levels = summing_levels(P)
    far = [device(flip(me, bit), fs) for bit in levels]
    greet(others + far[2:-2], right, left, has_right, has_left)

    def gain_copy(level):
        return remote(spread_ref, grecv.at[level], g_s.at[level], g_r.at[level], far[level])

    def gain_next(level):
        gain_copy(level).wait()
        spread_ref[...] += grecv[level]
        if level + 1 < len(levels):
            gain_copy(level + 1).start()

    def a2a_copy(d):
        return remote(
            packed_ref.at[plane[d]], wrecv.at[s], a2a_s.at[d], a2a_r.at[d], others[d]
        )

    def x_copy(number, index, to):
        view = xs.at[:, rows_at(index, 64), :]
        return remote(view, view, n1_s.at[number], n1_r.at[number], to)

    def ffn_copy(which):
        return remote(
            ffn_ref.at[which], across_ref.at[which], ffn_s.at[which], ffn_r.at[which], xmate
        )

    spread_ref[...] = gains_ref[...].astype(bf).astype(f32)
    gain_copy(0).start()
    for d in range(7):
        a2a_copy(d).start()
    wrecv[s] = packed_ref[s]
    xs[:, rows_at(hd, 64), :] = x_ref[...]
    for level in range(len(levels) - 2):
        gain_next(level)
    x_copy(0, hd, xmate).start()
    gain_next(len(levels) - 2)
    x_copy(1, hd, ymate).start()
    for which in range(2):
        ffn_copy(which).start()
    for d in range(7):
        a2a_copy(d).wait()
    for one in range(8):
        whole[one * shard : (one + 1) * shard, :] = wrecv[one, :shard, :].astype(f32)
    for j in range(3):
        w6[2 * j + c, rows_at(p0, deep), :] = whole[:, j * HD : (j + 1) * HD].astype(bf)

    def chunk(j):
        def view(p):
            return w6.at[2 * j + c, rows_at(p, deep)]

        send, arrived, drain = line_copies(
            view, p0, right, left, has_right, has_left, wz_s.at[j], wz_r.at[j]
        )

        def over(p):
            return remote(view(p), view(p), wd_s.at[j, p], wd_r.at[j, p], core)

        def begin():
            send(p0)
            over(p0).start()

        def step(k):
            p = order(k)
            arrived(p)
            send(p)
            over(p).start()

        def have():
            for p in range(P):
                over(p).wait_recv()

        def finish():
            for p in range(P):
                over(p).wait_send()
                drain(p)

        return begin, step, have, finish

    begin0, step0, have0, finish0 = chunk(0)
    begin1, step1, have1, finish1 = chunk(1)
    begin2, step2, have2, finish2 = chunk(2)
    begin0()
    x_copy(0, hd, xmate).wait()
    x_copy(2, flip(hd, 1), ymate).start()
    for k in range(1, P):
        step0(k)
    begin1()
    gain_next(len(levels) - 1)
    x_copy(1, hd, ymate).wait()
    x_copy(2, flip(hd, 1), ymate).wait()

    def norm_rows(number, carry):
        for kind in range(2):
            rows = rows_at(number, 64)
            unit, _ = unit_rows(xs[kind, rows, :].astype(f32))
            feats_ref[kind, rows, :] = (unit * spread_ref[0:1, :]).astype(bf)
        return carry

    lax.fori_loop(0, 4, norm_rows, 0)
    have0()

    def kv_rows(p, core_index):
        return rows_at(2 * p + core_index, 256)

    for kind in range(2):
        feats = feats_ref[kind]
        cosine = cos_ref[kind * 256 : (kind + 1) * 256, :]
        sine = sin_ref[kind * 256 : (kind + 1) * 256, :]
        block = kv_rows(p0 if kind == 0 else P, c)
        kv_ref[block, :HD] = turn(mm(feats, w6[0], NN), cosine, sine, False).astype(bf)
        kv_ref[block, HD:] = mm(feats, w6[1], NN).astype(bf)

    def kv_view(p):
        return kv_ref.at[kv_rows(p, c)]

    kv_send, kv_arrived, kv_drain = line_copies(
        kv_view, p0, right, left, has_right, has_left, kz_s, kz_r
    )

    def kv_over(p):
        return remote(kv_view(p), kv_view(p), kd_s.at[p], kd_r.at[p], core)

    kv_send(p0)
    kv_over(p0).start()
    kv_over(P).start()
    for k in range(1, P):
        step1(k)
    have1()
    for kind in range(2):
        feats = feats_ref[kind]
        cosine = cos_ref[kind * 256 : (kind + 1) * 256, :]
        sine = sin_ref[kind * 256 : (kind + 1) * 256, :]
        for head in range(2):
            queries_ref[kind, head * 256 : (head + 1) * 256, :] = turn(
                mm(feats, w6[2 + head], NN), cosine, sine, False
            ).astype(bf)
    for k in range(1, P):
        p = order(k)
        kv_arrived(p)
        kv_send(p)
        kv_over(p).start()
    begin2()
    total[...] = jnp.zeros_like(total)
    mix_ref[...] = jnp.zeros_like(mix_ref)

    def flash(p, kind, masked):
        rows = rows_at(p, 512)
        bent = jnp.tanh(
            mm(queries_ref[kind], kv_ref[rows, :HD], NT) * (HD ** (-0.5) / SOFT_CAP)
        )
        grown = jnp.exp(SOFT_CAP * bent)
        if masked:
            grown = jnp.where(kpos_ref[p] <= qpos_ref[kind], grown, 0.0)
        total[kind] += (
            grown[:, :128] + grown[:, 128:256] + grown[:, 256:384] + grown[:, 384:512]
        )
        mix_ref[kind] += mm(grown.astype(bf), kv_ref[rows, HD:], NN)

    kv_over(P).wait_recv()
    flash(P, 1, True)

    def tile(k, carry):
        p = order(k)
        kv_over(p).wait_recv()
        flash(p, 0, True)
        flash(p, 1, False)

        @pl.when(k > 0)
        def _():
            step2(k)

        return carry

    lax.fori_loop(0, P, tile, 0)
    for kind in range(2):
        inverse = 1.0 / jnp.sum(total[kind], axis=-1, keepdims=True)
        norm_ref[kind] = inverse
        mixed = mix_ref[kind] * inverse
        mix_ref[kind] = mixed
        low_ref[kind] = mixed.astype(bf)
    have2()
    saved = pltpu.make_async_copy(w6, w6_ref, keep)
    saved.start()

    def project(side):
        for kind in range(2):
            picked = pl.ds(pl.multiple_of(side * 128, 128), 128)
            second = pl.ds(pl.multiple_of(256 + side * 128, 128), 128)
            for first, wide in spans(width, 768):
                cols = slice(first, first + wide)
                part[kind, picked, cols] = (
                    mm(low_ref[kind, picked, :], w6[4, cols, :], NT)
                    + mm(low_ref[kind, second, :], w6[5, cols, :], NT)
                ).astype(bf)

    def y_copy(number, index):
        return remote(
            part.at[:, rows_at(index, 64), :],
            yrecv.at[number],
            rs_s.at[number],
            rs_r.at[number],
            ymate,
        )

    project(1 - y0)
    y_copy(0, flip(flip(hd, 2), 1)).start()
    y_copy(1, flip(hd, 2)).start()
    project(y0)
    y_copy(0, 0).wait()
    there = rows_at(flip(hd, 1), 64)
    part[:, there, :] = (part[:, there, :].astype(f32) + yrecv[0].astype(f32)).astype(bf)
    last_copy = remote(part.at[:, there, :], xrecv, rs_s.at[2], rs_r.at[2], xmate)
    last_copy.start()
    y_copy(1, 0).wait()
    last_copy.wait()
    branch_ref[...] = (
        part[:, rows_at(hd, 64), :].astype(f32) + yrecv[1].astype(f32) + xrecv[...].astype(f32)
    )
    for finish in (finish0, finish1, finish2):
        finish()
    for p in range(P):
        kv_drain(p)
        kv_over(p).wait_send()
    kv_over(P).wait_send()
    for which in range(2):
        ffn_copy(which).wait()
    saved.wait()


def attend_call(mesh_shape, shard, x, packed, gains, cosine, sine, qpos, kpos, ffn):
    fs = mesh_shape["fsdp"]
    devices = mesh_shape["ctx"] * fs
    planes = devices // 8
    width = x.shape[2]
    bf, f32 = jnp.bfloat16, jnp.float32
    vmem = pl.BlockSpec(memory_space=pltpu.VMEM)
    hbm = pl.BlockSpec(memory_space=pl.ANY)
    dma = pltpu.SemaphoreType.DMA
    shape = jax.ShapeDtypeStruct
    kv_rows = (2 * planes + 2) * 256
    return pl.pallas_call(
        functools.partial(attend_kernel, planes, fs, shard),
        out_shape=(
            shape((2,) + ffn.shape[1:], bf),
            shape((2, 64, width), f32),
            shape((6, width, HD), bf),
            shape((2, 256, width), bf),
            shape((2, 512, HD), bf),
            shape((kv_rows, 2 * HD), bf),
            shape((2, 512, HD), bf),
            shape((2, 512, HD), f32),
            shape((2, 512, 1), f32),
            shape((8, width), f32),
        ),
        in_specs=[vmem] * 7 + [hbm],
        out_specs=(hbm, vmem, hbm) + (vmem,) * 7,
        scratch_shapes=[
            pltpu.VMEM((6, width, HD), bf),
            pltpu.VMEM(packed.shape, bf),
            pltpu.VMEM((8 * shard, 3 * HD), f32),
            pltpu.VMEM((2, 512, 128), f32),
            pltpu.VMEM((2, 256, width), bf),
            pltpu.VMEM((2, 2, 64, width), bf),
            pltpu.VMEM((2, 64, width), bf),
            pltpu.VMEM((len(summing_levels(planes)), 8, width), f32),
            pltpu.VMEM((2, 256, width), bf),
            dma((7,)),
            dma((7,)),
            dma((3,)),
            dma((3,)),
            dma((3, 2, planes)),
            dma((3, planes)),
            dma((3, planes)),
            dma((3, planes)),
            dma((2, planes)),
            dma((planes,)),
            dma((planes + 1,)),
            dma((planes + 1,)),
            dma((5,)),
            dma((5,)),
            dma((3,)),
            dma((3,)),
            dma((2,)),
            dma((2,)),
            dma,
        ],
        compiler_params=pltpu.CompilerParams(
            collective_id=2, has_side_effects=True, vmem_limit_bytes=56 * 2**20
        ),
        name="attend",
    )(x, packed, gains, cosine, sine, qpos, kpos, ffn)


def retrace_kernel(
    planes,
    fs,
    shard,
    da_ref,
    dh_ref,
    x_ref,
    gain_ref,
    gsum_ref,
    cos_ref,
    sin_ref,
    qpos_ref,
    kpos_ref,
    queries_ref,
    kv_ref,
    low_ref,
    mix_ref,
    norm_ref,
    w6_ref,
    feats_ref,
    dw_ref,
    gin_ref,
    gw_ref,
    gall_ref,
    across_ref,
    w6,
    feats,
    dap,
    dob,
    delta,
    dq,
    dqkv,
    kvg,
    kvd,
    kvz,
    dw6,
    dwd,
    dwz,
    whole,
    asend,
    part,
    yrecv,
    xrecv,
    grecv,
    load,
    a2a_s,
    a2a_r,
    n1_s,
    n1_r,
    wz_s,
    wz_r,
    wd_s,
    wd_r,
    kz_s,
    kz_r,
    kd_s,
    kd_r,
    g_s,
    g_r,
    rs_s,
    rs_r,
    ffn_s,
    ffn_r,
):
    P = planes
    bf, f32 = jnp.bfloat16, jnp.float32
    width = da_ref.shape[2]
    deep = 8 * shard
    me = place(fs)
    s, hd, c = me % 8, (me % 8) // 2, me % 2
    y0 = hd // 2
    p0, right, left, has_right, has_left = neighbours(me, P, fs)
    order = line_order(p0, P)
    core = device(flip(me, 1), fs)
    xmate = device(flip(me, 2), fs)
    ymate = device(flip(me, 4), fs)
    plane = [(s + d) % 8 for d in range(1, 8)]
    others = [device(p0 * 8 + one, fs) for one in plane]
    levels = summing_levels(P)
    far = [device(flip(me, bit), fs) for bit in levels]
    greet(others + far[2:-2], right, left, has_right, has_left)

    def gain_copy(level):
        return remote(gall_ref, grecv.at[level], g_s.at[level], g_r.at[level], far[level])

    def gain_next(level):
        gain_copy(level).wait()
        gall_ref[...] += grecv[level]
        if level + 1 < len(levels):
            gain_copy(level + 1).start()

    def da_copy(number, index, to):
        view = dap.at[:, rows_at(index, 64), :]
        return remote(view, view, n1_s.at[number], n1_r.at[number], to)

    def ffn_copy(which):
        return remote(
            dw_ref.at[which], across_ref.at[which], ffn_s.at[which], ffn_r.at[which], xmate
        )

    dap[:, rows_at(hd, 64), :] = da_ref[...]
    da_copy(0, hd, xmate).start()
    da_copy(1, hd, ymate).start()
    for which in range(2):
        ffn_copy(which).start()
    loads = [
        pltpu.make_async_copy(w6_ref, w6, load.at[0]),
        pltpu.make_async_copy(feats_ref, feats, load.at[1]),
    ]
    for one in loads:
        one.start()
    gall_ref[...] = gsum_ref[...]
    gain_copy(0).start()
    dq[...] = jnp.zeros_like(dq)
    da_copy(0, hd, xmate).wait()
    da_copy(2, flip(hd, 1), ymate).start()
    for one in loads:
        one.wait()
    da_copy(1, hd, ymate).wait()
    da_copy(2, flip(hd, 1), ymate).wait()
    for kind in range(2):
        for head in range(2):
            rows = slice(head * 256, (head + 1) * 256)
            dob[kind, rows, :] = mm(dap[kind], w6[4 + head], NN).astype(bf)
        delta[kind] = jnp.sum(dob[kind].astype(f32) * mix_ref[kind], axis=-1, keepdims=True)

    def weight(index, left_of, right_of):
        for first, wide in spans(width, 768):
            cols = slice(first, first + wide)
            dw6[index, cols, :] = (
                mm(left_of[0, :, cols], right_of(0), TN) + mm(left_of[1, :, cols], right_of(1), TN)
            ).astype(bf)

    def chunk(j):
        def over():
            return remote(
                dw6.at[2 * j + 1 - c], dwd.at[j], wd_s.at[j], wd_r.at[j], core
            )

        def add():
            over().wait_recv()

            def some(p, carry):
                rows = rows_at(p, deep)
                dw6[2 * j + c, rows, :] = (
                    dw6[2 * j + c, rows, :].astype(f32) + dwd[j, rows, :].astype(f32)
                ).astype(bf)
                return carry

            lax.fori_loop(0, P, some, 0)

        onward, settle, drain = chain_copies(
            lambda p: dw6.at[2 * j + c, rows_at(p, deep)],
            lambda into: dwz.at[j, rows_at(into, deep)],
            p0,
            P,
            right,
            left,
            has_right,
            has_left,
            wz_s.at[j],
            wz_r.at[j],
        )

        def finish():
            over().wait_send()
            for p in range(P):
                drain(p)

        return over, add, onward, settle, finish

    over0, add0, onward0, settle0, finish0 = chunk(0)
    over1, add1, onward1, settle1, finish1 = chunk(1)
    over2, add2, onward2, settle2, finish2 = chunk(2)
    for head in range(2):
        weight(4 + head, dap, lambda kind: low_ref[kind, head * 256 : (head + 1) * 256, :])
    over2().start()
    gain_next(0)

    def flash(p, kind, masked):
        rows = rows_at(p, 512)
        keys, values = kv_ref[rows, :HD], kv_ref[rows, HD:]
        bent = jnp.tanh(mm(queries_ref[kind], keys, NT) * (HD ** (-0.5) / SOFT_CAP))
        soft = jnp.exp(SOFT_CAP * bent) * norm_ref[kind]
        if masked:
            soft = jnp.where(kpos_ref[p] <= qpos_ref[kind], soft, 0.0)
        dots = mm(dob[kind], values, NT)
        score = (soft * (dots - delta[kind]) * (1.0 - bent * bent) * HD ** (-0.5)).astype(bf)
        dq[kind] += mm(score, keys, NN)
        return mm(score, queries_ref[kind], TN), mm(soft.astype(bf), dob[kind], TN)

    def half(p, core_index):
        return rows_at(2 * p + core_index, 256)

    def kv_over(p):
        return remote(
            kvg.at[half(p, 1 - c)], kvd.at[rows_at(p, 256)], kd_s.at[p], kd_r.at[p], core
        )

    def kv_add(p):
        kv_over(p).wait_recv()
        rows = half(p, c)
        kvg[rows, :] = (
            kvg[rows, :].astype(f32) + kvd[rows_at(p, 256), :].astype(f32)
        ).astype(bf)

    kv_onward, kv_settle, kv_drain = chain_copies(
        lambda p: kvg.at[half(p, c)],
        lambda into: kvz.at[rows_at(into, 256)],
        p0,
        P,
        right,
        left,
        has_right,
        has_left,
        kz_s,
        kz_r,
    )
    dk, dv = flash(P, 1, True)
    kvg[rows_at(P, 512), :HD] = dk.astype(bf)
    kvg[rows_at(P, 512), HD:] = dv.astype(bf)
    kv_over(P).start()
    add2()

    def tile(j, carry):
        p = order(P - 1 - j)
        dk, dv = flash(p, 0, True)
        more_dk, more_dv = flash(p, 1, False)
        kvg[rows_at(p, 512), :HD] = (dk + more_dk).astype(bf)
        kvg[rows_at(p, 512), HD:] = (dv + more_dv).astype(bf)
        kv_over(p).start()

        @pl.when(j < P - 1)
        def _():
            onward2(p)

        return carry

    lax.fori_loop(0, P, tile, 0)
    gain_next(1)
    for kind in range(2):
        rows = slice(kind * 256, (kind + 1) * 256)
        for head in range(2):
            cols = slice(head * 256, (head + 1) * 256)
            dqkv[2 + head, rows, :] = turn(
                dq[kind, cols, :], cos_ref[rows, :], sin_ref[rows, :], True
            ).astype(bf)
    for head in range(2):
        weight(2 + head, feats, lambda kind: dqkv[2 + head, kind * 256 : (kind + 1) * 256, :])
    over1().start()

    def kv_step(j, carry):
        p = order(P - 1 - j)
        kv_add(p)
        kv_onward(p)
        return carry

    lax.fori_loop(0, P - 1, kv_step, 0)
    settle2()
    add1()

    def q_step(j, carry):
        onward1(order(P - 1 - j))
        return carry

    lax.fori_loop(0, P - 1, q_step, 0)
    kv_add(P)
    kv_add(p0)
    kv_settle()
    for kind in range(2):
        rows = slice(kind * 256, (kind + 1) * 256)
        block = half(p0 if kind == 0 else P, c)
        dqkv[0, rows, :] = turn(
            kvg[block, :HD].astype(f32), cos_ref[rows, :], sin_ref[rows, :], True
        ).astype(bf)
        dqkv[1, rows, :] = kvg[block, HD:]
    for one in range(2):
        weight(one, feats, lambda kind: dqkv[one, kind * 256 : (kind + 1) * 256, :])
    over0().start()

    def project(side):
        for kind in range(2):
            picked = pl.ds(pl.multiple_of(side * 128, 128), 128)
            source = pl.ds(pl.multiple_of(kind * 256 + side * 128, 128), 128)
            for first, wide in spans(width, 768):
                cols = slice(first, first + wide)
                summed = mm(dqkv[0, source, :], w6[0, cols, :], NT)
                for one in range(1, 4):
                    summed = summed + mm(dqkv[one, source, :], w6[one, cols, :], NT)
                part[kind, picked, cols] = summed.astype(bf)

    def y_copy(number, index):
        return remote(
            part.at[:, rows_at(index, 64), :],
            yrecv.at[number],
            rs_s.at[number],
            rs_r.at[number],
            ymate,
        )

    project(1 - y0)
    y_copy(0, flip(flip(hd, 2), 1)).start()
    y_copy(1, flip(hd, 2)).start()
    add0()

    def last_step(j, carry):
        onward0(order(P - 1 - j))
        return carry

    lax.fori_loop(0, P - 1, last_step, 0)
    project(y0)
    y_copy(0, 0).wait()
    there = rows_at(flip(hd, 1), 64)
    part[:, there, :] = (part[:, there, :].astype(f32) + yrecv[0].astype(f32)).astype(bf)
    last_copy = remote(part.at[:, there, :], xrecv, rs_s.at[2], rs_r.at[2], xmate)
    last_copy.start()
    settle1()
    settle0()
    for j in range(3):
        whole[:, j * HD : (j + 1) * HD] = dw6[2 * j + c, rows_at(p0, deep), :].astype(f32)
    asend[...] = jnp.zeros_like(asend)
    for one in range(8):
        asend[one, :shard, :] = whole[one * shard : (one + 1) * shard, :].astype(bf)

    def a2a_copy(d):
        return remote(asend.at[plane[d]], gw_ref.at[s], a2a_s.at[d], a2a_r.at[d], others[d])

    for d in range(7):
        a2a_copy(d).start()
    gw_ref[s] = asend[s]
    y_copy(1, 0).wait()
    last_copy.wait()
    for number in range(2, len(levels)):
        gain_next(number)
    for kind in range(2):
        grads = (
            part[kind, rows_at(hd, 64), :].astype(f32)
            + yrecv[1, kind].astype(f32)
            + xrecv[kind].astype(f32)
        ) * gain_ref[0:1, :]
        unit, inverse = unit_rows(x_ref[kind].astype(f32))
        gin_ref[kind] = (
            dh_ref[kind]
            + inverse * (grads - unit * jnp.mean(grads * unit, axis=-1, keepdims=True))
        ).astype(bf)
    for d in range(7):
        a2a_copy(d).wait()
    for finish in (finish0, finish1, finish2):
        finish()
    for p in range(P):
        kv_drain(p)
        kv_over(p).wait_send()
    kv_over(P).wait_send()
    for which in range(2):
        ffn_copy(which).wait()


def retrace_call(
    mesh_shape, shard, da, dh, x, gain, gsum, cosine, sine, qpos, kpos, saved, partial
):
    w6, feats, queries, kv, low, mix, norm = saved
    fs = mesh_shape["fsdp"]
    planes = mesh_shape["ctx"] * fs // 8
    width = da.shape[2]
    bf, f32 = jnp.bfloat16, jnp.float32
    vmem = pl.BlockSpec(memory_space=pltpu.VMEM)
    hbm = pl.BlockSpec(memory_space=pl.ANY)
    dma = pltpu.SemaphoreType.DMA
    shape = jax.ShapeDtypeStruct
    deep = 8 * shard
    padded = shard + -shard % 16
    levels = len(summing_levels(planes))
    return pl.pallas_call(
        functools.partial(retrace_kernel, planes, fs, shard),
        out_shape=(
            shape((2, 64, width), bf),
            shape((8, padded, 3 * HD), bf),
            shape((8, width), f32),
            shape(partial.shape, bf),
        ),
        in_specs=[vmem] * 14 + [hbm] * 3,
        out_specs=(vmem, vmem, vmem, hbm),
        scratch_shapes=[
            pltpu.VMEM((6, width, HD), bf),
            pltpu.VMEM((2, 256, width), bf),
            pltpu.VMEM((2, 256, width), bf),
            pltpu.VMEM((2, 512, HD), bf),
            pltpu.VMEM((2, 512, 1), f32),
            pltpu.VMEM((2, 512, HD), f32),
            pltpu.VMEM((4, 512, HD), bf),
            pltpu.VMEM(((2 * planes + 2) * 256, 2 * HD), bf),
            pltpu.VMEM(((planes + 1) * 256, 2 * HD), bf),
            pltpu.VMEM(((planes + 1) * 256, 2 * HD), bf),
            pltpu.VMEM((6, width, HD), bf),
            pltpu.VMEM((3, width, HD), bf),
            pltpu.VMEM((3, (planes + 1) * deep, HD), bf),
            pltpu.VMEM((deep, 3 * HD), f32),
            pltpu.VMEM((8, padded, 3 * HD), bf),
            pltpu.VMEM((2, 256, width), bf),
            pltpu.VMEM((2, 2, 64, width), bf),
            pltpu.VMEM((2, 64, width), bf),
            pltpu.VMEM((levels, 8, width), f32),
            dma((2,)),
            dma((7,)),
            dma((7,)),
            dma((3,)),
            dma((3,)),
            dma((3, planes)),
            dma((3, planes + 1)),
            dma((3,)),
            dma((3,)),
            dma((planes,)),
            dma((planes + 1,)),
            dma((planes + 1,)),
            dma((planes + 1,)),
            dma((levels,)),
            dma((levels,)),
            dma((3,)),
            dma((3,)),
            dma((2,)),
            dma((2,)),
        ],
        compiler_params=pltpu.CompilerParams(
            collective_id=3, has_side_effects=True, vmem_limit_bytes=60 * 2**20
        ),
        name="retrace",
    )(da, dh, x, gain, gsum, cosine, sine, qpos, kpos, queries, kv, low, mix, norm, w6, feats, partial)


def ffn_kernel(
    planes,
    fs,
    branch_ref,
    x_ref,
    dy_ref,
    gain_ref,
    own_ref,
    across_ref,
    out_ref,
    dh_ref,
    da_ref,
    gsum_ref,
    dwown_ref,
    dwside_ref,
    dwdown_ref,
    w,
    hidden_in,
    ffn,
    n2all,
    dfall,
    gate,
    up,
    act,
    part,
    yrecv,
    zrecv,
    stage,
    load,
    push_s,
    push_r,
    ag_ys,
    ag_yr,
    ag_zs,
    ag_zr,
    rs_ys,
    rs_yr,
    rs_zs,
    rs_zr,
    dw_s,
    dw_r,
    down_s,
    down_r,
    store,
    ready,
):
    P = planes
    rows, width = x_ref.shape
    slot = own_ref.shape[1]
    hidden = 4 * slot
    bf, f32 = jnp.bfloat16, jnp.float32
    me = place(fs)
    y0 = (me // 4) % 2
    p0, right, left, has_right, has_left = neighbours(me, P, fs)
    order = line_order(p0, P)
    core = device(flip(me, 1), fs)
    xmate = device(flip(me, 2), fs)
    partner = device(flip(me, 4), fs)

    def block(p, y):
        return rows_at(p * 2 + y, rows)

    def pair(p):
        return rows_at(p, 2 * rows)

    def at(p):
        return rows_at(p, rows)

    def some_rows(body):
        def step(number, carry):
            body(rows_at(number, 32))
            return carry

        lax.fori_loop(0, rows // 32, step, 0)

    own_rows = (p0 * 2 + y0) * rows

    def inside(chunk):
        return pl.ds(pl.multiple_of(own_rows + chunk.start, 32), 32)

    local = [
        pltpu.make_async_copy(own_ref.at[which], w.at[which, pl.ds(0, slot)], load.at[which])
        for which in range(3)
    ] + [
        pltpu.make_async_copy(
            across_ref.at[which], w.at[which, pl.ds(slot, slot)], load.at[3 + which]
        )
        for which in range(2)
    ]
    for copy in local:
        copy.start()
    greet([core, xmate, partner], right, left, has_right, has_left)
    pushes = [
        remote(
            own_ref.at[which],
            w.at[which, pl.ds(2 * slot, slot)],
            push_s.at[which],
            push_r.at[which],
            core,
        )
        for which in range(3)
    ] + [
        remote(
            across_ref.at[which],
            w.at[which, pl.ds(3 * slot, slot)],
            push_s.at[3 + which],
            push_r.at[3 + which],
            core,
        )
        for which in range(2)
    ]
    down_across = remote(
        own_ref.at[2], w.at[2, pl.ds(slot, slot)], push_s.at[5], push_r.at[5], xmate
    )
    down_over = remote(
        w.at[2, pl.ds(slot, slot)],
        w.at[2, pl.ds(3 * slot, slot)],
        push_s.at[6],
        push_r.at[6],
        core,
    )
    down_across.start()

    def enter(chunk):
        unit, _ = unit_rows(branch_ref[chunk, :])
        values = x_ref[chunk, :].astype(f32) + unit * gain_ref[1:2, :]
        hidden_in[chunk, :] = values
        unit, _ = unit_rows(values)
        n2all[inside(chunk), :] = (unit * gain_ref[2:3, :]).astype(bf)

    some_rows(enter)

    def gather(buf, turn, compute):
        def y_copy(p, y):
            return remote(
                buf.at[block(p, y)], buf.at[block(p, y)], ag_ys.at[turn, p], ag_yr.at[turn, p], partner
            )

        send, arrived, drain_z = line_copies(
            lambda p: buf.at[block(p, y0)],
            p0,
            right,
            left,
            has_right,
            has_left,
            ag_zs.at[turn],
            ag_zr.at[turn],
        )
        send(p0)
        y_copy(p0, y0).start()
        if turn == 0:
            for copy in pushes:
                copy.start()

        def step(k, carry):
            @pl.when(k < P)
            def _():
                p = order(k)
                arrived(p)
                send(p)
                y_copy(p, y0).start()

            q = order(k - 1)
            y_copy(q, 1 - y0).wait_recv()
            compute(q, k)
            return carry

        lax.fori_loop(1, P + 1, step, 0)

        def drain(p, carry):
            y_copy(p, y0).wait_send()
            drain_z(p)
            return carry

        lax.fori_loop(0, P, drain, 0)

    def scatter(turn, beside):
        def y_copy(p):
            return remote(
                part.at[block(p, 1 - y0)],
                yrecv.at[at(p)],
                rs_ys.at[turn, p],
                rs_yr.at[turn, p],
                partner,
            )

        onward, settle, drain_z = chain_copies(
            lambda p: part.at[block(p, y0)],
            lambda into: zrecv.at[at(into)],
            p0,
            P,
            right,
            left,
            has_right,
            has_left,
            rs_zs.at[turn],
            rs_zr.at[turn],
        )

        def y_add(p):
            y_copy(p).wait_recv()
            part[block(p, y0), :] = (
                part[block(p, y0), :].astype(f32) + yrecv[at(p), :].astype(f32)
            ).astype(bf)

        def start_y(j, carry):
            y_copy(order(P - 1 - j)).start()
            return carry

        lax.fori_loop(0, P, start_y, 0)
        if beside is None:

            def step(j, carry):
                p = order(P - 1 - j)
                y_add(p)
                onward(p)
                return carry

            lax.fori_loop(0, P - 1, step, 0)
        else:
            for j in range(P - 1):
                beside(j)
                p = order(P - 1 - j)
                y_add(p)
                onward(p)
            beside(P - 1)
        y_add(p0)
        settle()
        ffn[...] = part[block(p0, y0), :].astype(f32)

        def drain(p, carry):
            y_copy(p).wait_send()
            drain_z(p)
            return carry

        lax.fori_loop(0, P, drain, 0)

    def forward_down(p):
        for first, wide in spans(width, 768):
            cols = slice(first, first + wide)
            part[pair(p), cols] = mm(act[pair(p), :], w[2, :, cols], NN).astype(bf)

    def forward(p, k):
        @pl.when(k == 1)
        def _():
            for which in (0, 1, 3, 4):
                local[which].wait()
                pushes[which].wait_recv()

        feats = n2all[pair(p), :]
        for first, wide in spans(hidden, 256):
            cols = slice(first, first + wide)
            gates = mm(feats, w[0, cols, :], NT)
            ups = mm(feats, w[1, cols, :], NT)
            bent = jnp.tanh(GELU_A * (gates + GELU_B * gates * gates * gates))
            gate[pair(p), cols] = gates.astype(bf)
            up[pair(p), cols] = ups.astype(bf)
            act[pair(p), cols] = (0.5 * gates * (1.0 + bent) * ups).astype(bf)

        @pl.when(k == P - 2)
        def _():
            down_across.wait_recv()
            down_over.start()

        @pl.when(k == P - 1)
        def _():
            local[2].wait()
            pushes[2].wait_recv()
            down_over.wait_recv()

            def early(number, carry):
                forward_down(order(number))
                return carry

            lax.fori_loop(0, P - 1, early, 0)

        @pl.when(k == P)
        def _():
            forward_down(p)

    gather(n2all, 0, forward)
    scatter(0, None)
    gsum_ref[...] = jnp.zeros_like(gsum_ref)

    def leave(chunk):
        unit, inverse = unit_rows(ffn[chunk, :])
        out_ref[chunk, :] = (hidden_in[chunk, :] + unit * gain_ref[3:4, :]).astype(bf)
        upstream = dy_ref[chunk, :].astype(f32)
        gsum_ref[3:4, :] += jnp.sum(upstream * unit, axis=0, keepdims=True)
        pulled = upstream * gain_ref[3:4, :]
        dfall[inside(chunk), :] = (
            inverse * (pulled - unit * jnp.mean(pulled * unit, axis=-1, keepdims=True))
        ).astype(bf)

    some_rows(leave)

    def backward(p, k):
        grads = dfall[pair(p), :]
        for first, wide in spans(hidden, 256):
            cols = slice(first, first + wide)
            dact = mm(grads, w[2, cols, :], NT)
            gates = gate[pair(p), cols].astype(f32)
            ups = up[pair(p), cols].astype(f32)
            square = gates * gates
            bent = jnp.tanh(GELU_A * (gates + GELU_B * gates * square))
            half = 0.5 * (1.0 + bent)
            slope = half + 0.5 * gates * (1.0 - bent * bent) * (
                GELU_A * (1.0 + 3.0 * GELU_B * square)
            )
            gate[pair(p), cols] = (dact * ups * slope).astype(bf)
            up[pair(p), cols] = (dact * gates * half).astype(bf)
        for first, wide in spans(width, 768):
            cols = slice(first, first + wide)
            part[pair(p), cols] = (
                mm(gate[pair(p), :], w[0, :, cols], NN) + mm(up[pair(p), :], w[1, :, cols], NN)
            ).astype(bf)

    gather(dfall, 1, backward)
    for copy in pushes:
        copy.wait_send()
    down_across.wait_send()
    down_over.wait_send()
    pl.semaphore_signal(ready, inc=1, device_id=core, device_id_type=MESH)
    pl.semaphore_wait(ready, 1)
    chunks = spans(width, 768)
    tasks = [(which, number) for which in (2, 0, 1) for number in range(len(chunks))]

    def dw_push(task):
        which, number = tasks[task]
        cols = pl.ds(*chunks[number])
        return remote(
            w.at[which, pl.ds(2 * slot, 2 * slot), cols],
            w.at[which, pl.ds(0, 2 * slot), cols],
            dw_s.at[task],
            dw_r.at[task],
            core,
        )

    def dw_out(which):
        return pltpu.make_async_copy(w.at[which, pl.ds(0, slot)], dwown_ref.at[which], store.at[which])

    def dw_side(which):
        return pltpu.make_async_copy(
            w.at[which, pl.ds(slot, slot)], dwside_ref.at[which], store.at[3 + which]
        )

    dw_down = remote(w.at[2, pl.ds(slot, slot)], dwdown_ref, down_s, down_r, xmate)

    def dw_finish(task):
        which, number = tasks[task]
        first, wide = chunks[number]
        cols = slice(first, first + wide)
        dw_push(task).wait_recv()
        w[which, : 2 * slot, cols] = (
            stage[task % 2].astype(f32) + w[which, : 2 * slot, cols].astype(f32)
        ).astype(bf)
        if number == len(chunks) - 1:
            dw_out(which).start()
            if which == 2:
                dw_down.start()
            else:
                dw_side(which).start()

    def weight_grad(task):
        which, number = tasks[task]
        first, wide = chunks[number]
        left_side = (gate, up, act)[which]
        right_side = (n2all, n2all, dfall)[which]
        summed = mm(left_side[...], right_side[:, first : first + wide], TN)
        w[which, 2 * slot :, first : first + wide] = summed[2 * slot :].astype(bf)
        stage[task % 2] = summed[: 2 * slot].astype(bf)
        dw_push(task).start()
        if task:
            dw_finish(task - 1)

    shares = [range(0, 4), range(4, 6), range(6, 8), range(8, 9)]

    def beside(j):
        if j < len(shares):
            for task in shares[j]:
                weight_grad(task)

    scatter(1, beside)

    def back(chunk):
        unit, inverse = unit_rows(hidden_in[chunk, :])
        grads = ffn[chunk, :]
        gsum_ref[2:3, :] += jnp.sum(grads * unit, axis=0, keepdims=True)
        pulled = grads * gain_ref[2:3, :]
        dres = dy_ref[chunk, :].astype(f32) + inverse * (
            pulled - unit * jnp.mean(pulled * unit, axis=-1, keepdims=True)
        )
        dh_ref[chunk, :] = dres
        unit, inverse = unit_rows(branch_ref[chunk, :])
        gsum_ref[1:2, :] += jnp.sum(dres * unit, axis=0, keepdims=True)
        pulled = dres * gain_ref[1:2, :]
        da_ref[chunk, :] = (
            inverse * (pulled - unit * jnp.mean(pulled * unit, axis=-1, keepdims=True))
        ).astype(bf)

    some_rows(back)
    dw_finish(len(tasks) - 1)
    for task in range(len(tasks)):
        dw_push(task).wait_send()
    for which in range(3):
        dw_out(which).wait()
    for which in range(2):
        dw_side(which).wait()
    dw_down.wait()


def ffn_call(mesh_shape, branch, x, dy, gain, own, across):
    fs = mesh_shape["fsdp"]
    planes = mesh_shape["ctx"] * fs // 8
    rows, width = x.shape
    slot = own.shape[1]
    hidden = 4 * slot
    tokens = planes * 2 * rows
    bf, f32 = jnp.bfloat16, jnp.float32
    vmem = pl.BlockSpec(memory_space=pltpu.VMEM)
    hbm = pl.BlockSpec(memory_space=pl.ANY)
    dma = pltpu.SemaphoreType.DMA
    shape = jax.ShapeDtypeStruct
    return pl.pallas_call(
        functools.partial(ffn_kernel, planes, fs),
        out_shape=(
            shape((rows, width), bf),
            shape((rows, width), f32),
            shape((rows, width), bf),
            shape((8, width), f32),
            shape((3, slot, width), bf),
            shape((2, slot, width), bf),
            shape((slot, width), bf),
        ),
        in_specs=[vmem, vmem, vmem, vmem, hbm, hbm],
        out_specs=(vmem, vmem, vmem, vmem, hbm, hbm, hbm),
        scratch_shapes=[
            pltpu.VMEM((3, hidden, width), bf),
            pltpu.VMEM((rows, width), f32),
            pltpu.VMEM((rows, width), f32),
            pltpu.VMEM((tokens, width), bf),
            pltpu.VMEM((tokens, width), bf),
            pltpu.VMEM((tokens, hidden), bf),
            pltpu.VMEM((tokens, hidden), bf),
            pltpu.VMEM((tokens, hidden), bf),
            pltpu.VMEM((tokens, width), bf),
            pltpu.VMEM((planes * rows, width), bf),
            pltpu.VMEM(((planes + 1) * rows, width), bf),
            pltpu.VMEM((2, 2 * slot, 768), bf),
            dma((5,)),
            dma((7,)),
            dma((7,)),
            dma((2, planes)),
            dma((2, planes)),
            dma((2, 2, planes)),
            dma((2, planes)),
            dma((2, planes)),
            dma((2, planes)),
            dma((2, planes)),
            dma((2, planes + 1)),
            dma((9,)),
            dma((9,)),
            dma,
            dma,
            dma((5,)),
            pltpu.SemaphoreType.REGULAR,
        ],
        compiler_params=pltpu.CompilerParams(
            collective_id=1, has_side_effects=True, vmem_limit_bytes=62 * 2**20
        ),
        name="ffn",
    )(branch, x, dy, gain, own, across)


CONTRACT_ROWS = (((0,), (0,)), ((), ()))
CONTRACT_COLS = (((1,), (1,)), ((), ()))


def from_partner(array, axis, apart):
    return lax.ppermute(array, axis, [(i, i ^ 1 << apart) for i in range(lax.axis_size(axis))])


def normalize(values):
    inverse = lax.rsqrt(jnp.mean(values * values, axis=-1, keepdims=True) + NORM_EPS)
    return (values * inverse, inverse)


def norm_back(unit_values, inverse, grad_unit):
    return inverse * (
        grad_unit - unit_values * jnp.mean(grad_unit * unit_values, axis=-1, keepdims=True)
    )


def row_meta(blocks, prompt):
    offsets = jnp.arange(BLK, dtype=jnp.int32)
    natural = (blocks[:, None] * BLK + offsets[None, :]).reshape(-1)
    group_span = 2 * prompt
    inner_index = natural % group_span
    group_id = natural // group_span
    in_continuation = inner_index >= prompt
    segment = jnp.where(in_continuation, 1 + (inner_index - prompt) // CONT_LEN, 0)
    position = jnp.where(in_continuation, prompt + (inner_index - prompt) % CONT_LEN, inner_index)
    stride = prompt // CONT_LEN + 1
    return (position, group_id * stride + segment, group_id * stride)


def rope_tables(position):
    frequency = 10000.0 ** (-(jnp.arange(HD // 2, dtype=jnp.float32) * 2.0 / HD))
    angles = position.astype(jnp.float32)[:, None] * frequency[None, :]
    return (jnp.cos(angles), jnp.sin(angles))


def rotate(values, cosine, sine_table):
    half_width = values.shape[-1] // 2
    first_half, second_half = (values[..., :half_width], values[..., half_width:])
    cosine, sine_table = (cosine[:, None, :], sine_table[:, None, :])
    return jnp.concatenate(
        [
            first_half * cosine - second_half * sine_table,
            second_half * cosine + first_half * sine_table,
        ],
        axis=-1,
    )


def unrotate(grads, cosine, sine_table):
    half_width = grads.shape[-1] // 2
    first_half, second_half = (grads[..., :half_width], grads[..., half_width:])
    cosine, sine_table = (cosine[:, None, :], sine_table[:, None, :])
    return jnp.concatenate(
        [
            first_half * cosine + second_half * sine_table,
            second_half * cosine - first_half * sine_table,
        ],
        axis=-1,
    )


def placing(block_table, me, devices, prompt):
    planes = devices // 8
    position = row_meta(block_table, prompt)[0].reshape(planes, 4, 2, 2, 64)
    by_core = position.transpose(0, 2, 3, 1, 4).reshape(planes, 2, 2, 256)
    here = lax.dynamic_index_in_dim(by_core, me // 8, 0, keepdims=False)
    own = lax.dynamic_index_in_dim(here, me % 2, 0, keepdims=False)
    cosine, sine = rope_tables(own.reshape(-1))
    qpos = jnp.tile(own[:, None, :], (1, 2, 1)).reshape(2, 512, 1)
    kpos = jnp.concatenate([by_core[:, :, 0].reshape(planes, 512), here[:, 1].reshape(1, 512)])
    return cosine, sine, qpos, kpos.reshape(planes + 1, 1, 512)


def pack_weights(w_query, w_key, w_value, w_output):
    shard = w_query.shape[0]
    heads, kv = w_query.shape[1] // HD, w_key.shape[1] // HD
    pair = jnp.stack([w_key.reshape(shard, kv, HD), w_value.reshape(shard, kv, HD)], axis=2)
    packed = jnp.concatenate(
        [
            pair.reshape(shard, heads, HD),
            w_query.reshape(shard, heads, HD),
            w_output.T.reshape(shard, heads, HD),
        ],
        axis=-1,
    ).astype(jnp.bfloat16)
    packed = packed.transpose(1, 0, 2)
    return jnp.pad(packed, ((0, 0), (0, -shard % 16), (0, 0)))


def pack_gains(gains, me, width):
    own = jnp.stack(gains).astype(jnp.bfloat16).astype(jnp.float32)
    wide = jnp.zeros((8, width), jnp.float32)
    return lax.dynamic_update_slice(wide, own, (0, me * own.shape[1]))


def visible(query_pos, query_doc, query_base, key_pos, key_doc):
    earlier = key_pos[None, :] <= query_pos[:, None]
    shared = (key_doc[None, :] == query_doc[:, None]) | (key_doc[None, :] == query_base[:, None])
    return earlier & shared


def gated(gate_values, up_values):
    return jax.nn.gelu(gate_values, approximate=True) * up_values


def ffn_gathered(hidden_res, normed_h, upstream, gain_four, w_gate, w_up, w_down):
    bfloat = jnp.bfloat16
    pair_weights = jnp.stack([w_gate, w_up]).astype(bfloat)
    down_local = w_down.astype(bfloat)
    gate_up = jnp.einsum(
        "rd,sdf->rsf",
        lax.all_gather(normed_h, ("ctx", "fsdp"), axis=0, tiled=True),
        pair_weights,
        preferred_element_type=jnp.float32,
    )
    activated = gated(gate_up[:, 0], gate_up[:, 1]).astype(bfloat)
    part_rows = activated
    ffn_raw = lax.psum_scatter(
        jnp.dot(part_rows, down_local, preferred_element_type=jnp.float32).astype(bfloat),
        ("ctx", "fsdp"),
        scatter_dimension=0,
        tiled=True,
    ).astype(jnp.float32)
    unit_f, inv_f = normalize(ffn_raw)
    layer_out = (hidden_res + unit_f * gain_four).astype(bfloat)
    grad_four = jnp.sum(upstream * unit_f, axis=0)
    grad_ffn = norm_back(unit_f, inv_f, upstream * gain_four).astype(bfloat)
    grad_piece = lax.all_gather(grad_ffn, ("ctx", "fsdp"), axis=0, tiled=True)
    normed_piece = lax.all_gather(normed_h, ("ctx", "fsdp"), axis=0, tiled=True)
    act_grad = lax.dot_general(
        grad_piece, down_local, CONTRACT_COLS, preferred_element_type=jnp.float32
    )
    pull_piece = jax.vjp(gated, gate_up[:, 0], gate_up[:, 1])[1]
    gate_grad, up_grad = pull_piece(act_grad)
    pair_low = jnp.stack([gate_grad, up_grad], axis=1).astype(bfloat)
    down_sum = lax.dot_general(
        activated, grad_piece, CONTRACT_ROWS, preferred_element_type=jnp.float32
    )
    pair_sum = jnp.einsum("nd,nsf->sdf", normed_piece, pair_low, preferred_element_type=jnp.float32)
    grad_gate = pair_sum[0]
    grad_up = pair_sum[1]
    part_rows = pair_low
    grad_normed_h = lax.psum_scatter(
        jnp.einsum("nsf,sdf->nd", part_rows, pair_weights, preferred_element_type=jnp.float32).astype(bfloat),
        ("ctx", "fsdp"),
        scatter_dimension=0,
        tiled=True,
    ).astype(jnp.float32)
    return (layer_out, grad_normed_h, grad_four, grad_gate, grad_up, down_sum)


def on_device(
    tokens_in,
    block_table,
    w_query,
    w_key,
    w_value,
    w_output,
    w_gate,
    w_up,
    w_down,
    gain_attn_in,
    gain_attn_out,
    gain_ffn_in,
    gain_ffn_out,
    cotangent,
):
    row_count, model_width = tokens_in.shape
    devices = lax.axis_size(("ctx", "fsdp"))
    slot_count = block_table.shape[0] // devices
    prompt = 2 * devices * BLK
    all_rows = row_count * devices
    device_here = lax.axis_index(("ctx", "fsdp"))
    head_count = w_query.shape[1] // HD
    kv_count = w_key.shape[1] // HD
    groups = head_count // kv_count
    score_scale = HD ** (-0.5)
    bfloat = jnp.bfloat16
    gathered = (
        lax.all_gather(w_query.astype(bfloat), ("ctx", "fsdp"), axis=0, tiled=True),
        lax.all_gather(w_key.astype(bfloat), ("ctx", "fsdp"), axis=0, tiled=True),
        lax.all_gather(w_value.astype(bfloat), ("ctx", "fsdp"), axis=0, tiled=True),
        lax.all_gather(w_output.astype(bfloat), ("ctx", "fsdp"), axis=1, tiled=True),
        lax.all_gather(gain_attn_in.astype(bfloat), ("ctx", "fsdp"), axis=0, tiled=True),
        lax.all_gather(gain_attn_out.astype(bfloat), ("ctx", "fsdp"), axis=0, tiled=True),
        lax.all_gather(gain_ffn_in.astype(bfloat), ("ctx", "fsdp"), axis=0, tiled=True),
        lax.all_gather(gain_ffn_out.astype(bfloat), ("ctx", "fsdp"), axis=0, tiled=True),
    )
    query_weight, key_weight, value_weight, output_weight = (
        gathered[0],
        gathered[1],
        gathered[2],
        gathered[3],
    )
    gain_one = gathered[4].astype(jnp.float32)
    gain_two = gathered[5].astype(jnp.float32)
    gain_three = gathered[6].astype(jnp.float32)
    gain_four = gathered[7].astype(jnp.float32)
    key_meta = row_meta(block_table, prompt)
    key_pos, key_doc = (key_meta[0], key_meta[1])
    my_blocks = lax.dynamic_slice_in_dim(block_table, device_here * slot_count, slot_count)
    query_pos, query_doc, query_base = row_meta(my_blocks, prompt)
    cosine, sine_table = rope_tables(query_pos)
    inputs = tokens_in.astype(jnp.float32)
    unit_x, inv_x = normalize(inputs)
    normed_x = (unit_x * gain_one).astype(bfloat)
    query_raw = jnp.dot(normed_x, query_weight, preferred_element_type=jnp.float32).reshape(
        row_count, head_count, HD
    )
    queries = (
        rotate(query_raw, cosine, sine_table)
        .astype(bfloat)
        .reshape(row_count, kv_count, groups, HD)
    )
    key_raw = jnp.dot(normed_x, key_weight, preferred_element_type=jnp.float32).reshape(
        row_count, kv_count, HD
    )
    keys = rotate(key_raw, cosine, sine_table).astype(bfloat)
    values = (
        jnp.dot(normed_x, value_weight, preferred_element_type=jnp.float32)
        .reshape(row_count, kv_count, HD)
        .astype(bfloat)
    )

    def key_block_meta(first_row, block_width):
        block_pos = lax.dynamic_slice_in_dim(key_pos, first_row, block_width)
        block_doc = lax.dynamic_slice_in_dim(key_doc, first_row, block_width)
        return visible(query_pos, query_doc, query_base, block_pos, block_doc)[:, None, None, :]

    def bent_scores(key_block):
        scores = jnp.einsum(
            "rgjd,kgd->rgjk", queries, key_block, preferred_element_type=jnp.float32
        )
        return jnp.tanh(scores * (score_scale / SOFT_CAP))

    start_state = (
        jnp.full((row_count, kv_count, groups), MASKED, jnp.float32),
        jnp.zeros((row_count, kv_count, groups), jnp.float32),
        jnp.zeros((row_count, kv_count, groups, HD), jnp.float32),
    )
    key_piece = lax.all_gather(keys, ("ctx", "fsdp"), axis=0, tiled=True)
    value_piece = lax.all_gather(values, ("ctx", "fsdp"), axis=0, tiled=True)
    piece_rows = key_piece.shape[0]
    block_width = math.gcd(piece_rows, KBLK)

    def attend_block_step(block_index, state):
        running_max, running_sum, running_out = state
        offset = block_index * block_width
        key_block = lax.dynamic_slice_in_dim(key_piece, offset, block_width, 0)
        value_block = lax.dynamic_slice_in_dim(value_piece, offset, block_width, 0)
        allowed = key_block_meta(offset, block_width)
        capped = jnp.where(allowed, SOFT_CAP * bent_scores(key_block), MASKED)
        fresh_max = jnp.maximum(running_max, jnp.max(capped, axis=-1))
        decay = jnp.exp(running_max - fresh_max)
        weights_soft = jnp.where(allowed, jnp.exp(capped - fresh_max[..., None]), 0.0)
        running_sum = running_sum * decay + jnp.sum(weights_soft, axis=-1)
        running_out = running_out * decay[..., None] + jnp.einsum(
            "rgjk,kgd->rgjd",
            weights_soft.astype(bfloat),
            value_block,
            preferred_element_type=jnp.float32,
        )
        return (fresh_max, running_sum, running_out)

    running_max, running_sum, running_out = lax.fori_loop(
        0, piece_rows // block_width, attend_block_step, start_state
    )
    log_total = running_max + jnp.log(running_sum)
    attended = (running_out / running_sum[..., None]).reshape(row_count, head_count * HD)
    attended_low = attended.astype(bfloat)
    branch_raw = jnp.dot(attended_low, output_weight, preferred_element_type=jnp.float32)
    unit_a, inv_a = normalize(branch_raw)
    hidden_res = inputs + unit_a * gain_two
    unit_h, inv_h = normalize(hidden_res)
    normed_h = (unit_h * gain_three).astype(bfloat)
    upstream = cotangent.astype(jnp.float32)
    layer_out, grad_normed_h, grad_four, grad_gate, grad_up, down_sum = ffn_gathered(
        hidden_res, normed_h, upstream, gain_four, w_gate, w_up, w_down
    )
    grad_three = jnp.sum(grad_normed_h * unit_h, axis=0)
    grad_res = upstream + norm_back(unit_h, inv_h, grad_normed_h * gain_three)
    grad_two = jnp.sum(grad_res * unit_a, axis=0)
    grad_branch = norm_back(unit_a, inv_a, grad_res * gain_two).astype(bfloat)
    grad_att = lax.dot_general(
        grad_branch, output_weight, CONTRACT_COLS, preferred_element_type=jnp.float32
    ).astype(bfloat)
    grad_heads = grad_att.reshape(row_count, kv_count, groups, HD)
    row_delta = jnp.sum(
        grad_heads.astype(jnp.float32) * attended.reshape(row_count, kv_count, groups, HD), axis=-1
    )
    begin_state = (
        jnp.zeros((row_count, kv_count, groups, HD), jnp.float32),
        jnp.zeros((all_rows, kv_count, HD), jnp.float32),
        jnp.zeros((all_rows, kv_count, HD), jnp.float32),
    )
    retrace_key_piece = lax.all_gather(keys, ("ctx", "fsdp"), axis=0, tiled=True)
    retrace_value_piece = lax.all_gather(values, ("ctx", "fsdp"), axis=0, tiled=True)
    piece_rows = retrace_key_piece.shape[0]
    retrace_block_width = math.gcd(piece_rows, KBLK)

    def retrace_block_step(block_index, state):
        query_sum, key_sums, value_sums = state
        offset = block_index * retrace_block_width
        key_block = lax.dynamic_slice_in_dim(retrace_key_piece, offset, retrace_block_width, 0)
        value_block = lax.dynamic_slice_in_dim(retrace_value_piece, offset, retrace_block_width, 0)
        allowed = key_block_meta(offset, retrace_block_width)
        bent = bent_scores(key_block)
        weights_soft = jnp.where(allowed, jnp.exp(SOFT_CAP * bent - log_total[..., None]), 0.0)
        value_dots = jnp.einsum(
            "rgjd,kgd->rgjk", grad_heads, value_block, preferred_element_type=jnp.float32
        )
        score_grad = (
            weights_soft * (value_dots - row_delta[..., None]) * (1.0 - bent * bent) * score_scale
        ).astype(bfloat)
        query_sum = query_sum + jnp.einsum(
            "rgjk,kgd->rgjd", score_grad, key_block, preferred_element_type=jnp.float32
        )
        key_part = jnp.einsum(
            "rgjk,rgjd->kgd", score_grad, queries, preferred_element_type=jnp.float32
        )
        value_part = jnp.einsum(
            "rgjk,rgjd->kgd",
            weights_soft.astype(bfloat),
            grad_heads,
            preferred_element_type=jnp.float32,
        )
        key_sums = lax.dynamic_update_slice_in_dim(key_sums, key_part, offset, 0)
        value_sums = lax.dynamic_update_slice_in_dim(value_sums, value_part, offset, 0)
        return (query_sum, key_sums, value_sums)

    query_sum, key_sums, value_sums = lax.fori_loop(
        0, piece_rows // retrace_block_width, retrace_block_step, begin_state
    )
    mate_count = CONT_LEN // (2 * BLK)
    tail_shape = key_sums.shape[1:]
    key_slots = key_sums.reshape((devices, slot_count, BLK) + tail_shape)
    value_slots = value_sums.reshape((devices, slot_count, BLK) + tail_shape)
    prompt_rows = 2 * BLK * devices
    key_head, value_head = (
        lax.psum_scatter(
            key_slots[:, :2].reshape((prompt_rows,) + tail_shape),
            ("ctx", "fsdp"),
            scatter_dimension=0,
            tiled=True,
        ),
        lax.psum_scatter(
            value_slots[:, :2].reshape((prompt_rows,) + tail_shape),
            ("ctx", "fsdp"),
            scatter_dimension=0,
            tiled=True,
        ),
    )
    group_start = device_here // mate_count * mate_count
    later_both = jnp.stack(
        [
            lax.dynamic_slice_in_dim(key_slots[:, 2:], group_start, mate_count, 0),
            lax.dynamic_slice_in_dim(value_slots[:, 2:], group_start, mate_count, 0),
        ],
        axis=1,
    )
    rank_inner = device_here % mate_count
    for level in reversed(range(mate_count.bit_length() - 1)):
        half_count = later_both.shape[0] // 2
        upper_side = rank_inner >> level & 1 == 1
        lower_half = later_both[:half_count]
        upper_half = later_both[half_count:]
        kept = jnp.where(upper_side, upper_half, lower_half)
        given = jnp.where(upper_side, lower_half, upper_half)
        later_both = kept + from_partner(given.astype(jnp.bfloat16), ("ctx", "fsdp"), level).astype(
            given.dtype
        )
    key_mine = jnp.concatenate(
        [key_head, later_both[0, 0].reshape((2 * BLK,) + tail_shape)], axis=0
    )
    value_mine = jnp.concatenate(
        [value_head, later_both[0, 1].reshape((2 * BLK,) + tail_shape)], axis=0
    )
    grad_q = (
        unrotate(query_sum.reshape(row_count, head_count, HD), cosine, sine_table)
        .reshape(row_count, head_count * HD)
        .astype(bfloat)
    )
    grad_k = unrotate(key_mine, cosine, sine_table).reshape(row_count, kv_count * HD).astype(bfloat)
    grad_v = value_mine.reshape(row_count, kv_count * HD).astype(bfloat)
    grad_normed_x = lax.dot_general(
        grad_q, query_weight, CONTRACT_COLS, preferred_element_type=jnp.float32
    )
    grad_normed_x = grad_normed_x + lax.dot_general(
        grad_k, key_weight, CONTRACT_COLS, preferred_element_type=jnp.float32
    )
    grad_normed_x = grad_normed_x + lax.dot_general(
        grad_v, value_weight, CONTRACT_COLS, preferred_element_type=jnp.float32
    )
    grad_one = jnp.sum(grad_normed_x * unit_x, axis=0)
    grad_in = (grad_res + norm_back(unit_x, inv_x, grad_normed_x * gain_one)).astype(bfloat)
    projection_grads = jnp.concatenate([grad_q, grad_k, grad_v], axis=1)
    input_term = lax.dot_general(
        normed_x, projection_grads, CONTRACT_ROWS, preferred_element_type=jnp.float32
    )
    output_term = lax.dot_general(
        grad_branch, attended_low, CONTRACT_ROWS, preferred_element_type=jnp.float32
    )
    input_share, output_share, share_one, share_two, share_three, share_four = (
        lax.psum_scatter(input_term, ("ctx", "fsdp"), scatter_dimension=0, tiled=True),
        lax.psum_scatter(output_term, ("ctx", "fsdp"), scatter_dimension=0, tiled=True),
        lax.psum_scatter(grad_one, ("ctx", "fsdp"), scatter_dimension=0, tiled=True),
        lax.psum_scatter(grad_two, ("ctx", "fsdp"), scatter_dimension=0, tiled=True),
        lax.psum_scatter(grad_three, ("ctx", "fsdp"), scatter_dimension=0, tiled=True),
        lax.psum_scatter(grad_four, ("ctx", "fsdp"), scatter_dimension=0, tiled=True),
    )
    query_cols = head_count * HD
    key_cols = kv_count * HD
    grad_query = input_share[:, :query_cols]
    grad_key = input_share[:, query_cols : query_cols + key_cols]
    grad_value = input_share[:, query_cols + key_cols :]
    grad_output = output_share.T
    return (
        layer_out,
        grad_in,
        grad_query,
        grad_key,
        grad_value,
        grad_output,
        grad_gate,
        grad_up,
        down_sum,
        share_one,
        share_two,
        share_three,
        share_four,
    )


def kernels_fit(mesh_shape, rows, width, slot):
    planes = mesh_shape["ctx"] * mesh_shape["fsdp"] // 8
    tokens, hidden = planes * 2 * rows, 4 * slot
    wide_rows = 3 * hidden + 3 * tokens + (2 * planes + 1) * rows
    held = 2 * width * wide_rows + 6 * tokens * hidden + 2 * 2 * 768 * hidden
    return rows == 128 and planes == 4 and slot % 16 == 0 and held < 48 * 2**20


def on_device_kernels(
    mesh_shape,
    tokens_in,
    block_table,
    w_query,
    w_key,
    w_value,
    w_output,
    w_gate,
    w_up,
    w_down,
    gain_attn_in,
    gain_attn_out,
    gain_ffn_in,
    gain_ffn_out,
    cotangent,
):
    axes = ("ctx", "fsdp")
    bf, f32 = jnp.bfloat16, jnp.float32
    rows, width = tokens_in.shape
    shard = w_query.shape[0]
    devices = lax.axis_size(axes)
    me = lax.axis_index(axes)
    cosine, sine, qpos, kpos = placing(block_table, me, devices, 2 * devices * BLK)
    packed = pack_weights(w_query, w_key, w_value, w_output)
    gains = pack_gains((gain_attn_in, gain_attn_out, gain_ffn_in, gain_ffn_out), me, width)
    own = jnp.stack([w_gate.T.astype(bf), w_up.T.astype(bf), w_down.astype(bf)])
    split = (2, rows // 2, width)
    x = tokens_in.reshape(split)
    across, branch, *saved, gains = attend_call(
        mesh_shape, shard, x, packed, gains, cosine, sine, qpos, kpos, own
    )
    layer_out, grad_res, grad_branch, sums, mine, side, down = ffn_call(
        mesh_shape, branch.reshape(rows, width), tokens_in, cotangent, gains, own, across
    )
    grad_in, pieces, sums, side = retrace_call(
        mesh_shape,
        shard,
        grad_branch.reshape(split),
        grad_res.reshape(split),
        x,
        gains,
        sums,
        cosine,
        sine,
        qpos,
        kpos,
        saved,
        side,
    )
    pieces = pieces[:, :shard].astype(f32).transpose(1, 0, 2)
    pairs = pieces[:, :, :HD].reshape(shard, -1, 2, HD)
    grad_key = pairs[:, :, 0].reshape(w_key.shape)
    grad_value = pairs[:, :, 1].reshape(w_value.shape)
    grad_query = pieces[:, :, HD : 2 * HD].reshape(w_query.shape)
    grad_output = pieces[:, :, 2 * HD :].reshape(shard, -1).T
    grad_one = (
        jnp.sum(w_query.astype(bf).astype(f32) * grad_query, axis=1)
        + jnp.sum(w_key.astype(bf).astype(f32) * grad_key, axis=1)
        + jnp.sum(w_value.astype(bf).astype(f32) * grad_value, axis=1)
    ) / gain_attn_in.astype(bf).astype(f32)
    shares = lax.dynamic_slice(sums, (1, me * shard), (3, shard))
    return (
        layer_out,
        grad_in.reshape(rows, width),
        grad_query,
        grad_key,
        grad_value,
        grad_output,
        (mine[0].astype(f32) + side[0].astype(f32)).T,
        (mine[1].astype(f32) + side[1].astype(f32)).T,
        mine[2].astype(f32) + down.astype(f32),
        grad_one,
        shares[0],
        shares[1],
        shares[2],
    )


def solution(mesh):
    placed = (
        P(("ctx", "fsdp"), None),
        P(),
        P(("ctx", "fsdp"), None),
        P(("ctx", "fsdp"), None),
        P(("ctx", "fsdp"), None),
        P(None, ("ctx", "fsdp")),
        P(None, ("ctx", "fsdp")),
        P(None, ("ctx", "fsdp")),
        P(("ctx", "fsdp"), None),
        P(("ctx", "fsdp")),
        P(("ctx", "fsdp")),
        P(("ctx", "fsdp")),
        P(("ctx", "fsdp")),
        P(("ctx", "fsdp"), None),
    )
    shape = dict(mesh.shape)

    def program(tokens_in, *others):
        devices = shape["ctx"] * shape["fsdp"]
        rows, width = tokens_in.shape
        slot = others[7].shape[0] // devices
        if kernels_fit(shape, rows // devices, width, slot):
            body = functools.partial(on_device_kernels, shape)
        else:
            body = on_device
        return placed_over(mesh, placed, body)(tokens_in, *others)

    return program


def placed_over(mesh, placed, body):
    return jax.shard_map(
        body,
        mesh=mesh,
        in_specs=placed,
        out_specs=(
            P(("ctx", "fsdp"), None),
            P(("ctx", "fsdp"), None),
            P(("ctx", "fsdp"), None),
            P(("ctx", "fsdp"), None),
            P(("ctx", "fsdp"), None),
            P(None, ("ctx", "fsdp")),
            P(None, ("ctx", "fsdp")),
            P(None, ("ctx", "fsdp")),
            P(("ctx", "fsdp"), None),
            P(("ctx", "fsdp")),
            P(("ctx", "fsdp")),
            P(("ctx", "fsdp")),
            P(("ctx", "fsdp")),
        ),
        check_vma=False,
    )
```

```python
import functools
import math

import jax
import jax.numpy as jnp
from jax import lax
from jax.experimental import pallas as pl
from jax.experimental.pallas import tpu as pltpu
from jax.sharding import PartitionSpec as P

HD = 256
BLK = 32
CONT_LEN = 512
KBLK = 1024


SOFT_CAP = 50.0
MASKED = -1e30
MESH = pl.DeviceIdType.MESH
NT = (((1,), (1,)), ((), ()))
NN = (((1,), (0,)), ((), ()))
TN = (((0,), (0,)), ((), ()))
NORM_EPS = 1e-06
GELU_A = 0.7978845608028654
GELU_B = 0.044715


def mm(left, right, dims):
    return lax.dot_general(left, right, dims, preferred_element_type=jnp.float32)


def spans(total, width):
    return [(at, min(width, total - at)) for at in range(0, total, width)]


def flip(index, bit):
    return index + bit - 2 * bit * ((index // bit) % 2)


def place(fs):
    return lax.axis_index("ctx") * fs + lax.axis_index("fsdp")


def device(index, fs):
    return (index // fs, index % fs)


def remote(src, dst, send, recv, to):
    return pltpu.make_async_remote_copy(
        src_ref=src, dst_ref=dst, send_sem=send, recv_sem=recv, device_id=to, device_id_type=MESH
    )


def line_order(p0, planes):
    few = jnp.minimum(p0, planes - 1 - p0)

    def order(k):
        two_sided = jnp.where(k % 2 == 1, p0 - (k + 1) // 2, p0 + (k + 1) // 2)
        one_sided = jnp.where(p0 > planes - 1 - p0, p0 - (k - few), p0 + (k - few))
        return jnp.where(k <= 2 * few, two_sided, one_sided)

    return order


def neighbours(me, planes, fs):
    p0 = me // 8
    right = device(jnp.minimum(me + 8, 8 * planes - 8 + me % 8), fs)
    left = device(jnp.maximum(me - 8, me % 8), fs)
    return p0, right, left, p0 < planes - 1, p0 > 0


def greet(peers, right, left, has_right, has_left):
    barrier = pltpu.get_barrier_semaphore()
    for peer in peers:
        pl.semaphore_signal(barrier, inc=1, device_id=peer, device_id_type=MESH)

    @pl.when(has_right)
    def _():
        pl.semaphore_signal(barrier, inc=1, device_id=right, device_id_type=MESH)

    @pl.when(has_left)
    def _():
        pl.semaphore_signal(barrier, inc=1, device_id=left, device_id_type=MESH)

    pl.semaphore_wait(
        barrier, len(peers) + jnp.where(has_right, 1, 0) + jnp.where(has_left, 1, 0)
    )


def rows_at(index, size):
    return pl.ds(pl.multiple_of(index * size, size), size)


def line_copies(view, p0, right, left, has_right, has_left, send_sem, recv_sem):
    def copy(p, to, way):
        return remote(view(p), view(p), send_sem.at[way, p], recv_sem.at[p], to)

    def send(p):
        @pl.when(has_right & (p <= p0))
        def _():
            copy(p, right, 0).start()

        @pl.when(has_left & (p >= p0))
        def _():
            copy(p, left, 1).start()

    def arrived(p):
        copy(p, right, 0).wait_recv()

    def drain(p):
        @pl.when(has_right & (p <= p0))
        def _():
            copy(p, right, 0).wait_send()

        @pl.when(has_left & (p >= p0))
        def _():
            copy(p, left, 1).wait_send()

    return send, arrived, drain


def chain_copies(view, slot, p0, planes, right, left, has_right, has_left, send_sem, recv_sem):
    def copy(p, to, into):
        return remote(view(p), slot(into), send_sem.at[p], recv_sem.at[into], to)

    def add(into, p):
        copy(p, right, into).wait_recv()
        mine = view(p)
        mine[...] = (
            mine[...].astype(jnp.float32) + slot(into)[...].astype(jnp.float32)
        ).astype(mine.dtype)

    def onward(p):
        @pl.when((has_left & (p > p0)) | (has_right & (p < p0)))
        def _():
            add(p, p)

        @pl.when(p > p0)
        def _():
            copy(p, right, p).start()

        @pl.when(p < p0)
        def _():
            copy(p, left, jnp.where(p == p0 - 1, planes, p)).start()

    def settle():
        @pl.when(has_left)
        def _():
            add(p0, p0)

        @pl.when(has_right)
        def _():
            add(planes, p0)

    def drain(p):
        @pl.when(p != p0)
        def _():
            copy(p, right, p).wait_send()

    return onward, settle, drain


def summing_levels(planes):
    return [2, 4, 1] + [8 << bit for bit in range(planes.bit_length() - 1)]


def unit_rows(values):
    inverse = lax.rsqrt(jnp.mean(values * values, axis=-1, keepdims=True) + NORM_EPS)
    return values * inverse, inverse


def plane_gather(buf, hd, xmate, ymate, send_sem, recv_sem):
    def copy(number, rows, to):
        view = buf.at[:, rows, :]
        return remote(view, view, send_sem.at[number], recv_sem.at[number], to)

    def part_of(index, lower):
        return pl.ds(pl.multiple_of(index * 64 + 32 * lower, 32), 32)

    own_x = copy(0, rows_at(hd, 64), xmate)
    own_y = copy(1, rows_at(hd, 64), ymate)
    on_y = copy(2, part_of(flip(hd, 1), 0), ymate)
    on_x = copy(3, part_of(flip(hd, 2), 1), xmate)
    return own_x, own_y, on_y, on_x


def plane_sum(part, wide, hd, xmate, ymate, yhalf, xhalf, yfull, xfull, send_sem, recv_sem):
    xm, ym = flip(hd, 1), flip(hd, 2)
    dg = flip(xm, 2)

    def cols(h):
        return pl.ds(pl.multiple_of(h * wide, 128), wide)

    def part_of(index, lower):
        return pl.ds(pl.multiple_of(index * 64 + 32 * lower, 32), 32)

    def copy(h, number):
        rows, into, to = routes[number]
        return remote(
            part.at[:, rows, cols(h)],
            into.at[h],
            send_sem.at[h, number],
            recv_sem.at[h, number],
            to,
        )

    routes = (
        (part_of(dg, 0), yhalf, ymate),
        (part_of(dg, 1), xhalf, xmate),
        (rows_at(xm, 64), xfull, xmate),
        (rows_at(ym, 64), yfull, ymate),
    )

    def first(h):
        for number in range(2):
            copy(h, number).start()

    def second(h):
        for number, rows, came in ((0, part_of(xm, 0), yhalf), (1, part_of(ym, 1), xhalf)):
            copy(h, number).wait_recv()
            part[:, rows, cols(h)] = (
                part[:, rows, cols(h)].astype(jnp.float32) + came[h].astype(jnp.float32)
            ).astype(part.dtype)
            copy(h, number + 2).start()

    def last(h):
        for number in (2, 3):
            copy(h, number).wait_recv()
        return (
            part[:, rows_at(hd, 64), cols(h)].astype(jnp.float32)
            + yfull[h].astype(jnp.float32)
            + xfull[h].astype(jnp.float32)
        )

    def drain(h):
        for number in range(4):
            copy(h, number).wait_send()

    return cols, first, second, last, drain


def plane_scratch(width):
    bf = jnp.bfloat16
    wide = width // 2
    return [
        pltpu.VMEM((2, 2, 32, wide), bf),
        pltpu.VMEM((2, 2, 32, wide), bf),
        pltpu.VMEM((2, 2, 64, wide), bf),
        pltpu.VMEM((2, 2, 64, wide), bf),
        pltpu.SemaphoreType.DMA((2, 4)),
        pltpu.SemaphoreType.DMA((2, 4)),
    ]


def turn(values, cosine, sine, back):
    half = values.shape[-1] // 2
    first, second = values[:, :half], values[:, half:]
    if back:
        return jnp.concatenate(
            [first * cosine + second * sine, second * cosine - first * sine], axis=-1
        )
    return jnp.concatenate([first * cosine - second * sine, second * cosine + first * sine], axis=-1)


def attend_kernel(
    planes,
    fs,
    shard,
    x_ref,
    packed_ref,
    gains_ref,
    cos_ref,
    sin_ref,
    qpos_ref,
    kpos_ref,
    ffn_ref,
    across_ref,
    branch_ref,
    w6_out,
    feats_out,
    queries_out,
    kv_out,
    low_out,
    mix_out,
    norm_ref,
    spread_ref,
    w6,
    feats_ref,
    queries_ref,
    kv_ref,
    low_ref,
    mix_ref,
    wrecv,
    whole,
    total,
    part,
    yhalf,
    xhalf,
    yfull,
    xfull,
    rs_s,
    rs_r,
    grecv,
    xs,
    a2a_s,
    a2a_r,
    n1_s,
    n1_r,
    wz_s,
    wz_r,
    wd_s,
    wd_r,
    kz_s,
    kz_r,
    kd_s,
    kd_r,
    g_s,
    g_r,
    ffn_s,
    ffn_r,
    keep,
):
    P = planes
    bf, f32 = jnp.bfloat16, jnp.float32
    width = x_ref.shape[2]
    deep = 8 * shard
    me = place(fs)
    s, hd, c = me % 8, (me % 8) // 2, me % 2
    p0, right, left, has_right, has_left = neighbours(me, P, fs)
    order = line_order(p0, P)
    core = device(flip(me, 1), fs)
    xmate = device(flip(me, 2), fs)
    ymate = device(flip(me, 4), fs)
    plane = [(s + d) % 8 for d in range(1, 8)]
    others = [device(p0 * 8 + one, fs) for one in plane]
    levels = summing_levels(P)
    far = [device(flip(me, bit), fs) for bit in levels]
    greet(others + far[4:], right, left, has_right, has_left)

    kept = [
        pltpu.make_async_copy(held, out, keep.at[number])
        for number, (held, out) in enumerate(
            (
                (w6, w6_out),
                (feats_ref, feats_out),
                (queries_ref, queries_out),
                (kv_ref, kv_out),
                (low_ref, low_out),
                (mix_ref, mix_out),
            )
        )
    ]

    def keep_all(first, last):
        for one in kept[first:last]:
            one.start()

    def gain_copy(level):
        return remote(spread_ref, grecv.at[level], g_s.at[level], g_r.at[level], far[level])

    def gain_next(level):
        gain_copy(level).wait()
        spread_ref[...] += grecv[level]
        if level + 1 < len(levels):
            gain_copy(level + 1).start()

    def a2a_copy(j, d):
        return remote(
            packed_ref.at[plane[d], j], wrecv.at[s, j], a2a_s.at[j, d], a2a_r.at[j, d], others[d]
        )

    own_x, own_y, on_y, on_x = plane_gather(xs, hd, xmate, ymate, n1_s, n1_r)

    def ffn_copy(which):
        return remote(
            ffn_ref.at[which], across_ref.at[which], ffn_s.at[which], ffn_r.at[which], xmate
        )

    spread_ref[...] = gains_ref[...].astype(bf).astype(f32)
    gain_copy(0).start()
    def a2a_start(j):
        for d in range(7):
            a2a_copy(j, d).start()

    a2a_start(0)
    wrecv[s] = packed_ref[s]
    xs[:, rows_at(hd, 64), :] = x_ref[...]
    gain_next(0)
    a2a_start(1)
    own_x.start()
    own_y.start()
    gain_next(1)

    def assemble(j):
        for d in range(7):
            a2a_copy(j, d).wait_recv()
        for one in range(8):
            whole[one * shard : (one + 1) * shard, :] = wrecv[one, j, :shard, :].astype(f32)
        w6[2 * j + c, rows_at(p0, deep), :] = whole[...].astype(bf)

    def chunk(j):
        def view(p):
            return w6.at[2 * j + c, rows_at(p, deep)]

        send, arrived, drain = line_copies(
            view, p0, right, left, has_right, has_left, wz_s.at[j], wz_r.at[j]
        )

        def over(p):
            return remote(view(p), view(p), wd_s.at[j, p], wd_r.at[j, p], core)

        def begin():
            send(p0)
            over(p0).start()

        def step(k):
            p = order(k)
            arrived(p)
            send(p)
            over(p).start()

        def have(p):
            over(p).wait_recv()

        def finish():
            for p in range(P):
                over(p).wait_send()
                drain(p)

        return begin, step, have, finish

    begin0, step0, have0, finish0 = chunk(0)
    begin1, step1, have1, finish1 = chunk(1)
    begin2, step2, have2, finish2 = chunk(2)
    assemble(0)
    begin0()
    gain_next(2)
    assemble(1)
    for k in range(1, P):
        step0(k)
        if k + 2 < len(levels):
            gain_next(k + 2)
        if k == 1:
            own_x.wait_recv()
            on_y.start()
        if k == 2:
            own_y.wait_recv()
            on_x.start()
            a2a_start(2)
            for which in range(2):
                ffn_copy(which).start()
    begin1()
    for level in range(P + 2, len(levels)):
        gain_next(level)
    on_y.wait_recv()
    on_x.wait_recv()

    def norm_rows(number, carry):
        for kind in range(2):
            rows = rows_at(number, 64)
            unit, _ = unit_rows(xs[kind, rows, :].astype(f32))
            feats_ref[kind, rows, :] = (unit * spread_ref[0:1, :]).astype(bf)
        return carry

    lax.fori_loop(0, 4, norm_rows, 0)
    for p in range(P):
        have0(p)

    def kv_rows(p, core_index):
        return rows_at(2 * p + core_index, 256)

    for kind in range(2):
        feats = feats_ref[kind]
        cosine = cos_ref[kind * 256 : (kind + 1) * 256, :]
        sine = sin_ref[kind * 256 : (kind + 1) * 256, :]
        block = kv_rows(p0 if kind == 0 else P, c)
        kv_ref[block, :HD] = turn(mm(feats, w6[0], NN), cosine, sine, False).astype(bf)
        kv_ref[block, HD:] = mm(feats, w6[1], NN).astype(bf)

    def kv_view(p):
        return kv_ref.at[kv_rows(p, c)]

    kv_send, kv_arrived, kv_drain = line_copies(
        kv_view, p0, right, left, has_right, has_left, kz_s, kz_r
    )

    def kv_over(p):
        return remote(kv_view(p), kv_view(p), kd_s.at[p], kd_r.at[p], core)

    kv_send(p0)
    kv_over(p0).start()
    kv_over(P).start()
    for k in range(1, P):
        step1(k)
    for p in range(P):
        have1(p)
    for kind in range(2):
        feats = feats_ref[kind]
        cosine = cos_ref[kind * 256 : (kind + 1) * 256, :]
        sine = sin_ref[kind * 256 : (kind + 1) * 256, :]
        for head in range(2):
            queries_ref[kind, head * 256 : (head + 1) * 256, :] = turn(
                mm(feats, w6[2 + head], NN), cosine, sine, False
            ).astype(bf)
    for k in range(1, P):
        p = order(k)
        kv_arrived(p)
        kv_send(p)
        kv_over(p).start()
    assemble(2)
    begin2()
    total[...] = jnp.zeros_like(total)
    mix_ref[...] = jnp.zeros_like(mix_ref)

    def flash(p, kind, masked):
        rows = rows_at(p, 512)
        bent = jnp.tanh(
            mm(queries_ref[kind], kv_ref[rows, :HD], NT) * (HD ** (-0.5) / SOFT_CAP)
        )
        grown = jnp.exp(SOFT_CAP * bent)
        if masked:
            grown = jnp.where(kpos_ref[p] <= qpos_ref[kind], grown, 0.0)
        total[kind] += (
            grown[:, :128] + grown[:, 128:256] + grown[:, 256:384] + grown[:, 384:512]
        )
        mix_ref[kind] += mm(grown.astype(bf), kv_ref[rows, HD:], NN)

    kv_over(P).wait_recv()
    flash(P, 1, True)

    def tile(k, carry):
        p = order(k)
        kv_over(p).wait_recv()
        flash(p, 0, True)
        flash(p, 1, False)

        @pl.when((k > 0) & (k < P - 1))
        def _():
            step2(k)

        return carry

    lax.fori_loop(0, P, tile, 0)
    for kind in range(2):
        inverse = 1.0 / jnp.sum(total[kind], axis=-1, keepdims=True)
        norm_ref[kind] = inverse
        mixed = mix_ref[kind] * inverse
        mix_ref[kind] = mixed
        low_ref[kind] = mixed.astype(bf)
    wide = width // 2
    cols, first, second, last, drain_sum = plane_sum(
        part, wide, hd, xmate, ymate, yhalf, xhalf, yfull, xfull, rs_s, rs_r
    )

    def project(h):
        for p in range(P // 2):
            have2(h * (P // 2) + p)
        for kind in range(2):
            for at, size in spans(wide, 384):
                rows = pl.ds(pl.multiple_of(h * wide + at, 128), size)
                part[kind, :, rows] = (
                    mm(low_ref[kind, :256, :], w6[4, rows, :], NT)
                    + mm(low_ref[kind, 256:, :], w6[5, rows, :], NT)
                ).astype(bf)
        first(h)

    near = p0 // (P // 2)
    keep_all(1, 6)
    project(near)
    step2(P - 1)
    second(near)
    project(1 - near)
    keep_all(0, 1)
    second(1 - near)
    for h in range(2):
        branch_ref[:, :, h * wide : (h + 1) * wide] = last(h)
    for h in range(2):
        drain_sum(h)
    for one in (own_x, own_y, on_y, on_x):
        one.wait_send()
    for j in range(3):
        for d in range(7):
            a2a_copy(j, d).wait_send()
    for finish in (finish0, finish1, finish2):
        finish()
    for p in range(P):
        kv_drain(p)
        kv_over(p).wait_send()
    kv_over(P).wait_send()
    for which in range(2):
        ffn_copy(which).wait()
    for one in kept:
        one.wait()


def attend_call(mesh_shape, shard, x, packed, gains, cosine, sine, qpos, kpos, ffn):
    fs = mesh_shape["fsdp"]
    devices = mesh_shape["ctx"] * fs
    planes = devices // 8
    width = x.shape[2]
    bf, f32 = jnp.bfloat16, jnp.float32
    vmem = pl.BlockSpec(memory_space=pltpu.VMEM)
    hbm = pl.BlockSpec(memory_space=pl.ANY)
    dma = pltpu.SemaphoreType.DMA
    shape = jax.ShapeDtypeStruct
    kv_rows = (2 * planes + 2) * 256
    return pl.pallas_call(
        functools.partial(attend_kernel, planes, fs, shard),
        out_shape=(
            shape((2,) + ffn.shape[1:], bf),
            shape((2, 64, width), f32),
            shape((6, width, HD), bf),
            shape((2, 256, width), bf),
            shape((2, 512, HD), bf),
            shape((kv_rows, 2 * HD), bf),
            shape((2, 512, HD), bf),
            shape((2, 512, HD), f32),
            shape((2, 512, 1), f32),
            shape((8, width), f32),
        ),
        in_specs=[vmem] * 7 + [hbm],
        out_specs=(hbm, vmem) + (hbm,) * 6 + (vmem,) * 2,
        scratch_shapes=[
            pltpu.VMEM((6, width, HD), bf),
            pltpu.VMEM((2, 256, width), bf),
            pltpu.VMEM((2, 512, HD), bf),
            pltpu.VMEM((kv_rows, 2 * HD), bf),
            pltpu.VMEM((2, 512, HD), bf),
            pltpu.VMEM((2, 512, HD), f32),
            pltpu.VMEM(packed.shape, bf),
            pltpu.VMEM((8 * shard, HD), f32),
            pltpu.VMEM((2, 512, 128), f32),
            pltpu.VMEM((2, 256, width), bf),
            *plane_scratch(width),
            pltpu.VMEM((len(summing_levels(planes)), 8, width), f32),
            pltpu.VMEM((2, 256, width), bf),
            dma((3, 7)),
            dma((3, 7)),
            dma((4,)),
            dma((4,)),
            dma((3, 2, planes)),
            dma((3, planes)),
            dma((3, planes)),
            dma((3, planes)),
            dma((2, planes)),
            dma((planes,)),
            dma((planes + 1,)),
            dma((planes + 1,)),
            dma((5,)),
            dma((5,)),
            dma((2,)),
            dma((2,)),
            dma((6,)),
        ],
        compiler_params=pltpu.CompilerParams(
            collective_id=2, has_side_effects=True, vmem_limit_bytes=56 * 2**20
        ),
        name="attend",
    )(x, packed, gains, cosine, sine, qpos, kpos, ffn)


def retrace_kernel(
    planes,
    fs,
    shard,
    da_ref,
    dh_ref,
    x_ref,
    gain_ref,
    gsum_ref,
    cos_ref,
    sin_ref,
    qpos_ref,
    kpos_ref,
    norm_ref,
    w6_in,
    feats_in,
    queries_in,
    kv_in,
    low_in,
    mix_in,
    dw_ref,
    gin_ref,
    gw_ref,
    gall_ref,
    across_ref,
    w6,
    feats,
    queries_ref,
    kv_ref,
    low_ref,
    mix_ref,
    dap,
    dob,
    delta,
    dq,
    dqkv,
    kvg,
    kvd,
    kvz,
    dw6,
    dwd,
    dwz,
    whole,
    asend,
    dn1,
    part,
    yhalf,
    xhalf,
    yfull,
    xfull,
    rs_s,
    rs_r,
    grecv,
    load,
    a2a_s,
    a2a_r,
    n1_s,
    n1_r,
    wz_s,
    wz_r,
    wd_s,
    wd_r,
    kz_s,
    kz_r,
    kd_s,
    kd_r,
    g_s,
    g_r,
    ffn_s,
    ffn_r,
):
    P = planes
    bf, f32 = jnp.bfloat16, jnp.float32
    width = da_ref.shape[2]
    deep = 8 * shard
    me = place(fs)
    s, hd, c = me % 8, (me % 8) // 2, me % 2
    p0, right, left, has_right, has_left = neighbours(me, P, fs)
    order = line_order(p0, P)
    core = device(flip(me, 1), fs)
    xmate = device(flip(me, 2), fs)
    ymate = device(flip(me, 4), fs)
    plane = [(s + d) % 8 for d in range(1, 8)]
    others = [device(p0 * 8 + one, fs) for one in plane]
    levels = summing_levels(P)
    far = [device(flip(me, bit), fs) for bit in levels]
    greet(others + far[4:], right, left, has_right, has_left)

    def gain_copy(level):
        return remote(gall_ref, grecv.at[level], g_s.at[level], g_r.at[level], far[level])

    def gain_next(level):
        gain_copy(level).wait()
        gall_ref[...] += grecv[level]
        if level + 1 < len(levels):
            gain_copy(level + 1).start()

    own_x, own_y, on_y, on_x = plane_gather(dap, hd, xmate, ymate, n1_s, n1_r)

    def ffn_copy(which):
        return remote(
            dw_ref.at[which], across_ref.at[which], ffn_s.at[which], ffn_r.at[which], xmate
        )

    dap[:, rows_at(hd, 64), :] = da_ref[...]
    gall_ref[...] = gsum_ref[...]
    gain_copy(0).start()
    own_x.start()
    own_y.start()
    loads = [
        pltpu.make_async_copy(source, held, load.at[number])
        for number, (source, held) in enumerate(
            (
                (w6_in, w6),
                (low_in, low_ref),
                (mix_in, mix_ref),
                (queries_in, queries_ref),
                (kv_in, kv_ref),
                (feats_in, feats),
            )
        )
    ]
    for one in loads:
        one.start()
    dq[...] = jnp.zeros_like(dq)
    asend[...] = jnp.zeros_like(asend)
    gain_next(0)
    own_x.wait_recv()
    on_y.start()
    own_y.wait_recv()
    on_x.start()
    for which in range(2):
        ffn_copy(which).start()
    for one in loads:
        one.wait()
    gain_next(1)
    on_y.wait_recv()
    on_x.wait_recv()
    for kind in range(2):
        for head in range(2):
            rows = slice(head * 256, (head + 1) * 256)
            dob[kind, rows, :] = mm(dap[kind], w6[4 + head], NN).astype(bf)
        delta[kind] = jnp.sum(dob[kind].astype(f32) * mix_ref[kind], axis=-1, keepdims=True)

    def weight(index, left_of, right_of):
        for first, wide in spans(width, 768):
            cols = slice(first, first + wide)
            dw6[index, cols, :] = (
                mm(left_of[0, :, cols], right_of(0), TN) + mm(left_of[1, :, cols], right_of(1), TN)
            ).astype(bf)

    def chunk(j):
        def over():
            return remote(
                dw6.at[2 * j + 1 - c], dwd.at[j], wd_s.at[j], wd_r.at[j], core
            )

        def add():
            over().wait_recv()

            def some(p, carry):
                rows = rows_at(p, deep)
                dw6[2 * j + c, rows, :] = (
                    dw6[2 * j + c, rows, :].astype(f32) + dwd[j, rows, :].astype(f32)
                ).astype(bf)
                return carry

            lax.fori_loop(0, P, some, 0)

        onward, settle, drain = chain_copies(
            lambda p: dw6.at[2 * j + c, rows_at(p, deep)],
            lambda into: dwz.at[j, rows_at(into, deep)],
            p0,
            P,
            right,
            left,
            has_right,
            has_left,
            wz_s.at[j],
            wz_r.at[j],
        )

        def finish():
            over().wait_send()
            for p in range(P):
                drain(p)

        return over, add, onward, settle, finish

    def a2a_copy(j, d):
        return remote(
            asend.at[plane[d], j], gw_ref.at[s, j], a2a_s.at[j, d], a2a_r.at[j, d], others[d]
        )

    def spread(j):
        whole[...] = dw6[2 * j + c, rows_at(p0, deep), :].astype(f32)
        for one in range(8):
            asend[one, j, :shard, :] = whole[one * shard : (one + 1) * shard, :].astype(bf)
        for d in range(7):
            a2a_copy(j, d).start()
        gw_ref[s, j] = asend[s, j]

    over0, add0, onward0, settle0, finish0 = chunk(0)
    over1, add1, onward1, settle1, finish1 = chunk(1)
    over2, add2, onward2, settle2, finish2 = chunk(2)
    for head in range(2):
        weight(4 + head, dap, lambda kind: low_ref[kind, head * 256 : (head + 1) * 256, :])
    over2().start()
    gain_next(2)

    def flash(p, kind, masked):
        rows = rows_at(p, 512)
        keys, values = kv_ref[rows, :HD], kv_ref[rows, HD:]
        bent = jnp.tanh(mm(queries_ref[kind], keys, NT) * (HD ** (-0.5) / SOFT_CAP))
        soft = jnp.exp(SOFT_CAP * bent) * norm_ref[kind]
        if masked:
            soft = jnp.where(kpos_ref[p] <= qpos_ref[kind], soft, 0.0)
        dots = mm(dob[kind], values, NT)
        score = (soft * (dots - delta[kind]) * (1.0 - bent * bent) * HD ** (-0.5)).astype(bf)
        dq[kind] += mm(score, keys, NN)
        return mm(score, queries_ref[kind], TN), mm(soft.astype(bf), dob[kind], TN)

    def half(p, core_index):
        return rows_at(2 * p + core_index, 256)

    def kv_over(p):
        return remote(
            kvg.at[half(p, 1 - c)], kvd.at[rows_at(p, 256)], kd_s.at[p], kd_r.at[p], core
        )

    def kv_add(p):
        kv_over(p).wait_recv()
        rows = half(p, c)
        kvg[rows, :] = (
            kvg[rows, :].astype(f32) + kvd[rows_at(p, 256), :].astype(f32)
        ).astype(bf)

    kv_onward, kv_settle, kv_drain = chain_copies(
        lambda p: kvg.at[half(p, c)],
        lambda into: kvz.at[rows_at(into, 256)],
        p0,
        P,
        right,
        left,
        has_right,
        has_left,
        kz_s,
        kz_r,
    )
    dk, dv = flash(P, 1, True)
    kvg[rows_at(P, 512), :HD] = dk.astype(bf)
    kvg[rows_at(P, 512), HD:] = dv.astype(bf)
    kv_over(P).start()
    add2()

    def tile(j, carry):
        p = order(P - 1 - j)
        dk, dv = flash(p, 0, True)
        more_dk, more_dv = flash(p, 1, False)
        kvg[rows_at(p, 512), :HD] = (dk + more_dk).astype(bf)
        kvg[rows_at(p, 512), HD:] = (dv + more_dv).astype(bf)
        kv_over(p).start()

        @pl.when(j < P - 1)
        def _():
            onward2(p)

        return carry

    lax.fori_loop(0, P, tile, 0)
    gain_next(3)
    for kind in range(2):
        rows = slice(kind * 256, (kind + 1) * 256)
        for head in range(2):
            cols = slice(head * 256, (head + 1) * 256)
            dqkv[2 + head, rows, :] = turn(
                dq[kind, cols, :], cos_ref[rows, :], sin_ref[rows, :], True
            ).astype(bf)
    for head in range(2):
        weight(2 + head, feats, lambda kind: dqkv[2 + head, kind * 256 : (kind + 1) * 256, :])
    over1().start()

    def kv_step(j, carry):
        p = order(P - 1 - j)
        kv_add(p)
        kv_onward(p)
        return carry

    lax.fori_loop(0, P - 1, kv_step, 0)
    settle2()
    spread(2)
    add1()

    def q_step(j, carry):
        onward1(order(P - 1 - j))
        return carry

    lax.fori_loop(0, P - 1, q_step, 0)
    kv_add(P)
    kv_add(p0)
    kv_settle()
    for kind in range(2):
        rows = slice(kind * 256, (kind + 1) * 256)
        block = half(p0 if kind == 0 else P, c)
        dqkv[0, rows, :] = turn(
            kvg[block, :HD].astype(f32), cos_ref[rows, :], sin_ref[rows, :], True
        ).astype(bf)
        dqkv[1, rows, :] = kvg[block, HD:]
    for one in range(2):
        weight(one, feats, lambda kind: dqkv[one, kind * 256 : (kind + 1) * 256, :])
    over0().start()

    wide = width // 2
    cols, first, second, last, drain_sum = plane_sum(
        part, wide, hd, xmate, ymate, yhalf, xhalf, yfull, xfull, rs_s, rs_r
    )

    def project(h):
        for kind in range(2):
            source = slice(kind * 256, (kind + 1) * 256)
            for at, size in spans(wide, 384):
                rows = slice(h * wide + at, h * wide + at + size)
                summed = mm(dqkv[0, source, :], w6[0, rows, :], NT)
                for one in range(1, 4):
                    summed = summed + mm(dqkv[one, source, :], w6[one, rows, :], NT)
                part[kind, :, rows] = summed.astype(bf)
        first(h)

    add0()

    def last_step(j, carry):
        onward0(order(P - 1 - j))
        return carry

    project(0)
    lax.fori_loop(0, 1, last_step, 0)
    project(1)
    settle1()
    spread(1)
    second(0)
    lax.fori_loop(1, P - 1, last_step, 0)
    second(1)
    for number in range(4, len(levels)):
        gain_next(number)
    for h in range(2):
        dn1[:, :, h * wide : (h + 1) * wide] = last(h) * gain_ref[0:1, h * wide : (h + 1) * wide]
    settle0()
    spread(0)
    for kind in range(2):
        unit, inverse = unit_rows(x_ref[kind].astype(f32))
        grads = dn1[kind]
        gin_ref[kind] = (
            dh_ref[kind]
            + inverse * (grads - unit * jnp.mean(grads * unit, axis=-1, keepdims=True))
        ).astype(bf)
    for j in range(3):
        for d in range(7):
            a2a_copy(j, d).wait()
    for h in range(2):
        drain_sum(h)
    for one in (own_x, own_y, on_y, on_x):
        one.wait_send()
    for finish in (finish0, finish1, finish2):
        finish()
    for p in range(P):
        kv_drain(p)
        kv_over(p).wait_send()
    kv_over(P).wait_send()
    for which in range(2):
        ffn_copy(which).wait()


def retrace_call(
    mesh_shape, shard, da, dh, x, gain, gsum, cosine, sine, qpos, kpos, saved, partial
):
    w6, feats, queries, kv, low, mix, norm = saved
    fs = mesh_shape["fsdp"]
    planes = mesh_shape["ctx"] * fs // 8
    width = da.shape[2]
    bf, f32 = jnp.bfloat16, jnp.float32
    vmem = pl.BlockSpec(memory_space=pltpu.VMEM)
    hbm = pl.BlockSpec(memory_space=pl.ANY)
    dma = pltpu.SemaphoreType.DMA
    shape = jax.ShapeDtypeStruct
    deep = 8 * shard
    padded = shard + -shard % 16
    levels = len(summing_levels(planes))
    return pl.pallas_call(
        functools.partial(retrace_kernel, planes, fs, shard),
        out_shape=(
            shape((2, 64, width), bf),
            shape((8, 3, padded, HD), bf),
            shape((8, width), f32),
            shape(partial.shape, bf),
        ),
        in_specs=[vmem] * 10 + [hbm] * 7,
        out_specs=(vmem, vmem, vmem, hbm),
        scratch_shapes=[
            pltpu.VMEM((6, width, HD), bf),
            pltpu.VMEM((2, 256, width), bf),
            pltpu.VMEM((2, 512, HD), bf),
            pltpu.VMEM(((2 * planes + 2) * 256, 2 * HD), bf),
            pltpu.VMEM((2, 512, HD), bf),
            pltpu.VMEM((2, 512, HD), f32),
            pltpu.VMEM((2, 256, width), bf),
            pltpu.VMEM((2, 512, HD), bf),
            pltpu.VMEM((2, 512, 1), f32),
            pltpu.VMEM((2, 512, HD), f32),
            pltpu.VMEM((4, 512, HD), bf),
            pltpu.VMEM(((2 * planes + 2) * 256, 2 * HD), bf),
            pltpu.VMEM(((planes + 1) * 256, 2 * HD), bf),
            pltpu.VMEM(((planes + 1) * 256, 2 * HD), bf),
            pltpu.VMEM((6, width, HD), bf),
            pltpu.VMEM((3, width, HD), bf),
            pltpu.VMEM((3, (planes + 1) * deep, HD), bf),
            pltpu.VMEM((deep, HD), f32),
            pltpu.VMEM((8, 3, padded, HD), bf),
            pltpu.VMEM((2, 64, width), f32),
            pltpu.VMEM((2, 256, width), bf),
            *plane_scratch(width),
            pltpu.VMEM((levels, 8, width), f32),
            dma((6,)),
            dma((3, 7)),
            dma((3, 7)),
            dma((4,)),
            dma((4,)),
            dma((3, planes)),
            dma((3, planes + 1)),
            dma((3,)),
            dma((3,)),
            dma((planes,)),
            dma((planes + 1,)),
            dma((planes + 1,)),
            dma((planes + 1,)),
            dma((levels,)),
            dma((levels,)),
            dma((2,)),
            dma((2,)),
        ],
        compiler_params=pltpu.CompilerParams(
            collective_id=3, has_side_effects=True, vmem_limit_bytes=60 * 2**20
        ),
        name="retrace",
    )(
        da,
        dh,
        x,
        gain,
        gsum,
        cosine,
        sine,
        qpos,
        kpos,
        norm,
        w6,
        feats,
        queries,
        kv,
        low,
        mix,
        partial,
    )


def ffn_kernel(
    planes,
    fs,
    branch_ref,
    x_ref,
    dy_ref,
    gain_ref,
    own_ref,
    across_ref,
    out_ref,
    dh_ref,
    da_ref,
    gsum_ref,
    dwown_ref,
    dwside_ref,
    dwdown_ref,
    w,
    hidden_in,
    ffn,
    n2all,
    dfall,
    gate,
    up,
    act,
    part,
    yrecv,
    zrecv,
    zhalf,
    stage,
    load,
    push_s,
    push_r,
    ag_ys,
    ag_yr,
    ag_zs,
    ag_zr,
    rs_ys,
    rs_yr,
    rs_zs,
    rs_zr,
    ag_bs,
    ag_br,
    rs_bs,
    rs_br,
    dw_s,
    dw_r,
    down_s,
    down_r,
    store,
    ready,
):
    P = planes
    rows, width = x_ref.shape
    slot = own_ref.shape[1]
    hidden = 4 * slot
    bf, f32 = jnp.bfloat16, jnp.float32
    me = place(fs)
    y0 = (me // 4) % 2
    p0, right, left, has_right, has_left = neighbours(me, P, fs)
    order = line_order(p0, P)
    core = device(flip(me, 1), fs)
    xmate = device(flip(me, 2), fs)
    partner = device(flip(me, 4), fs)

    def block(p, y):
        return rows_at(p * 2 + y, rows)

    def pair(p):
        return rows_at(p, 2 * rows)

    def at(p):
        return rows_at(p, rows)

    def some_rows(body):
        def step(number, carry):
            body(rows_at(number, 32))
            return carry

        lax.fori_loop(0, rows // 32, step, 0)

    own_rows = (p0 * 2 + y0) * rows

    def inside(chunk):
        return pl.ds(pl.multiple_of(own_rows + chunk.start, 32), 32)

    local = [
        pltpu.make_async_copy(own_ref.at[which], w.at[which, pl.ds(0, slot)], load.at[which])
        for which in range(3)
    ] + [
        pltpu.make_async_copy(
            across_ref.at[which], w.at[which, pl.ds(slot, slot)], load.at[3 + which]
        )
        for which in range(2)
    ]
    for copy in local:
        copy.start()
    greet([core, xmate, partner], right, left, has_right, has_left)
    pushes = [
        remote(
            own_ref.at[which],
            w.at[which, pl.ds(2 * slot, slot)],
            push_s.at[which],
            push_r.at[which],
            core,
        )
        for which in range(3)
    ] + [
        remote(
            across_ref.at[which],
            w.at[which, pl.ds(3 * slot, slot)],
            push_s.at[3 + which],
            push_r.at[3 + which],
            core,
        )
        for which in range(2)
    ]
    down_across = remote(
        own_ref.at[2], w.at[2, pl.ds(slot, slot)], push_s.at[5], push_r.at[5], xmate
    )
    down_over = remote(
        w.at[2, pl.ds(slot, slot)],
        w.at[2, pl.ds(3 * slot, slot)],
        push_s.at[6],
        push_r.at[6],
        core,
    )
    down_across.start()

    def enter(chunk):
        unit, _ = unit_rows(branch_ref[chunk, :])
        values = x_ref[chunk, :].astype(f32) + unit * gain_ref[1:2, :]
        hidden_in[chunk, :] = values
        unit, _ = unit_rows(values)
        n2all[inside(chunk), :] = (unit * gain_ref[2:3, :]).astype(bf)

    some_rows(enter)

    half = rows // 2
    ends = (0, P - 1)

    def is_end(p):
        return (p == 0) | (p == P - 1)

    def upper(p, y):
        return pl.ds(pl.multiple_of((p * 2 + y) * rows, half), half)

    def lower(p, y):
        return pl.ds(pl.multiple_of((p * 2 + y) * rows + half, half), half)

    def gather(buf, turn, compute):
        def y_copy(p, y):
            view = buf.at[block(p, y)]
            return remote(view, view, ag_ys.at[turn, p], ag_yr.at[turn, p], partner)

        def y_half(p, y):
            view = buf.at[upper(p, y)]
            return remote(view, view, ag_ys.at[turn, p], ag_yr.at[turn, p], partner)

        def side_copy(number):
            view = buf.at[lower(ends[number], 1 - y0)]
            return remote(
                view,
                view,
                ag_bs.at[turn, number],
                ag_br.at[turn, number],
                (right, left)[number],
            )

        passes = (has_right, has_left)
        send, arrived, drain_z = line_copies(
            lambda p: buf.at[block(p, y0)],
            p0,
            right,
            left,
            has_right,
            has_left,
            ag_zs.at[turn],
            ag_zr.at[turn],
        )
        send(p0)
        y_copy(p0, y0).start()
        if turn == 0:
            for copy in pushes:
                copy.start()

        def inside_line(p):
            return (p >= 0) & (p < P)

        def step(s, carry):
            for p in (p0 - s, p0 + s):

                @pl.when(inside_line(p))
                def _():
                    arrived(p)
                    send(p)

                @pl.when(inside_line(p) & is_end(p))
                def _():
                    y_half(p, y0).start()

                @pl.when(inside_line(p) & ~is_end(p))
                def _():
                    y_copy(p, y0).start()

            for number in range(2):

                @pl.when((s > 1) & ((ends[number] - p0 == s - 1) | (p0 - ends[number] == s - 1)))
                def _():
                    side_copy(number).wait_recv()

                    @pl.when(passes[number])
                    def _():
                        side_copy(number).start()

            @pl.when(s == 1)
            def _():
                y_copy(p0, 1 - y0).wait_recv()

                for number in range(2):

                    @pl.when(p0 == ends[number])
                    def _():
                        side_copy(number).start()

            compute.before(s)

            def one(way, carry):
                q = p0 + (2 * way - 1) * (s - 1)

                @pl.when(inside_line(q) & ((s > 1) | (way == 0)))
                def _():
                    @pl.when((s > 1) & is_end(q))
                    def _():
                        y_half(q, 1 - y0).wait_recv()

                    @pl.when((s > 1) & ~is_end(q))
                    def _():
                        y_copy(q, 1 - y0).wait_recv()

                    compute.pair(q, s)

                return carry

            lax.fori_loop(0, 2, one, 0)
            compute.after(s)
            return carry

        lax.fori_loop(1, P + 1, step, 0)

        def drain(p, carry):
            @pl.when(is_end(p) & (p != p0))
            def _():
                y_half(p, y0).wait_send()

            @pl.when(~is_end(p) | (p == p0))
            def _():
                y_copy(p, y0).wait_send()

            drain_z(p)
            return carry

        lax.fori_loop(0, P, drain, 0)
        for number in range(2):

            @pl.when(passes[number])
            def _():
                side_copy(number).wait_send()

    def scatter(turn, beside):
        def y_copy(p):
            return remote(
                part.at[block(p, 1 - y0)],
                yrecv.at[at(p)],
                rs_ys.at[turn, p],
                rs_yr.at[turn, p],
                partner,
            )

        def y_half(p):
            return remote(
                part.at[upper(p, 1 - y0)],
                yrecv.at[pl.ds(pl.multiple_of(p * rows, half), half)],
                rs_ys.at[turn, p],
                rs_yr.at[turn, p],
                partner,
            )

        onward, settle, drain_z = chain_copies(
            lambda p: part.at[block(p, y0)],
            lambda into: zrecv.at[at(into)],
            p0,
            P,
            right,
            left,
            has_right,
            has_left,
            rs_zs.at[turn],
            rs_zr.at[turn],
        )

        def side_copy(number):
            return remote(
                part.at[lower(ends[number], 1 - y0)],
                zhalf.at[number],
                rs_bs.at[turn, number],
                rs_br.at[turn, number],
                (left, right)[number],
            )

        before = (has_right, has_left)

        def side_add(number):
            side_copy(number).wait_recv()
            mine = lower(ends[number], 1 - y0)
            part[mine, :] = (part[mine, :].astype(f32) + zhalf[number].astype(f32)).astype(bf)

        def side_turn(number):
            @pl.when((p0 != ends[number]) & before[number])
            def _():
                side_add(number)

            @pl.when(p0 != ends[number])
            def _():
                side_copy(number).start()

        def y_add(p, carry=None):
            @pl.when(is_end(p) & (p != p0))
            def _():
                y_half(p).wait_recv()
                mine = upper(p, y0)
                part[mine, :] = (
                    part[mine, :].astype(f32)
                    + yrecv[pl.ds(pl.multiple_of(p * rows, half), half), :].astype(f32)
                ).astype(bf)

            @pl.when(~is_end(p) | (p == p0))
            def _():
                y_copy(p).wait_recv()
                mine = block(p, y0)
                part[mine, :] = (part[mine, :].astype(f32) + yrecv[at(p), :].astype(f32)).astype(bf)

        for number in range(2):

            @pl.when((p0 != ends[number]) & ~before[number])
            def _():
                side_copy(number).start()

        def start_y(j, carry):
            p = order(P - 1 - j)

            @pl.when(is_end(p))
            def _():
                y_half(p).start()

            @pl.when(~is_end(p))
            def _():
                y_copy(p).start()

            return carry

        lax.fori_loop(0, P - 1, start_y, 0)

        @pl.when(~is_end(p0))
        def _():
            y_copy(p0).start()

        if beside is not None:
            beside(0)

        @pl.when(p0 < P // 2)
        def _():
            for number in (1, 0):

                @pl.when((p0 != ends[number]) & before[number])
                def _():
                    side_turn(number)

        @pl.when(p0 >= P // 2)
        def _():
            for number in (0, 1):

                @pl.when((p0 != ends[number]) & before[number])
                def _():
                    side_turn(number)

        for j in range(P - 1):
            if beside is not None and j:
                beside(j)
            p = order(P - 1 - j)
            y_add(p)
            onward(p)
            if j == 1:
                for number in range(2):

                    @pl.when(p0 == ends[number])
                    def _():
                        side_add(number)
                        y_copy(p0).start()

        if beside is not None:
            beside(P - 1)
        y_add(p0)
        settle()
        ffn[...] = part[block(p0, y0), :].astype(f32)

        def drain(p, carry):
            @pl.when(is_end(p) & (p != p0))
            def _():
                y_half(p).wait_send()

            @pl.when(~is_end(p) | (p == p0))
            def _():
                y_copy(p).wait_send()

            drain_z(p)
            return carry

        lax.fori_loop(0, P, drain, 0)
        for number in range(2):

            @pl.when(p0 != ends[number])
            def _():
                side_copy(number).wait_send()

    def forward_down(p):
        for first, wide in spans(width, 768):
            cols = slice(first, first + wide)
            part[pair(p), cols] = mm(act[pair(p), :], w[2, :, cols], NN).astype(bf)

    class Forward:
        def before(s):
            @pl.when(s == 1)
            def _():
                for which in (0, 1, 3, 4):
                    local[which].wait()
                    pushes[which].wait_recv()

            @pl.when(s == 3)
            def _():
                local[2].wait()
                pushes[2].wait_recv()
                down_over.wait_recv()

                def early(q, carry):
                    @pl.when((q - p0 < 2) & (p0 - q < 2))
                    def _():
                        forward_down(q)

                    return carry

                lax.fori_loop(0, P, early, 0)

        def pair(p, s):
            feats = n2all[pair(p), :]
            for first, wide in spans(hidden, 256):
                cols = slice(first, first + wide)
                gates = mm(feats, w[0, cols, :], NT)
                ups = mm(feats, w[1, cols, :], NT)
                bent = jnp.tanh(GELU_A * (gates + GELU_B * gates * gates * gates))
                gate[pair(p), cols] = gates.astype(bf)
                up[pair(p), cols] = ups.astype(bf)
                act[pair(p), cols] = (0.5 * gates * (1.0 + bent) * ups).astype(bf)

            @pl.when(s >= 3)
            def _():
                forward_down(p)

        def after(s):
            @pl.when(s == 2)
            def _():
                down_across.wait_recv()
                down_over.start()

    gather(n2all, 0, Forward)
    scatter(0, None)
    gsum_ref[...] = jnp.zeros_like(gsum_ref)

    def leave(chunk):
        unit, inverse = unit_rows(ffn[chunk, :])
        out_ref[chunk, :] = (hidden_in[chunk, :] + unit * gain_ref[3:4, :]).astype(bf)
        upstream = dy_ref[chunk, :].astype(f32)
        gsum_ref[3:4, :] += jnp.sum(upstream * unit, axis=0, keepdims=True)
        pulled = upstream * gain_ref[3:4, :]
        dfall[inside(chunk), :] = (
            inverse * (pulled - unit * jnp.mean(pulled * unit, axis=-1, keepdims=True))
        ).astype(bf)

    some_rows(leave)

    class Backward:
        def before(s):
            return None

        def after(s):
            return None

        def pair(p, s):
            backward(p)

    def backward(p):
        grads = dfall[pair(p), :]
        for first, wide in spans(hidden, 256):
            cols = slice(first, first + wide)
            dact = mm(grads, w[2, cols, :], NT)
            gates = gate[pair(p), cols].astype(f32)
            ups = up[pair(p), cols].astype(f32)
            square = gates * gates
            bent = jnp.tanh(GELU_A * (gates + GELU_B * gates * square))
            half = 0.5 * (1.0 + bent)
            slope = half + 0.5 * gates * (1.0 - bent * bent) * (
                GELU_A * (1.0 + 3.0 * GELU_B * square)
            )
            gate[pair(p), cols] = (dact * ups * slope).astype(bf)
            up[pair(p), cols] = (dact * gates * half).astype(bf)
        for first, wide in spans(width, 768):
            cols = slice(first, first + wide)
            part[pair(p), cols] = (
                mm(gate[pair(p), :], w[0, :, cols], NN) + mm(up[pair(p), :], w[1, :, cols], NN)
            ).astype(bf)

    gather(dfall, 1, Backward)
    for copy in pushes:
        copy.wait_send()
    down_across.wait_send()
    down_over.wait_send()
    pl.semaphore_signal(ready, inc=1, device_id=core, device_id_type=MESH)
    pl.semaphore_wait(ready, 1)
    chunks = spans(width, 768)
    tasks = [(which, number) for which in (2, 0, 1) for number in range(len(chunks))]

    def dw_push(task):
        which, number = tasks[task]
        cols = pl.ds(*chunks[number])
        return remote(
            w.at[which, pl.ds(2 * slot, 2 * slot), cols],
            w.at[which, pl.ds(0, 2 * slot), cols],
            dw_s.at[task],
            dw_r.at[task],
            core,
        )

    def dw_out(which):
        return pltpu.make_async_copy(w.at[which, pl.ds(0, slot)], dwown_ref.at[which], store.at[which])

    def dw_side(which):
        return pltpu.make_async_copy(
            w.at[which, pl.ds(slot, slot)], dwside_ref.at[which], store.at[3 + which]
        )

    dw_down = remote(w.at[2, pl.ds(slot, slot)], dwdown_ref, down_s, down_r, xmate)

    def dw_finish(task):
        which, number = tasks[task]
        first, wide = chunks[number]
        cols = slice(first, first + wide)
        dw_push(task).wait_recv()
        w[which, : 2 * slot, cols] = (
            stage[task % 2].astype(f32) + w[which, : 2 * slot, cols].astype(f32)
        ).astype(bf)
        if number == len(chunks) - 1:
            dw_out(which).start()
            if which == 2:
                dw_down.start()
            else:
                dw_side(which).start()

    def weight_grad(task):
        which, number = tasks[task]
        first, wide = chunks[number]
        left_side = (gate, up, act)[which]
        right_side = (n2all, n2all, dfall)[which]
        summed = mm(left_side[...], right_side[:, first : first + wide], TN)
        w[which, 2 * slot :, first : first + wide] = summed[2 * slot :].astype(bf)
        stage[task % 2] = summed[: 2 * slot].astype(bf)
        dw_push(task).start()
        if task:
            dw_finish(task - 1)

    shares = [range(0, 4), range(4, 6), range(6, 8), range(8, 9)]

    def beside(j):
        if j < len(shares):
            for task in shares[j]:
                weight_grad(task)

    scatter(1, beside)

    def back(chunk):
        unit, inverse = unit_rows(hidden_in[chunk, :])
        grads = ffn[chunk, :]
        gsum_ref[2:3, :] += jnp.sum(grads * unit, axis=0, keepdims=True)
        pulled = grads * gain_ref[2:3, :]
        dres = dy_ref[chunk, :].astype(f32) + inverse * (
            pulled - unit * jnp.mean(pulled * unit, axis=-1, keepdims=True)
        )
        dh_ref[chunk, :] = dres
        unit, inverse = unit_rows(branch_ref[chunk, :])
        gsum_ref[1:2, :] += jnp.sum(dres * unit, axis=0, keepdims=True)
        pulled = dres * gain_ref[1:2, :]
        da_ref[chunk, :] = (
            inverse * (pulled - unit * jnp.mean(pulled * unit, axis=-1, keepdims=True))
        ).astype(bf)

    some_rows(back)
    dw_finish(len(tasks) - 1)
    for task in range(len(tasks)):
        dw_push(task).wait_send()
    for which in range(3):
        dw_out(which).wait()
    for which in range(2):
        dw_side(which).wait()
    dw_down.wait()


def ffn_call(mesh_shape, branch, x, dy, gain, own, across):
    fs = mesh_shape["fsdp"]
    planes = mesh_shape["ctx"] * fs // 8
    rows, width = x.shape
    slot = own.shape[1]
    hidden = 4 * slot
    tokens = planes * 2 * rows
    bf, f32 = jnp.bfloat16, jnp.float32
    vmem = pl.BlockSpec(memory_space=pltpu.VMEM)
    hbm = pl.BlockSpec(memory_space=pl.ANY)
    dma = pltpu.SemaphoreType.DMA
    shape = jax.ShapeDtypeStruct
    return pl.pallas_call(
        functools.partial(ffn_kernel, planes, fs),
        out_shape=(
            shape((rows, width), bf),
            shape((rows, width), f32),
            shape((rows, width), bf),
            shape((8, width), f32),
            shape((3, slot, width), bf),
            shape((2, slot, width), bf),
            shape((slot, width), bf),
        ),
        in_specs=[vmem, vmem, vmem, vmem, hbm, hbm],
        out_specs=(vmem, vmem, vmem, vmem, hbm, hbm, hbm),
        scratch_shapes=[
            pltpu.VMEM((3, hidden, width), bf),
            pltpu.VMEM((rows, width), f32),
            pltpu.VMEM((rows, width), f32),
            pltpu.VMEM((tokens, width), bf),
            pltpu.VMEM((tokens, width), bf),
            pltpu.VMEM((tokens, hidden), bf),
            pltpu.VMEM((tokens, hidden), bf),
            pltpu.VMEM((tokens, hidden), bf),
            pltpu.VMEM((tokens, width), bf),
            pltpu.VMEM((planes * rows, width), bf),
            pltpu.VMEM(((planes + 1) * rows, width), bf),
            pltpu.VMEM((2, rows // 2, width), bf),
            pltpu.VMEM((2, 2 * slot, 768), bf),
            dma((5,)),
            dma((7,)),
            dma((7,)),
            dma((2, planes)),
            dma((2, planes)),
            dma((2, 2, planes)),
            dma((2, planes)),
            dma((2, planes)),
            dma((2, planes)),
            dma((2, planes)),
            dma((2, planes + 1)),
            dma((2, 2)),
            dma((2, 2)),
            dma((2, 2)),
            dma((2, 2)),
            dma((9,)),
            dma((9,)),
            dma,
            dma,
            dma((5,)),
            pltpu.SemaphoreType.REGULAR,
        ],
        compiler_params=pltpu.CompilerParams(
            collective_id=1, has_side_effects=True, vmem_limit_bytes=62 * 2**20
        ),
        name="ffn",
    )(branch, x, dy, gain, own, across)


CONTRACT_ROWS = (((0,), (0,)), ((), ()))
CONTRACT_COLS = (((1,), (1,)), ((), ()))


def from_partner(array, axis, apart):
    return lax.ppermute(array, axis, [(i, i ^ 1 << apart) for i in range(lax.axis_size(axis))])


def normalize(values):
    inverse = lax.rsqrt(jnp.mean(values * values, axis=-1, keepdims=True) + NORM_EPS)
    return (values * inverse, inverse)


def norm_back(unit_values, inverse, grad_unit):
    return inverse * (
        grad_unit - unit_values * jnp.mean(grad_unit * unit_values, axis=-1, keepdims=True)
    )


def row_meta(blocks, prompt):
    offsets = jnp.arange(BLK, dtype=jnp.int32)
    natural = (blocks[:, None] * BLK + offsets[None, :]).reshape(-1)
    group_span = 2 * prompt
    inner_index = natural % group_span
    group_id = natural // group_span
    in_continuation = inner_index >= prompt
    segment = jnp.where(in_continuation, 1 + (inner_index - prompt) // CONT_LEN, 0)
    position = jnp.where(in_continuation, prompt + (inner_index - prompt) % CONT_LEN, inner_index)
    stride = prompt // CONT_LEN + 1
    return (position, group_id * stride + segment, group_id * stride)


def rope_tables(position):
    frequency = 10000.0 ** (-(jnp.arange(HD // 2, dtype=jnp.float32) * 2.0 / HD))
    angles = position.astype(jnp.float32)[:, None] * frequency[None, :]
    return (jnp.cos(angles), jnp.sin(angles))


def rotate(values, cosine, sine_table):
    half_width = values.shape[-1] // 2
    first_half, second_half = (values[..., :half_width], values[..., half_width:])
    cosine, sine_table = (cosine[:, None, :], sine_table[:, None, :])
    return jnp.concatenate(
        [
            first_half * cosine - second_half * sine_table,
            second_half * cosine + first_half * sine_table,
        ],
        axis=-1,
    )


def unrotate(grads, cosine, sine_table):
    half_width = grads.shape[-1] // 2
    first_half, second_half = (grads[..., :half_width], grads[..., half_width:])
    cosine, sine_table = (cosine[:, None, :], sine_table[:, None, :])
    return jnp.concatenate(
        [
            first_half * cosine + second_half * sine_table,
            second_half * cosine - first_half * sine_table,
        ],
        axis=-1,
    )


def placing(block_table, me, devices, prompt):
    planes = devices // 8
    position = row_meta(block_table, prompt)[0].reshape(planes, 4, 2, 2, 64)
    by_core = position.transpose(0, 2, 3, 1, 4).reshape(planes, 2, 2, 256)
    here = lax.dynamic_index_in_dim(by_core, me // 8, 0, keepdims=False)
    own = lax.dynamic_index_in_dim(here, me % 2, 0, keepdims=False)
    cosine, sine = rope_tables(own.reshape(-1))
    qpos = jnp.tile(own[:, None, :], (1, 2, 1)).reshape(2, 512, 1)
    kpos = jnp.concatenate([by_core[:, :, 0].reshape(planes, 512), here[:, 1].reshape(1, 512)])
    return cosine, sine, qpos, kpos.reshape(planes + 1, 1, 512)


def pack_weights(w_query, w_key, w_value, w_output):
    shard = w_query.shape[0]
    heads, kv = w_query.shape[1] // HD, w_key.shape[1] // HD
    pair = jnp.stack([w_key.reshape(shard, kv, HD), w_value.reshape(shard, kv, HD)], axis=2)
    packed = jnp.stack(
        [
            pair.reshape(shard, heads, HD),
            w_query.reshape(shard, heads, HD),
            w_output.T.reshape(shard, heads, HD),
        ]
    ).astype(jnp.bfloat16)
    packed = packed.transpose(2, 0, 1, 3)
    return jnp.pad(packed, ((0, 0), (0, 0), (0, -shard % 16), (0, 0)))


def pack_gains(gains, me, width):
    own = jnp.stack(gains).astype(jnp.bfloat16).astype(jnp.float32)
    wide = jnp.zeros((8, width), jnp.float32)
    return lax.dynamic_update_slice(wide, own, (0, me * own.shape[1]))


def visible(query_pos, query_doc, query_base, key_pos, key_doc):
    earlier = key_pos[None, :] <= query_pos[:, None]
    shared = (key_doc[None, :] == query_doc[:, None]) | (key_doc[None, :] == query_base[:, None])
    return earlier & shared


def gated(gate_values, up_values):
    return jax.nn.gelu(gate_values, approximate=True) * up_values


def ffn_gathered(hidden_res, normed_h, upstream, gain_four, w_gate, w_up, w_down):
    bfloat = jnp.bfloat16
    pair_weights = jnp.stack([w_gate, w_up]).astype(bfloat)
    down_local = w_down.astype(bfloat)
    gate_up = jnp.einsum(
        "rd,sdf->rsf",
        lax.all_gather(normed_h, ("ctx", "fsdp"), axis=0, tiled=True),
        pair_weights,
        preferred_element_type=jnp.float32,
    )
    activated = gated(gate_up[:, 0], gate_up[:, 1]).astype(bfloat)
    part_rows = activated
    ffn_raw = lax.psum_scatter(
        jnp.dot(part_rows, down_local, preferred_element_type=jnp.float32).astype(bfloat),
        ("ctx", "fsdp"),
        scatter_dimension=0,
        tiled=True,
    ).astype(jnp.float32)
    unit_f, inv_f = normalize(ffn_raw)
    layer_out = (hidden_res + unit_f * gain_four).astype(bfloat)
    grad_four = jnp.sum(upstream * unit_f, axis=0)
    grad_ffn = norm_back(unit_f, inv_f, upstream * gain_four).astype(bfloat)
    grad_piece = lax.all_gather(grad_ffn, ("ctx", "fsdp"), axis=0, tiled=True)
    normed_piece = lax.all_gather(normed_h, ("ctx", "fsdp"), axis=0, tiled=True)
    act_grad = lax.dot_general(
        grad_piece, down_local, CONTRACT_COLS, preferred_element_type=jnp.float32
    )
    pull_piece = jax.vjp(gated, gate_up[:, 0], gate_up[:, 1])[1]
    gate_grad, up_grad = pull_piece(act_grad)
    pair_low = jnp.stack([gate_grad, up_grad], axis=1).astype(bfloat)
    down_sum = lax.dot_general(
        activated, grad_piece, CONTRACT_ROWS, preferred_element_type=jnp.float32
    )
    pair_sum = jnp.einsum("nd,nsf->sdf", normed_piece, pair_low, preferred_element_type=jnp.float32)
    grad_gate = pair_sum[0]
    grad_up = pair_sum[1]
    part_rows = pair_low
    grad_normed_h = lax.psum_scatter(
        jnp.einsum("nsf,sdf->nd", part_rows, pair_weights, preferred_element_type=jnp.float32).astype(bfloat),
        ("ctx", "fsdp"),
        scatter_dimension=0,
        tiled=True,
    ).astype(jnp.float32)
    return (layer_out, grad_normed_h, grad_four, grad_gate, grad_up, down_sum)


def on_device(
    tokens_in,
    block_table,
    w_query,
    w_key,
    w_value,
    w_output,
    w_gate,
    w_up,
    w_down,
    gain_attn_in,
    gain_attn_out,
    gain_ffn_in,
    gain_ffn_out,
    cotangent,
):
    row_count, model_width = tokens_in.shape
    devices = lax.axis_size(("ctx", "fsdp"))
    slot_count = block_table.shape[0] // devices
    prompt = 2 * devices * BLK
    all_rows = row_count * devices
    device_here = lax.axis_index(("ctx", "fsdp"))
    head_count = w_query.shape[1] // HD
    kv_count = w_key.shape[1] // HD
    groups = head_count // kv_count
    score_scale = HD ** (-0.5)
    bfloat = jnp.bfloat16
    gathered = (
        lax.all_gather(w_query.astype(bfloat), ("ctx", "fsdp"), axis=0, tiled=True),
        lax.all_gather(w_key.astype(bfloat), ("ctx", "fsdp"), axis=0, tiled=True),
        lax.all_gather(w_value.astype(bfloat), ("ctx", "fsdp"), axis=0, tiled=True),
        lax.all_gather(w_output.astype(bfloat), ("ctx", "fsdp"), axis=1, tiled=True),
        lax.all_gather(gain_attn_in.astype(bfloat), ("ctx", "fsdp"), axis=0, tiled=True),
        lax.all_gather(gain_attn_out.astype(bfloat), ("ctx", "fsdp"), axis=0, tiled=True),
        lax.all_gather(gain_ffn_in.astype(bfloat), ("ctx", "fsdp"), axis=0, tiled=True),
        lax.all_gather(gain_ffn_out.astype(bfloat), ("ctx", "fsdp"), axis=0, tiled=True),
    )
    query_weight, key_weight, value_weight, output_weight = (
        gathered[0],
        gathered[1],
        gathered[2],
        gathered[3],
    )
    gain_one = gathered[4].astype(jnp.float32)
    gain_two = gathered[5].astype(jnp.float32)
    gain_three = gathered[6].astype(jnp.float32)
    gain_four = gathered[7].astype(jnp.float32)
    key_meta = row_meta(block_table, prompt)
    key_pos, key_doc = (key_meta[0], key_meta[1])
    my_blocks = lax.dynamic_slice_in_dim(block_table, device_here * slot_count, slot_count)
    query_pos, query_doc, query_base = row_meta(my_blocks, prompt)
    cosine, sine_table = rope_tables(query_pos)
    inputs = tokens_in.astype(jnp.float32)
    unit_x, inv_x = normalize(inputs)
    normed_x = (unit_x * gain_one).astype(bfloat)
    query_raw = jnp.dot(normed_x, query_weight, preferred_element_type=jnp.float32).reshape(
        row_count, head_count, HD
    )
    queries = (
        rotate(query_raw, cosine, sine_table)
        .astype(bfloat)
        .reshape(row_count, kv_count, groups, HD)
    )
    key_raw = jnp.dot(normed_x, key_weight, preferred_element_type=jnp.float32).reshape(
        row_count, kv_count, HD
    )
    keys = rotate(key_raw, cosine, sine_table).astype(bfloat)
    values = (
        jnp.dot(normed_x, value_weight, preferred_element_type=jnp.float32)
        .reshape(row_count, kv_count, HD)
        .astype(bfloat)
    )

    def key_block_meta(first_row, block_width):
        block_pos = lax.dynamic_slice_in_dim(key_pos, first_row, block_width)
        block_doc = lax.dynamic_slice_in_dim(key_doc, first_row, block_width)
        return visible(query_pos, query_doc, query_base, block_pos, block_doc)[:, None, None, :]

    def bent_scores(key_block):
        scores = jnp.einsum(
            "rgjd,kgd->rgjk", queries, key_block, preferred_element_type=jnp.float32
        )
        return jnp.tanh(scores * (score_scale / SOFT_CAP))

    start_state = (
        jnp.full((row_count, kv_count, groups), MASKED, jnp.float32),
        jnp.zeros((row_count, kv_count, groups), jnp.float32),
        jnp.zeros((row_count, kv_count, groups, HD), jnp.float32),
    )
    key_piece = lax.all_gather(keys, ("ctx", "fsdp"), axis=0, tiled=True)
    value_piece = lax.all_gather(values, ("ctx", "fsdp"), axis=0, tiled=True)
    piece_rows = key_piece.shape[0]
    block_width = math.gcd(piece_rows, KBLK)

    def attend_block_step(block_index, state):
        running_max, running_sum, running_out = state
        offset = block_index * block_width
        key_block = lax.dynamic_slice_in_dim(key_piece, offset, block_width, 0)
        value_block = lax.dynamic_slice_in_dim(value_piece, offset, block_width, 0)
        allowed = key_block_meta(offset, block_width)
        capped = jnp.where(allowed, SOFT_CAP * bent_scores(key_block), MASKED)
        fresh_max = jnp.maximum(running_max, jnp.max(capped, axis=-1))
        decay = jnp.exp(running_max - fresh_max)
        weights_soft = jnp.where(allowed, jnp.exp(capped - fresh_max[..., None]), 0.0)
        running_sum = running_sum * decay + jnp.sum(weights_soft, axis=-1)
        running_out = running_out * decay[..., None] + jnp.einsum(
            "rgjk,kgd->rgjd",
            weights_soft.astype(bfloat),
            value_block,
            preferred_element_type=jnp.float32,
        )
        return (fresh_max, running_sum, running_out)

    running_max, running_sum, running_out = lax.fori_loop(
        0, piece_rows // block_width, attend_block_step, start_state
    )
    log_total = running_max + jnp.log(running_sum)
    attended = (running_out / running_sum[..., None]).reshape(row_count, head_count * HD)
    attended_low = attended.astype(bfloat)
    branch_raw = jnp.dot(attended_low, output_weight, preferred_element_type=jnp.float32)
    unit_a, inv_a = normalize(branch_raw)
    hidden_res = inputs + unit_a * gain_two
    unit_h, inv_h = normalize(hidden_res)
    normed_h = (unit_h * gain_three).astype(bfloat)
    upstream = cotangent.astype(jnp.float32)
    layer_out, grad_normed_h, grad_four, grad_gate, grad_up, down_sum = ffn_gathered(
        hidden_res, normed_h, upstream, gain_four, w_gate, w_up, w_down
    )
    grad_three = jnp.sum(grad_normed_h * unit_h, axis=0)
    grad_res = upstream + norm_back(unit_h, inv_h, grad_normed_h * gain_three)
    grad_two = jnp.sum(grad_res * unit_a, axis=0)
    grad_branch = norm_back(unit_a, inv_a, grad_res * gain_two).astype(bfloat)
    grad_att = lax.dot_general(
        grad_branch, output_weight, CONTRACT_COLS, preferred_element_type=jnp.float32
    ).astype(bfloat)
    grad_heads = grad_att.reshape(row_count, kv_count, groups, HD)
    row_delta = jnp.sum(
        grad_heads.astype(jnp.float32) * attended.reshape(row_count, kv_count, groups, HD), axis=-1
    )
    begin_state = (
        jnp.zeros((row_count, kv_count, groups, HD), jnp.float32),
        jnp.zeros((all_rows, kv_count, HD), jnp.float32),
        jnp.zeros((all_rows, kv_count, HD), jnp.float32),
    )
    retrace_key_piece = lax.all_gather(keys, ("ctx", "fsdp"), axis=0, tiled=True)
    retrace_value_piece = lax.all_gather(values, ("ctx", "fsdp"), axis=0, tiled=True)
    piece_rows = retrace_key_piece.shape[0]
    retrace_block_width = math.gcd(piece_rows, KBLK)

    def retrace_block_step(block_index, state):
        query_sum, key_sums, value_sums = state
        offset = block_index * retrace_block_width
        key_block = lax.dynamic_slice_in_dim(retrace_key_piece, offset, retrace_block_width, 0)
        value_block = lax.dynamic_slice_in_dim(retrace_value_piece, offset, retrace_block_width, 0)
        allowed = key_block_meta(offset, retrace_block_width)
        bent = bent_scores(key_block)
        weights_soft = jnp.where(allowed, jnp.exp(SOFT_CAP * bent - log_total[..., None]), 0.0)
        value_dots = jnp.einsum(
            "rgjd,kgd->rgjk", grad_heads, value_block, preferred_element_type=jnp.float32
        )
        score_grad = (
            weights_soft * (value_dots - row_delta[..., None]) * (1.0 - bent * bent) * score_scale
        ).astype(bfloat)
        query_sum = query_sum + jnp.einsum(
            "rgjk,kgd->rgjd", score_grad, key_block, preferred_element_type=jnp.float32
        )
        key_part = jnp.einsum(
            "rgjk,rgjd->kgd", score_grad, queries, preferred_element_type=jnp.float32
        )
        value_part = jnp.einsum(
            "rgjk,rgjd->kgd",
            weights_soft.astype(bfloat),
            grad_heads,
            preferred_element_type=jnp.float32,
        )
        key_sums = lax.dynamic_update_slice_in_dim(key_sums, key_part, offset, 0)
        value_sums = lax.dynamic_update_slice_in_dim(value_sums, value_part, offset, 0)
        return (query_sum, key_sums, value_sums)

    query_sum, key_sums, value_sums = lax.fori_loop(
        0, piece_rows // retrace_block_width, retrace_block_step, begin_state
    )
    mate_count = CONT_LEN // (2 * BLK)
    tail_shape = key_sums.shape[1:]
    key_slots = key_sums.reshape((devices, slot_count, BLK) + tail_shape)
    value_slots = value_sums.reshape((devices, slot_count, BLK) + tail_shape)
    prompt_rows = 2 * BLK * devices
    key_head, value_head = (
        lax.psum_scatter(
            key_slots[:, :2].reshape((prompt_rows,) + tail_shape),
            ("ctx", "fsdp"),
            scatter_dimension=0,
            tiled=True,
        ),
        lax.psum_scatter(
            value_slots[:, :2].reshape((prompt_rows,) + tail_shape),
            ("ctx", "fsdp"),
            scatter_dimension=0,
            tiled=True,
        ),
    )
    group_start = device_here // mate_count * mate_count
    later_both = jnp.stack(
        [
            lax.dynamic_slice_in_dim(key_slots[:, 2:], group_start, mate_count, 0),
            lax.dynamic_slice_in_dim(value_slots[:, 2:], group_start, mate_count, 0),
        ],
        axis=1,
    )
    rank_inner = device_here % mate_count
    for level in reversed(range(mate_count.bit_length() - 1)):
        half_count = later_both.shape[0] // 2
        upper_side = rank_inner >> level & 1 == 1
        lower_half = later_both[:half_count]
        upper_half = later_both[half_count:]
        kept = jnp.where(upper_side, upper_half, lower_half)
        given = jnp.where(upper_side, lower_half, upper_half)
        later_both = kept + from_partner(given.astype(jnp.bfloat16), ("ctx", "fsdp"), level).astype(
            given.dtype
        )
    key_mine = jnp.concatenate(
        [key_head, later_both[0, 0].reshape((2 * BLK,) + tail_shape)], axis=0
    )
    value_mine = jnp.concatenate(
        [value_head, later_both[0, 1].reshape((2 * BLK,) + tail_shape)], axis=0
    )
    grad_q = (
        unrotate(query_sum.reshape(row_count, head_count, HD), cosine, sine_table)
        .reshape(row_count, head_count * HD)
        .astype(bfloat)
    )
    grad_k = unrotate(key_mine, cosine, sine_table).reshape(row_count, kv_count * HD).astype(bfloat)
    grad_v = value_mine.reshape(row_count, kv_count * HD).astype(bfloat)
    grad_normed_x = lax.dot_general(
        grad_q, query_weight, CONTRACT_COLS, preferred_element_type=jnp.float32
    )
    grad_normed_x = grad_normed_x + lax.dot_general(
        grad_k, key_weight, CONTRACT_COLS, preferred_element_type=jnp.float32
    )
    grad_normed_x = grad_normed_x + lax.dot_general(
        grad_v, value_weight, CONTRACT_COLS, preferred_element_type=jnp.float32
    )
    grad_one = jnp.sum(grad_normed_x * unit_x, axis=0)
    grad_in = (grad_res + norm_back(unit_x, inv_x, grad_normed_x * gain_one)).astype(bfloat)
    projection_grads = jnp.concatenate([grad_q, grad_k, grad_v], axis=1)
    input_term = lax.dot_general(
        normed_x, projection_grads, CONTRACT_ROWS, preferred_element_type=jnp.float32
    )
    output_term = lax.dot_general(
        grad_branch, attended_low, CONTRACT_ROWS, preferred_element_type=jnp.float32
    )
    input_share, output_share, share_one, share_two, share_three, share_four = (
        lax.psum_scatter(input_term, ("ctx", "fsdp"), scatter_dimension=0, tiled=True),
        lax.psum_scatter(output_term, ("ctx", "fsdp"), scatter_dimension=0, tiled=True),
        lax.psum_scatter(grad_one, ("ctx", "fsdp"), scatter_dimension=0, tiled=True),
        lax.psum_scatter(grad_two, ("ctx", "fsdp"), scatter_dimension=0, tiled=True),
        lax.psum_scatter(grad_three, ("ctx", "fsdp"), scatter_dimension=0, tiled=True),
        lax.psum_scatter(grad_four, ("ctx", "fsdp"), scatter_dimension=0, tiled=True),
    )
    query_cols = head_count * HD
    key_cols = kv_count * HD
    grad_query = input_share[:, :query_cols]
    grad_key = input_share[:, query_cols : query_cols + key_cols]
    grad_value = input_share[:, query_cols + key_cols :]
    grad_output = output_share.T
    return (
        layer_out,
        grad_in,
        grad_query,
        grad_key,
        grad_value,
        grad_output,
        grad_gate,
        grad_up,
        down_sum,
        share_one,
        share_two,
        share_three,
        share_four,
    )


def kernels_fit(mesh_shape, rows, width, slot):
    planes = mesh_shape["ctx"] * mesh_shape["fsdp"] // 8
    tokens, hidden = planes * 2 * rows, 4 * slot
    wide_rows = 3 * hidden + 3 * tokens + (2 * planes + 1) * rows
    held = 2 * width * wide_rows + 6 * tokens * hidden + 2 * 2 * 768 * hidden
    return rows == 128 and planes == 4 and slot % 16 == 0 and held < 48 * 2**20


def on_device_kernels(
    mesh_shape,
    tokens_in,
    block_table,
    w_query,
    w_key,
    w_value,
    w_output,
    w_gate,
    w_up,
    w_down,
    gain_attn_in,
    gain_attn_out,
    gain_ffn_in,
    gain_ffn_out,
    cotangent,
):
    axes = ("ctx", "fsdp")
    bf, f32 = jnp.bfloat16, jnp.float32
    rows, width = tokens_in.shape
    shard = w_query.shape[0]
    devices = lax.axis_size(axes)
    me = lax.axis_index(axes)
    cosine, sine, qpos, kpos = placing(block_table, me, devices, 2 * devices * BLK)
    packed = pack_weights(w_query, w_key, w_value, w_output)
    gains = pack_gains((gain_attn_in, gain_attn_out, gain_ffn_in, gain_ffn_out), me, width)
    own = jnp.stack([w_gate.T.astype(bf), w_up.T.astype(bf), w_down.astype(bf)])
    split = (2, rows // 2, width)
    x = tokens_in.reshape(split)
    across, branch, *saved, gains = attend_call(
        mesh_shape, shard, x, packed, gains, cosine, sine, qpos, kpos, own
    )
    layer_out, grad_res, grad_branch, sums, mine, side, down = ffn_call(
        mesh_shape, branch.reshape(rows, width), tokens_in, cotangent, gains, own, across
    )
    grad_in, pieces, sums, side = retrace_call(
        mesh_shape,
        shard,
        grad_branch.reshape(split),
        grad_res.reshape(split),
        x,
        gains,
        sums,
        cosine,
        sine,
        qpos,
        kpos,
        saved,
        side,
    )
    pieces = pieces[:, :, :shard].astype(f32).transpose(2, 1, 0, 3)
    pairs = pieces[:, 0].reshape(shard, -1, 2, HD)
    grad_key = pairs[:, :, 0].reshape(w_key.shape)
    grad_value = pairs[:, :, 1].reshape(w_value.shape)
    grad_query = pieces[:, 1].reshape(w_query.shape)
    grad_output = pieces[:, 2].reshape(shard, -1).T
    grad_one = (
        jnp.sum(w_query.astype(bf).astype(f32) * grad_query, axis=1)
        + jnp.sum(w_key.astype(bf).astype(f32) * grad_key, axis=1)
        + jnp.sum(w_value.astype(bf).astype(f32) * grad_value, axis=1)
    ) / gain_attn_in.astype(bf).astype(f32)
    shares = lax.dynamic_slice(sums, (1, me * shard), (3, shard))
    return (
        layer_out,
        grad_in.reshape(rows, width),
        grad_query,
        grad_key,
        grad_value,
        grad_output,
        (mine[0].astype(f32) + side[0].astype(f32)).T,
        (mine[1].astype(f32) + side[1].astype(f32)).T,
        mine[2].astype(f32) + down.astype(f32),
        grad_one,
        shares[0],
        shares[1],
        shares[2],
    )


def solution(mesh):
    placed = (
        P(("ctx", "fsdp"), None),
        P(),
        P(("ctx", "fsdp"), None),
        P(("ctx", "fsdp"), None),
        P(("ctx", "fsdp"), None),
        P(None, ("ctx", "fsdp")),
        P(None, ("ctx", "fsdp")),
        P(None, ("ctx", "fsdp")),
        P(("ctx", "fsdp"), None),
        P(("ctx", "fsdp")),
        P(("ctx", "fsdp")),
        P(("ctx", "fsdp")),
        P(("ctx", "fsdp")),
        P(("ctx", "fsdp"), None),
    )
    shape = dict(mesh.shape)

    def program(tokens_in, *others):
        devices = shape["ctx"] * shape["fsdp"]
        rows, width = tokens_in.shape
        slot = others[7].shape[0] // devices
        if kernels_fit(shape, rows // devices, width, slot):
            body = functools.partial(on_device_kernels, shape)
        else:
            body = on_device
        return placed_over(mesh, placed, body)(tokens_in, *others)

    return program


def placed_over(mesh, placed, body):
    return jax.shard_map(
        body,
        mesh=mesh,
        in_specs=placed,
        out_specs=(
            P(("ctx", "fsdp"), None),
            P(("ctx", "fsdp"), None),
            P(("ctx", "fsdp"), None),
            P(("ctx", "fsdp"), None),
            P(("ctx", "fsdp"), None),
            P(None, ("ctx", "fsdp")),
            P(None, ("ctx", "fsdp")),
            P(None, ("ctx", "fsdp")),
            P(("ctx", "fsdp"), None),
            P(("ctx", "fsdp")),
            P(("ctx", "fsdp")),
            P(("ctx", "fsdp")),
            P(("ctx", "fsdp")),
        ),
        check_vma=False,
    )
```

```python
import functools
import math

import jax
import jax.numpy as jnp
import numpy as np
from jax import lax
from jax.experimental import pallas as pl
from jax.experimental.pallas import tpu as pltpu
from jax.sharding import PartitionSpec as P

HD = 256
BLK = 32
CONT_LEN = 512
KBLK = 1024


SOFT_CAP = 50.0
MASKED = -1e30
MESH = pl.DeviceIdType.MESH
NT = (((1,), (1,)), ((), ()))
NN = (((1,), (0,)), ((), ()))
TN = (((0,), (0,)), ((), ()))
NORM_EPS = 1e-06
GELU_A = 0.7978845608028654
GELU_B = 0.044715


def mm(left, right, dims):
    return lax.dot_general(left, right, dims, preferred_element_type=jnp.float32)


def spans(total, width):
    return [(at, min(width, total - at)) for at in range(0, total, width)]


def flip(index, bit):
    return index + bit - 2 * bit * ((index // bit) % 2)


def place(fs):
    return lax.axis_index("ctx") * fs + lax.axis_index("fsdp")


def device(index, fs):
    return (index // fs, index % fs)


def remote(src, dst, send, recv, to):
    return pltpu.make_async_remote_copy(
        src_ref=src, dst_ref=dst, send_sem=send, recv_sem=recv, device_id=to, device_id_type=MESH
    )


def line_order(p0, planes):
    few = jnp.minimum(p0, planes - 1 - p0)

    def order(k):
        two_sided = jnp.where(k % 2 == 1, p0 - (k + 1) // 2, p0 + (k + 1) // 2)
        one_sided = jnp.where(p0 > planes - 1 - p0, p0 - (k - few), p0 + (k - few))
        return jnp.where(k <= 2 * few, two_sided, one_sided)

    return order


def neighbours(me, planes, fs):
    p0 = me // 8
    right = device(jnp.minimum(me + 8, 8 * planes - 8 + me % 8), fs)
    left = device(jnp.maximum(me - 8, me % 8), fs)
    return p0, right, left, p0 < planes - 1, p0 > 0


def greet(peers, right, left, has_right, has_left):
    barrier = pltpu.get_barrier_semaphore()
    for peer in peers:
        pl.semaphore_signal(barrier, inc=1, device_id=peer, device_id_type=MESH)

    @pl.when(has_right)
    def _():
        pl.semaphore_signal(barrier, inc=1, device_id=right, device_id_type=MESH)

    @pl.when(has_left)
    def _():
        pl.semaphore_signal(barrier, inc=1, device_id=left, device_id_type=MESH)

    pl.semaphore_wait(
        barrier, len(peers) + jnp.where(has_right, 1, 0) + jnp.where(has_left, 1, 0)
    )


def rows_at(index, size):
    return pl.ds(pl.multiple_of(index * size, size), size)


def line_copies(view, p0, right, left, has_right, has_left, send_sem, recv_sem):
    def copy(p, to, way):
        return remote(view(p), view(p), send_sem.at[way, p], recv_sem.at[p], to)

    def send(p):
        @pl.when(has_right & (p <= p0))
        def _():
            copy(p, right, 0).start()

        @pl.when(has_left & (p >= p0))
        def _():
            copy(p, left, 1).start()

    def arrived(p):
        copy(p, right, 0).wait_recv()

    def drain(p):
        @pl.when(has_right & (p <= p0))
        def _():
            copy(p, right, 0).wait_send()

        @pl.when(has_left & (p >= p0))
        def _():
            copy(p, left, 1).wait_send()

    return send, arrived, drain


def chain_copies(view, slot, p0, planes, right, left, has_right, has_left, send_sem, recv_sem):
    def copy(p, to, into):
        return remote(view(p), slot(into), send_sem.at[p], recv_sem.at[into], to)

    def add(into, p):
        copy(p, right, into).wait_recv()
        mine = view(p)
        mine[...] = (
            mine[...].astype(jnp.float32) + slot(into)[...].astype(jnp.float32)
        ).astype(mine.dtype)

    def onward(p):
        @pl.when((has_left & (p > p0)) | (has_right & (p < p0)))
        def _():
            add(p, p)

        @pl.when(p > p0)
        def _():
            copy(p, right, p).start()

        @pl.when(p < p0)
        def _():
            copy(p, left, jnp.where(p == p0 - 1, planes, p)).start()

    def settle():
        @pl.when(has_left)
        def _():
            add(p0, p0)

        @pl.when(has_right)
        def _():
            add(planes, p0)

    def drain(p):
        @pl.when(p != p0)
        def _():
            copy(p, right, p).wait_send()

    return onward, settle, drain


def summing_levels(planes):
    return [8 << bit for bit in range(planes.bit_length() - 1)] + [2, 4, 1]


def unit_rows(values):
    inverse = lax.rsqrt(jnp.mean(values * values, axis=-1, keepdims=True) + NORM_EPS)
    return values * inverse, inverse


def plane_gather(buf, hd, xmate, ymate, send_sem, recv_sem):
    def copy(number, rows, to):
        view = buf.at[:, rows, :]
        return remote(view, view, send_sem.at[number], recv_sem.at[number], to)

    def part_of(index, lower):
        return pl.ds(pl.multiple_of(index * 64 + 32 * lower, 32), 32)

    own_x = copy(0, rows_at(hd, 64), xmate)
    own_y = copy(1, rows_at(hd, 64), ymate)
    on_y = copy(2, part_of(flip(hd, 1), 0), ymate)
    on_x = copy(3, part_of(flip(hd, 2), 1), xmate)
    return own_x, own_y, on_y, on_x


def plane_sum(part, wide, hd, xmate, ymate, yhalf, xhalf, yfull, xfull, send_sem, recv_sem):
    xm, ym = flip(hd, 1), flip(hd, 2)
    dg = flip(xm, 2)

    def cols(h):
        return pl.ds(pl.multiple_of(h * wide, 128), wide)

    def part_of(index, lower):
        return pl.ds(pl.multiple_of(index * 64 + 32 * lower, 32), 32)

    def copy(h, number):
        rows, into, to = routes[number]
        return remote(
            part.at[:, rows, cols(h)],
            into.at[h],
            send_sem.at[h, number],
            recv_sem.at[h, number],
            to,
        )

    routes = (
        (part_of(dg, 0), yhalf, ymate),
        (part_of(dg, 1), xhalf, xmate),
        (rows_at(xm, 64), xfull, xmate),
        (rows_at(ym, 64), yfull, ymate),
    )

    def first(h):
        for number in range(2):
            copy(h, number).start()

    def second(h):
        for number, rows, came in ((0, part_of(xm, 0), yhalf), (1, part_of(ym, 1), xhalf)):
            copy(h, number).wait_recv()
            part[:, rows, cols(h)] = (
                part[:, rows, cols(h)].astype(jnp.float32) + came[h].astype(jnp.float32)
            ).astype(part.dtype)
            copy(h, number + 2).start()

    def last(h):
        for number in (2, 3):
            copy(h, number).wait_recv()
        return (
            part[:, rows_at(hd, 64), cols(h)].astype(jnp.float32)
            + yfull[h].astype(jnp.float32)
            + xfull[h].astype(jnp.float32)
        )

    def drain(h):
        for number in range(4):
            copy(h, number).wait_send()

    return cols, first, second, last, drain


def plane_scratch(width):
    bf = jnp.bfloat16
    wide = width // 2
    return [
        pltpu.VMEM((2, 2, 32, wide), bf),
        pltpu.VMEM((2, 2, 32, wide), bf),
        pltpu.VMEM((2, 2, 64, wide), bf),
        pltpu.VMEM((2, 2, 64, wide), bf),
        pltpu.SemaphoreType.DMA((2, 4)),
        pltpu.SemaphoreType.DMA((2, 4)),
    ]


def rope_constants(blocks):
    frequency = 10000.0 ** (-(np.arange(HD // 2) * 2.0 / HD))
    starts = np.arange(blocks)[:, None] * BLK * frequency[None, :]
    inner = np.arange(BLK)[:, None] * frequency[None, :]
    coarse = np.stack([np.cos(starts), np.sin(starts)], axis=1).astype(np.float32)
    fine = np.stack([np.cos(inner), np.sin(inner)]).astype(np.float32)
    return coarse, fine


def locate(planes, table_ref, coarse_ref, fine_ref, me, cosine, sine, qpos, kpos):
    head_blocks = 16 * planes
    span = CONT_LEN // BLK
    p0, c = me // 8, me % 2

    def block_of(p, pair, core_index, slot):
        found = table_ref[4 * (p * 8 + 2 * pair + core_index) + slot]
        if slot < 2:
            return found
        return head_blocks + lax.rem(found - head_blocks, span)

    lane = lax.broadcasted_iota(jnp.int32, (1, 512), 1)
    for p in range(planes + 1):
        start = jnp.zeros((1, 512), jnp.int32)
        for group in range(16):
            core_index, pair, part = group // 8, (group % 8) // 2, group % 2
            if p < planes:
                found = block_of(p, pair, core_index, part)
            else:
                found = block_of(p0, pair, core_index, 2 + part)
            start = jnp.where(lane // BLK == group, found, start)
        kpos[p] = start * BLK + lane % BLK
    row = lax.broadcasted_iota(jnp.int32, (BLK, 1), 0)
    for kind in range(2):
        for group in range(8):
            found = block_of(p0, group // 2, c, 2 * kind + group % 2)
            begin = group * BLK
            for head in range(2):
                qpos[kind, head * 256 + begin : head * 256 + begin + BLK, :] = found * BLK + row
            turned = coarse_ref[found]
            over_cos, over_sin = turned[0:1, :], turned[1:2, :]
            rows = slice(kind * 256 + begin, kind * 256 + begin + BLK)
            cosine[rows, :] = over_cos * fine_ref[0] - over_sin * fine_ref[1]
            sine[rows, :] = over_sin * fine_ref[0] + over_cos * fine_ref[1]


def turn(values, cosine, sine, back):
    half = values.shape[-1] // 2
    first, second = values[:, :half], values[:, half:]
    if back:
        return jnp.concatenate(
            [first * cosine + second * sine, second * cosine - first * sine], axis=-1
        )
    return jnp.concatenate([first * cosine - second * sine, second * cosine + first * sine], axis=-1)


def attend_kernel(
    planes,
    fs,
    shard,
    x_ref,
    wq_ref,
    wk_ref,
    wv_ref,
    wo_ref,
    gains_ref,
    table_ref,
    coarse_ref,
    fine_ref,
    gate_in,
    up_in,
    down_in,
    across_ref,
    branch_ref,
    w6_out,
    feats_out,
    queries_out,
    kv_out,
    low_out,
    mix_out,
    norm_ref,
    spread_ref,
    own_out,
    w6,
    feats_ref,
    queries_ref,
    kv_ref,
    low_ref,
    mix_ref,
    packed_ref,
    cos_ref,
    sin_ref,
    qpos_ref,
    kpos_ref,
    raw,
    ffn_ref,
    raw_sem,
    own_sem,
    wrecv,
    whole,
    total,
    part,
    yhalf,
    xhalf,
    yfull,
    xfull,
    rs_s,
    rs_r,
    grecv,
    xs,
    a2a_s,
    a2a_r,
    n1_s,
    n1_r,
    wz_s,
    wz_r,
    wd_s,
    wd_r,
    kz_s,
    kz_r,
    kd_s,
    kd_r,
    g_s,
    g_r,
    ffn_s,
    ffn_r,
    keep,
):
    P = planes
    bf, f32 = jnp.bfloat16, jnp.float32
    width = x_ref.shape[2]
    deep = 8 * shard
    me = place(fs)
    s, hd, c = me % 8, (me % 8) // 2, me % 2
    p0, right, left, has_right, has_left = neighbours(me, P, fs)
    order = line_order(p0, P)
    core = device(flip(me, 1), fs)
    xmate = device(flip(me, 2), fs)
    ymate = device(flip(me, 4), fs)
    plane = [(s + d) % 8 for d in range(1, 8)]
    others = [device(p0 * 8 + one, fs) for one in plane]
    levels = summing_levels(P)
    far = [device(flip(me, bit), fs) for bit in levels]
    greet(others + far[1:-3], right, left, has_right, has_left)

    kept = [
        pltpu.make_async_copy(held, out, keep.at[number])
        for number, (held, out) in enumerate(
            (
                (w6, w6_out),
                (feats_ref, feats_out),
                (queries_ref, queries_out),
                (kv_ref, kv_out),
                (low_ref, low_out),
                (mix_ref, mix_out),
            )
        )
    ]

    def keep_all(first, last):
        for one in kept[first:last]:
            one.start()

    def gain_copy(level):
        return remote(spread_ref, grecv.at[level], g_s.at[level], g_r.at[level], far[level])

    def gain_next(level):
        gain_copy(level).wait()
        spread_ref[...] += grecv[level]
        if level + 1 < len(levels):
            gain_copy(level + 1).start()

    def a2a_copy(j, d):
        return remote(
            packed_ref.at[plane[d], j], wrecv.at[s, j], a2a_s.at[j, d], a2a_r.at[j, d], others[d]
        )

    own_x, own_y, on_y, on_x = plane_gather(xs, hd, xmate, ymate, n1_s, n1_r)

    def ffn_copy(which):
        return remote(
            ffn_ref.at[which], across_ref.at[which], ffn_s.at[which], ffn_r.at[which], xmate
        )

    spread_ref[...] = gains_ref[...].astype(bf).astype(f32)
    gain_copy(0).start()
    raws = [
        pltpu.make_async_copy(source, held, raw_sem.at[number])
        for number, (source, held) in enumerate(
            ((gate_in, raw.at[0]), (up_in, raw.at[1]), (down_in, raw.at[2]))
        )
    ]
    for one in raws:
        one.start()
    owns = [
        pltpu.make_async_copy(ffn_ref.at[which], own_out.at[which], own_sem.at[which])
        for which in range(3)
    ]

    def ffn_turn(which):
        raws[which].wait()
        ffn_ref[which] = raw[which].astype(bf)
        owns[which].start()

    def pack(j):
        for one in range(8):
            cols = slice(one * HD, (one + 1) * HD)
            pair = slice(one // 2 * HD, (one // 2 + 1) * HD)
            if j == 0:
                piece = (wk_ref, wv_ref)[one % 2][:, pair]
            elif j == 1:
                piece = wq_ref[:, cols]
            else:
                piece = wo_ref[:, cols]
            packed_ref[one, j, :shard, :] = piece.astype(bf)
            if shard < packed_ref.shape[2]:
                packed_ref[one, j, shard:, :] = jnp.zeros(
                    (packed_ref.shape[2] - shard, HD), bf
                )

    def a2a_start(j):
        for d in range(7):
            a2a_copy(j, d).start()

    xs[:, rows_at(hd, 64), :] = x_ref[...]
    pack(0)
    a2a_start(0)
    pack(1)
    a2a_start(1)
    own_x.start()
    own_y.start()
    pack(2)
    wrecv[s] = packed_ref[s]
    for level in range(len(levels) - 3):
        gain_next(level)

    def assemble(j):
        for d in range(7):
            a2a_copy(j, d).wait_recv()
        for one in range(8):
            whole[one * shard : (one + 1) * shard, :] = wrecv[one, j, :shard, :].astype(f32)
        w6[2 * j + c, rows_at(p0, deep), :] = whole[...].astype(bf)

    def chunk(j):
        def view(p):
            return w6.at[2 * j + c, rows_at(p, deep)]

        send, arrived, drain = line_copies(
            view, p0, right, left, has_right, has_left, wz_s.at[j], wz_r.at[j]
        )

        def over(p):
            return remote(view(p), view(p), wd_s.at[j, p], wd_r.at[j, p], core)

        def begin():
            send(p0)
            over(p0).start()

        def step(k):
            p = order(k)
            arrived(p)
            send(p)
            over(p).start()

        def have(p):
            over(p).wait_recv()

        def finish():
            for p in range(P):
                over(p).wait_send()
                drain(p)

        return begin, step, have, finish

    begin0, step0, have0, finish0 = chunk(0)
    begin1, step1, have1, finish1 = chunk(1)
    begin2, step2, have2, finish2 = chunk(2)
    assemble(0)
    begin0()
    assemble(1)
    ffn_turn(0)
    for k in range(1, P):
        step0(k)
        if k == 1:
            own_x.wait_recv()
            on_y.start()
            gain_next(len(levels) - 3)
        if k == P - 2:
            own_y.wait_recv()
            on_x.start()
            a2a_start(2)
            ffn_copy(0).start()
            locate(P, table_ref, coarse_ref, fine_ref, me, cos_ref, sin_ref, qpos_ref, kpos_ref)
    begin1()
    ffn_turn(1)
    ffn_copy(1).start()
    gain_next(len(levels) - 2)
    gain_next(len(levels) - 1)
    on_y.wait_recv()
    on_x.wait_recv()

    def norm_rows(number, carry):
        for kind in range(2):
            rows = rows_at(number, 64)
            unit, _ = unit_rows(xs[kind, rows, :].astype(f32))
            feats_ref[kind, rows, :] = (unit * spread_ref[0:1, :]).astype(bf)
        return carry

    lax.fori_loop(0, 4, norm_rows, 0)
    for p in range(P):
        have0(p)

    def kv_rows(p, core_index):
        return rows_at(2 * p + core_index, 256)

    for kind in range(2):
        feats = feats_ref[kind]
        cosine = cos_ref[kind * 256 : (kind + 1) * 256, :]
        sine = sin_ref[kind * 256 : (kind + 1) * 256, :]
        block = kv_rows(p0 if kind == 0 else P, c)
        kv_ref[block, :HD] = turn(mm(feats, w6[0], NN), cosine, sine, False).astype(bf)
        kv_ref[block, HD:] = mm(feats, w6[1], NN).astype(bf)

    def kv_view(p):
        return kv_ref.at[kv_rows(p, c)]

    kv_send, kv_arrived, kv_drain = line_copies(
        kv_view, p0, right, left, has_right, has_left, kz_s, kz_r
    )

    def kv_over(p):
        return remote(kv_view(p), kv_view(p), kd_s.at[p], kd_r.at[p], core)

    kv_send(p0)
    kv_over(p0).start()
    kv_over(P).start()
    for k in range(1, P):
        step1(k)
    for p in range(P):
        have1(p)
    for kind in range(2):
        feats = feats_ref[kind]
        cosine = cos_ref[kind * 256 : (kind + 1) * 256, :]
        sine = sin_ref[kind * 256 : (kind + 1) * 256, :]
        for head in range(2):
            queries_ref[kind, head * 256 : (head + 1) * 256, :] = turn(
                mm(feats, w6[2 + head], NN), cosine, sine, False
            ).astype(bf)
    for k in range(1, P):
        p = order(k)
        kv_arrived(p)
        kv_send(p)
        kv_over(p).start()
    assemble(2)
    begin2()
    ffn_turn(2)
    total[...] = jnp.zeros_like(total)
    mix_ref[...] = jnp.zeros_like(mix_ref)

    def flash(p, kind, masked):
        rows = rows_at(p, 512)
        bent = jnp.tanh(
            mm(queries_ref[kind], kv_ref[rows, :HD], NT) * (HD ** (-0.5) / SOFT_CAP)
        )
        grown = jnp.exp(SOFT_CAP * bent)
        if masked:
            grown = jnp.where(kpos_ref[p] <= qpos_ref[kind], grown, 0.0)
        total[kind] += (
            grown[:, :128] + grown[:, 128:256] + grown[:, 256:384] + grown[:, 384:512]
        )
        mix_ref[kind] += mm(grown.astype(bf), kv_ref[rows, HD:], NN)

    kv_over(P).wait_recv()
    flash(P, 1, True)

    def tile(k, carry):
        p = order(k)
        kv_over(p).wait_recv()
        flash(p, 0, True)
        flash(p, 1, False)

        @pl.when((k > 0) & (k < P - 1))
        def _():
            step2(k)

        return carry

    lax.fori_loop(0, P, tile, 0)
    for kind in range(2):
        inverse = 1.0 / jnp.sum(total[kind], axis=-1, keepdims=True)
        norm_ref[kind] = inverse
        mixed = mix_ref[kind] * inverse
        mix_ref[kind] = mixed
        low_ref[kind] = mixed.astype(bf)
    wide = width // 2
    cols, first, second, last, drain_sum = plane_sum(
        part, wide, hd, xmate, ymate, yhalf, xhalf, yfull, xfull, rs_s, rs_r
    )

    def project(h):
        for p in range(P // 2):
            have2(h * (P // 2) + p)
        for kind in range(2):
            for at, size in spans(wide, 384):
                rows = pl.ds(pl.multiple_of(h * wide + at, 128), size)
                part[kind, :, rows] = (
                    mm(low_ref[kind, :256, :], w6[4, rows, :], NT)
                    + mm(low_ref[kind, 256:, :], w6[5, rows, :], NT)
                ).astype(bf)
        first(h)

    near = p0 // (P // 2)
    keep_all(1, 6)
    project(near)
    step2(P - 1)
    second(near)
    project(1 - near)
    keep_all(0, 1)
    second(1 - near)
    for h in range(2):
        branch_ref[:, :, h * wide : (h + 1) * wide] = last(h)
    for h in range(2):
        drain_sum(h)
    for one in (own_x, own_y, on_y, on_x):
        one.wait_send()
    for j in range(3):
        for d in range(7):
            a2a_copy(j, d).wait_send()
    for finish in (finish0, finish1, finish2):
        finish()
    for p in range(P):
        kv_drain(p)
        kv_over(p).wait_send()
    kv_over(P).wait_send()
    for which in range(2):
        ffn_copy(which).wait()
    for one in kept + owns:
        one.wait()


def attend_call(
    mesh_shape, x, w_query, w_key, w_value, w_output, gains, table, w_gate, w_up, w_down
):
    fs = mesh_shape["fsdp"]
    planes = mesh_shape["ctx"] * fs // 8
    shard, slot = w_query.shape[0], w_down.shape[0]
    padded = shard + -shard % 16
    width = x.shape[2]
    bf, f32 = jnp.bfloat16, jnp.float32
    vmem = pl.BlockSpec(memory_space=pltpu.VMEM)
    hbm = pl.BlockSpec(memory_space=pl.ANY)
    smem = pl.BlockSpec(memory_space=pltpu.SMEM)
    dma = pltpu.SemaphoreType.DMA
    shape = jax.ShapeDtypeStruct
    kv_rows = (2 * planes + 2) * 256
    coarse, fine = rope_constants(16 * planes + CONT_LEN // BLK)
    return pl.pallas_call(
        functools.partial(attend_kernel, planes, fs, shard),
        out_shape=(
            shape((2, slot, width), bf),
            shape((2, 64, width), f32),
            shape((6, width, HD), bf),
            shape((2, 256, width), bf),
            shape((2, 512, HD), bf),
            shape((kv_rows, 2 * HD), bf),
            shape((2, 512, HD), bf),
            shape((2, 512, HD), f32),
            shape((2, 512, 1), f32),
            shape((8, width), f32),
            shape((3, slot, width), bf),
        ),
        in_specs=[vmem] * 6 + [smem, vmem, vmem] + [hbm] * 3,
        out_specs=(hbm, vmem) + (hbm,) * 6 + (vmem,) * 2 + (hbm,),
        scratch_shapes=[
            pltpu.VMEM((6, width, HD), bf),
            pltpu.VMEM((2, 256, width), bf),
            pltpu.VMEM((2, 512, HD), bf),
            pltpu.VMEM((kv_rows, 2 * HD), bf),
            pltpu.VMEM((2, 512, HD), bf),
            pltpu.VMEM((2, 512, HD), f32),
            pltpu.VMEM((8, 3, padded, HD), bf),
            pltpu.VMEM((512, HD // 2), f32),
            pltpu.VMEM((512, HD // 2), f32),
            pltpu.VMEM((2, 512, 1), jnp.int32),
            pltpu.VMEM((planes + 1, 1, 512), jnp.int32),
            pltpu.VMEM((3, slot, width), f32),
            pltpu.VMEM((3, slot, width), bf),
            dma((3,)),
            dma((3,)),
            pltpu.VMEM((8, 3, padded, HD), bf),
            pltpu.VMEM((8 * shard, HD), f32),
            pltpu.VMEM((2, 512, 128), f32),
            pltpu.VMEM((2, 256, width), bf),
            *plane_scratch(width),
            pltpu.VMEM((len(summing_levels(planes)), 8, width), f32),
            pltpu.VMEM((2, 256, width), bf),
            dma((3, 7)),
            dma((3, 7)),
            dma((4,)),
            dma((4,)),
            dma((3, 2, planes)),
            dma((3, planes)),
            dma((3, planes)),
            dma((3, planes)),
            dma((2, planes)),
            dma((planes,)),
            dma((planes + 1,)),
            dma((planes + 1,)),
            dma((5,)),
            dma((5,)),
            dma((2,)),
            dma((2,)),
            dma((6,)),
        ],
        compiler_params=pltpu.CompilerParams(
            collective_id=2, has_side_effects=True, vmem_limit_bytes=56 * 2**20
        ),
        name="attend",
    )(
        x,
        w_query,
        w_key,
        w_value,
        w_output.T,
        gains,
        table,
        jnp.asarray(coarse),
        jnp.asarray(fine),
        w_gate.T,
        w_up.T,
        w_down,
    )


def retrace_kernel(
    planes,
    fs,
    shard,
    da_ref,
    dh_ref,
    x_ref,
    gain_ref,
    gsum_ref,
    table_ref,
    coarse_ref,
    fine_ref,
    norm_ref,
    w6_in,
    feats_in,
    queries_in,
    kv_in,
    low_in,
    mix_in,
    dw_ref,
    gin_ref,
    gw_ref,
    gall_ref,
    across_ref,
    w6,
    feats,
    queries_ref,
    kv_ref,
    low_ref,
    mix_ref,
    cos_ref,
    sin_ref,
    qpos_ref,
    kpos_ref,
    dap,
    dob,
    delta,
    dq,
    dqkv,
    kvg,
    kvd,
    kvz,
    dw6,
    dwd,
    dwz,
    whole,
    asend,
    dn1,
    part,
    yhalf,
    xhalf,
    yfull,
    xfull,
    rs_s,
    rs_r,
    grecv,
    load,
    a2a_s,
    a2a_r,
    n1_s,
    n1_r,
    wz_s,
    wz_r,
    wd_s,
    wd_r,
    kz_s,
    kz_r,
    kd_s,
    kd_r,
    g_s,
    g_r,
    ffn_s,
    ffn_r,
):
    P = planes
    bf, f32 = jnp.bfloat16, jnp.float32
    width = da_ref.shape[2]
    deep = 8 * shard
    me = place(fs)
    s, hd, c = me % 8, (me % 8) // 2, me % 2
    p0, right, left, has_right, has_left = neighbours(me, P, fs)
    order = line_order(p0, P)
    core = device(flip(me, 1), fs)
    xmate = device(flip(me, 2), fs)
    ymate = device(flip(me, 4), fs)
    plane = [(s + d) % 8 for d in range(1, 8)]
    others = [device(p0 * 8 + one, fs) for one in plane]
    levels = summing_levels(P)
    far = [device(flip(me, bit), fs) for bit in levels]
    greet(others + far[1:-3], right, left, has_right, has_left)

    def gain_copy(level):
        return remote(gall_ref, grecv.at[level], g_s.at[level], g_r.at[level], far[level])

    def gain_next(level):
        gain_copy(level).wait()
        gall_ref[...] += grecv[level]
        if level + 1 < len(levels):
            gain_copy(level + 1).start()

    own_x, own_y, on_y, on_x = plane_gather(dap, hd, xmate, ymate, n1_s, n1_r)

    def ffn_copy(which):
        return remote(
            dw_ref.at[which], across_ref.at[which], ffn_s.at[which], ffn_r.at[which], xmate
        )

    dap[:, rows_at(hd, 64), :] = da_ref[...]
    gall_ref[...] = gsum_ref[...]
    gain_copy(0).start()
    own_x.start()
    own_y.start()
    loads = [
        pltpu.make_async_copy(source, held, load.at[number])
        for number, (source, held) in enumerate(
            (
                (w6_in, w6),
                (low_in, low_ref),
                (mix_in, mix_ref),
                (queries_in, queries_ref),
                (kv_in, kv_ref),
                (feats_in, feats),
            )
        )
    ]
    for one in loads:
        one.start()
    dq[...] = jnp.zeros_like(dq)
    asend[...] = jnp.zeros_like(asend)
    locate(P, table_ref, coarse_ref, fine_ref, me, cos_ref, sin_ref, qpos_ref, kpos_ref)
    for number in range(2):
        gain_next(number)
    own_x.wait_recv()
    on_y.start()
    own_y.wait_recv()
    on_x.start()
    for which in range(2):
        ffn_copy(which).start()
    for one in loads:
        one.wait()
    on_y.wait_recv()
    on_x.wait_recv()
    for kind in range(2):
        for head in range(2):
            rows = slice(head * 256, (head + 1) * 256)
            dob[kind, rows, :] = mm(dap[kind], w6[4 + head], NN).astype(bf)
        delta[kind] = jnp.sum(dob[kind].astype(f32) * mix_ref[kind], axis=-1, keepdims=True)

    def weight(index, left_of, right_of):
        for first, wide in spans(width, 768):
            cols = slice(first, first + wide)
            dw6[index, cols, :] = (
                mm(left_of[0, :, cols], right_of(0), TN) + mm(left_of[1, :, cols], right_of(1), TN)
            ).astype(bf)

    def chunk(j):
        def over():
            return remote(
                dw6.at[2 * j + 1 - c], dwd.at[j], wd_s.at[j], wd_r.at[j], core
            )

        def add():
            over().wait_recv()

            def some(p, carry):
                rows = rows_at(p, deep)
                dw6[2 * j + c, rows, :] = (
                    dw6[2 * j + c, rows, :].astype(f32) + dwd[j, rows, :].astype(f32)
                ).astype(bf)
                return carry

            lax.fori_loop(0, P, some, 0)

        onward, settle, drain = chain_copies(
            lambda p: dw6.at[2 * j + c, rows_at(p, deep)],
            lambda into: dwz.at[j, rows_at(into, deep)],
            p0,
            P,
            right,
            left,
            has_right,
            has_left,
            wz_s.at[j],
            wz_r.at[j],
        )

        def finish():
            over().wait_send()
            for p in range(P):
                drain(p)

        return over, add, onward, settle, finish

    def a2a_copy(j, d):
        return remote(
            asend.at[plane[d], j], gw_ref.at[s, j], a2a_s.at[j, d], a2a_r.at[j, d], others[d]
        )

    def spread(j):
        whole[...] = dw6[2 * j + c, rows_at(p0, deep), :].astype(f32)
        for one in range(8):
            asend[one, j, :shard, :] = whole[one * shard : (one + 1) * shard, :].astype(bf)
        for d in range(7):
            a2a_copy(j, d).start()
        gw_ref[s, j] = asend[s, j]

    over0, add0, onward0, settle0, finish0 = chunk(0)
    over1, add1, onward1, settle1, finish1 = chunk(1)
    over2, add2, onward2, settle2, finish2 = chunk(2)
    for head in range(2):
        weight(4 + head, dap, lambda kind: low_ref[kind, head * 256 : (head + 1) * 256, :])
    over2().start()

    def flash(p, kind, masked):
        rows = rows_at(p, 512)
        keys, values = kv_ref[rows, :HD], kv_ref[rows, HD:]
        bent = jnp.tanh(mm(queries_ref[kind], keys, NT) * (HD ** (-0.5) / SOFT_CAP))
        soft = jnp.exp(SOFT_CAP * bent) * norm_ref[kind]
        if masked:
            soft = jnp.where(kpos_ref[p] <= qpos_ref[kind], soft, 0.0)
        dots = mm(dob[kind], values, NT)
        score = (soft * (dots - delta[kind]) * (1.0 - bent * bent) * HD ** (-0.5)).astype(bf)
        dq[kind] += mm(score, keys, NN)
        return mm(score, queries_ref[kind], TN), mm(soft.astype(bf), dob[kind], TN)

    def half(p, core_index):
        return rows_at(2 * p + core_index, 256)

    def kv_over(p):
        return remote(
            kvg.at[half(p, 1 - c)], kvd.at[rows_at(p, 256)], kd_s.at[p], kd_r.at[p], core
        )

    def kv_add(p):
        kv_over(p).wait_recv()
        rows = half(p, c)
        kvg[rows, :] = (
            kvg[rows, :].astype(f32) + kvd[rows_at(p, 256), :].astype(f32)
        ).astype(bf)

    kv_onward, kv_settle, kv_drain = chain_copies(
        lambda p: kvg.at[half(p, c)],
        lambda into: kvz.at[rows_at(into, 256)],
        p0,
        P,
        right,
        left,
        has_right,
        has_left,
        kz_s,
        kz_r,
    )
    dk, dv = flash(P, 1, True)
    kvg[rows_at(P, 512), :HD] = dk.astype(bf)
    kvg[rows_at(P, 512), HD:] = dv.astype(bf)
    kv_over(P).start()
    add2()

    def tile(j, carry):
        p = order(P - 1 - j)
        dk, dv = flash(p, 0, True)
        more_dk, more_dv = flash(p, 1, False)
        kvg[rows_at(p, 512), :HD] = (dk + more_dk).astype(bf)
        kvg[rows_at(p, 512), HD:] = (dv + more_dv).astype(bf)
        kv_over(p).start()

        @pl.when(j < P - 1)
        def _():
            onward2(p)

        return carry

    lax.fori_loop(0, P, tile, 0)
    gain_next(2)
    for kind in range(2):
        rows = slice(kind * 256, (kind + 1) * 256)
        for head in range(2):
            cols = slice(head * 256, (head + 1) * 256)
            dqkv[2 + head, rows, :] = turn(
                dq[kind, cols, :], cos_ref[rows, :], sin_ref[rows, :], True
            ).astype(bf)
    for head in range(2):
        weight(2 + head, feats, lambda kind: dqkv[2 + head, kind * 256 : (kind + 1) * 256, :])
    over1().start()

    def kv_step(j, carry):
        p = order(P - 1 - j)
        kv_add(p)
        kv_onward(p)
        return carry

    lax.fori_loop(0, P - 1, kv_step, 0)
    settle2()
    spread(2)
    add1()

    def q_step(j, carry):
        onward1(order(P - 1 - j))
        return carry

    lax.fori_loop(0, P - 1, q_step, 0)
    kv_add(P)
    kv_add(p0)
    kv_settle()
    for kind in range(2):
        rows = slice(kind * 256, (kind + 1) * 256)
        block = half(p0 if kind == 0 else P, c)
        dqkv[0, rows, :] = turn(
            kvg[block, :HD].astype(f32), cos_ref[rows, :], sin_ref[rows, :], True
        ).astype(bf)
        dqkv[1, rows, :] = kvg[block, HD:]
    for one in range(2):
        weight(one, feats, lambda kind: dqkv[one, kind * 256 : (kind + 1) * 256, :])
    over0().start()

    wide = width // 2
    cols, first, second, last, drain_sum = plane_sum(
        part, wide, hd, xmate, ymate, yhalf, xhalf, yfull, xfull, rs_s, rs_r
    )

    def project(h):
        for kind in range(2):
            source = slice(kind * 256, (kind + 1) * 256)
            for at, size in spans(wide, 384):
                rows = slice(h * wide + at, h * wide + at + size)
                summed = mm(dqkv[0, source, :], w6[0, rows, :], NT)
                for one in range(1, 4):
                    summed = summed + mm(dqkv[one, source, :], w6[one, rows, :], NT)
                part[kind, :, rows] = summed.astype(bf)
        first(h)

    add0()

    def last_step(j, carry):
        onward0(order(P - 1 - j))
        return carry

    project(0)
    lax.fori_loop(0, 1, last_step, 0)
    project(1)
    settle1()
    spread(1)
    second(0)
    lax.fori_loop(1, P - 1, last_step, 0)
    second(1)
    for number in range(3, len(levels)):
        gain_next(number)
    for h in range(2):
        dn1[:, :, h * wide : (h + 1) * wide] = last(h) * gain_ref[0:1, h * wide : (h + 1) * wide]
    settle0()
    spread(0)
    for kind in range(2):
        unit, inverse = unit_rows(x_ref[kind].astype(f32))
        grads = dn1[kind]
        gin_ref[kind] = (
            dh_ref[kind]
            + inverse * (grads - unit * jnp.mean(grads * unit, axis=-1, keepdims=True))
        ).astype(bf)
    for j in range(3):
        for d in range(7):
            a2a_copy(j, d).wait()
    for h in range(2):
        drain_sum(h)
    for one in (own_x, own_y, on_y, on_x):
        one.wait_send()
    for finish in (finish0, finish1, finish2):
        finish()
    for p in range(P):
        kv_drain(p)
        kv_over(p).wait_send()
    kv_over(P).wait_send()
    for which in range(2):
        ffn_copy(which).wait()


def retrace_call(
    mesh_shape, shard, da, dh, x, gain, gsum, table, saved, partial
):
    w6, feats, queries, kv, low, mix, norm = saved
    fs = mesh_shape["fsdp"]
    planes = mesh_shape["ctx"] * fs // 8
    width = da.shape[2]
    bf, f32 = jnp.bfloat16, jnp.float32
    vmem = pl.BlockSpec(memory_space=pltpu.VMEM)
    hbm = pl.BlockSpec(memory_space=pl.ANY)
    dma = pltpu.SemaphoreType.DMA
    shape = jax.ShapeDtypeStruct
    deep = 8 * shard
    padded = shard + -shard % 16
    levels = len(summing_levels(planes))
    smem = pl.BlockSpec(memory_space=pltpu.SMEM)
    coarse, fine = rope_constants(16 * planes + CONT_LEN // BLK)
    return pl.pallas_call(
        functools.partial(retrace_kernel, planes, fs, shard),
        out_shape=(
            shape((2, 64, width), bf),
            shape((8, 3, padded, HD), bf),
            shape((8, width), f32),
            shape(partial.shape, bf),
        ),
        in_specs=[vmem] * 5 + [smem] + [vmem] * 3 + [hbm] * 7,
        out_specs=(vmem, vmem, vmem, hbm),
        scratch_shapes=[
            pltpu.VMEM((6, width, HD), bf),
            pltpu.VMEM((2, 256, width), bf),
            pltpu.VMEM((2, 512, HD), bf),
            pltpu.VMEM(((2 * planes + 2) * 256, 2 * HD), bf),
            pltpu.VMEM((2, 512, HD), bf),
            pltpu.VMEM((2, 512, HD), f32),
            pltpu.VMEM((512, HD // 2), f32),
            pltpu.VMEM((512, HD // 2), f32),
            pltpu.VMEM((2, 512, 1), jnp.int32),
            pltpu.VMEM((planes + 1, 1, 512), jnp.int32),
            pltpu.VMEM((2, 256, width), bf),
            pltpu.VMEM((2, 512, HD), bf),
            pltpu.VMEM((2, 512, 1), f32),
            pltpu.VMEM((2, 512, HD), f32),
            pltpu.VMEM((4, 512, HD), bf),
            pltpu.VMEM(((2 * planes + 2) * 256, 2 * HD), bf),
            pltpu.VMEM(((planes + 1) * 256, 2 * HD), bf),
            pltpu.VMEM(((planes + 1) * 256, 2 * HD), bf),
            pltpu.VMEM((6, width, HD), bf),
            pltpu.VMEM((3, width, HD), bf),
            pltpu.VMEM((3, (planes + 1) * deep, HD), bf),
            pltpu.VMEM((deep, HD), f32),
            pltpu.VMEM((8, 3, padded, HD), bf),
            pltpu.VMEM((2, 64, width), f32),
            pltpu.VMEM((2, 256, width), bf),
            *plane_scratch(width),
            pltpu.VMEM((levels, 8, width), f32),
            dma((6,)),
            dma((3, 7)),
            dma((3, 7)),
            dma((4,)),
            dma((4,)),
            dma((3, planes)),
            dma((3, planes + 1)),
            dma((3,)),
            dma((3,)),
            dma((planes,)),
            dma((planes + 1,)),
            dma((planes + 1,)),
            dma((planes + 1,)),
            dma((levels,)),
            dma((levels,)),
            dma((2,)),
            dma((2,)),
        ],
        compiler_params=pltpu.CompilerParams(
            collective_id=3, has_side_effects=True, vmem_limit_bytes=60 * 2**20
        ),
        name="retrace",
    )(
        da,
        dh,
        x,
        gain,
        gsum,
        table,
        jnp.asarray(coarse),
        jnp.asarray(fine),
        norm,
        w6,
        feats,
        queries,
        kv,
        low,
        mix,
        partial,
    )


def ffn_kernel(
    planes,
    fs,
    branch_ref,
    x_ref,
    dy_ref,
    gain_ref,
    own_ref,
    across_ref,
    out_ref,
    dh_ref,
    da_ref,
    gsum_ref,
    dwown_ref,
    dwside_ref,
    dwdown_ref,
    w,
    hidden_in,
    ffn,
    n2all,
    dfall,
    gate,
    up,
    act,
    part,
    yrecv,
    zrecv,
    zhalf,
    stage,
    load,
    push_s,
    push_r,
    ag_ys,
    ag_yr,
    ag_zs,
    ag_zr,
    rs_ys,
    rs_yr,
    rs_zs,
    rs_zr,
    ag_bs,
    ag_br,
    rs_bs,
    rs_br,
    dw_s,
    dw_r,
    down_s,
    down_r,
    store,
    ready,
):
    P = planes
    rows, width = x_ref.shape
    slot = own_ref.shape[1]
    hidden = 4 * slot
    bf, f32 = jnp.bfloat16, jnp.float32
    me = place(fs)
    y0 = (me // 4) % 2
    p0, right, left, has_right, has_left = neighbours(me, P, fs)
    order = line_order(p0, P)
    core = device(flip(me, 1), fs)
    xmate = device(flip(me, 2), fs)
    partner = device(flip(me, 4), fs)

    def block(p, y):
        return rows_at(p * 2 + y, rows)

    def pair(p):
        return rows_at(p, 2 * rows)

    def at(p):
        return rows_at(p, rows)

    def some_rows(body):
        def step(number, carry):
            body(rows_at(number, 32))
            return carry

        lax.fori_loop(0, rows // 32, step, 0)

    own_rows = (p0 * 2 + y0) * rows

    def inside(chunk):
        return pl.ds(pl.multiple_of(own_rows + chunk.start, 32), 32)

    local = [
        pltpu.make_async_copy(own_ref.at[which], w.at[which, pl.ds(0, slot)], load.at[which])
        for which in range(3)
    ] + [
        pltpu.make_async_copy(
            across_ref.at[which], w.at[which, pl.ds(slot, slot)], load.at[3 + which]
        )
        for which in range(2)
    ]
    for copy in local:
        copy.start()
    greet([core, xmate, partner], right, left, has_right, has_left)
    pushes = [
        remote(
            own_ref.at[which],
            w.at[which, pl.ds(2 * slot, slot)],
            push_s.at[which],
            push_r.at[which],
            core,
        )
        for which in range(3)
    ] + [
        remote(
            across_ref.at[which],
            w.at[which, pl.ds(3 * slot, slot)],
            push_s.at[3 + which],
            push_r.at[3 + which],
            core,
        )
        for which in range(2)
    ]
    down_across = remote(
        own_ref.at[2], w.at[2, pl.ds(slot, slot)], push_s.at[5], push_r.at[5], xmate
    )
    down_over = remote(
        w.at[2, pl.ds(slot, slot)],
        w.at[2, pl.ds(3 * slot, slot)],
        push_s.at[6],
        push_r.at[6],
        core,
    )
    down_across.start()

    def enter(chunk):
        unit, _ = unit_rows(branch_ref[chunk, :])
        values = x_ref[chunk, :].astype(f32) + unit * gain_ref[1:2, :]
        hidden_in[chunk, :] = values
        unit, _ = unit_rows(values)
        n2all[inside(chunk), :] = (unit * gain_ref[2:3, :]).astype(bf)

    some_rows(enter)

    half = rows // 2
    ends = (0, P - 1)

    def is_end(p):
        return (p == 0) | (p == P - 1)

    def upper(p, y):
        return pl.ds(pl.multiple_of((p * 2 + y) * rows, half), half)

    def lower(p, y):
        return pl.ds(pl.multiple_of((p * 2 + y) * rows + half, half), half)

    def gather(buf, turn, compute):
        def y_copy(p, y):
            view = buf.at[block(p, y)]
            return remote(view, view, ag_ys.at[turn, p], ag_yr.at[turn, p], partner)

        def y_half(p, y):
            view = buf.at[upper(p, y)]
            return remote(view, view, ag_ys.at[turn, p], ag_yr.at[turn, p], partner)

        def side_copy(number):
            view = buf.at[lower(ends[number], 1 - y0)]
            return remote(
                view,
                view,
                ag_bs.at[turn, number],
                ag_br.at[turn, number],
                (right, left)[number],
            )

        passes = (has_right, has_left)
        send, arrived, drain_z = line_copies(
            lambda p: buf.at[block(p, y0)],
            p0,
            right,
            left,
            has_right,
            has_left,
            ag_zs.at[turn],
            ag_zr.at[turn],
        )
        send(p0)
        y_copy(p0, y0).start()
        if turn == 0:
            for copy in pushes:
                copy.start()

        def inside_line(p):
            return (p >= 0) & (p < P)

        def step(s, carry):
            for p in (p0 - s, p0 + s):

                @pl.when(inside_line(p))
                def _():
                    arrived(p)
                    send(p)

                @pl.when(inside_line(p) & is_end(p))
                def _():
                    y_half(p, y0).start()

                @pl.when(inside_line(p) & ~is_end(p))
                def _():
                    y_copy(p, y0).start()

            for number in range(2):

                @pl.when((s > 1) & ((ends[number] - p0 == s - 1) | (p0 - ends[number] == s - 1)))
                def _():
                    side_copy(number).wait_recv()

                    @pl.when(passes[number])
                    def _():
                        side_copy(number).start()

            @pl.when(s == 1)
            def _():
                y_copy(p0, 1 - y0).wait_recv()

                for number in range(2):

                    @pl.when(p0 == ends[number])
                    def _():
                        side_copy(number).start()

            compute.before(s)

            def one(way, carry):
                q = p0 + (2 * way - 1) * (s - 1)

                @pl.when(inside_line(q) & ((s > 1) | (way == 0)))
                def _():
                    @pl.when((s > 1) & is_end(q))
                    def _():
                        y_half(q, 1 - y0).wait_recv()

                    @pl.when((s > 1) & ~is_end(q))
                    def _():
                        y_copy(q, 1 - y0).wait_recv()

                    compute.pair(q, s)

                return carry

            lax.fori_loop(0, 2, one, 0)
            compute.after(s)
            return carry

        lax.fori_loop(1, P + 1, step, 0)

        def drain(p, carry):
            @pl.when(is_end(p) & (p != p0))
            def _():
                y_half(p, y0).wait_send()

            @pl.when(~is_end(p) | (p == p0))
            def _():
                y_copy(p, y0).wait_send()

            drain_z(p)
            return carry

        lax.fori_loop(0, P, drain, 0)
        for number in range(2):

            @pl.when(passes[number])
            def _():
                side_copy(number).wait_send()

    def scatter(turn, beside):
        def y_copy(p):
            return remote(
                part.at[block(p, 1 - y0)],
                yrecv.at[at(p)],
                rs_ys.at[turn, p],
                rs_yr.at[turn, p],
                partner,
            )

        def y_half(p):
            return remote(
                part.at[upper(p, 1 - y0)],
                yrecv.at[pl.ds(pl.multiple_of(p * rows, half), half)],
                rs_ys.at[turn, p],
                rs_yr.at[turn, p],
                partner,
            )

        onward, settle, drain_z = chain_copies(
            lambda p: part.at[block(p, y0)],
            lambda into: zrecv.at[at(into)],
            p0,
            P,
            right,
            left,
            has_right,
            has_left,
            rs_zs.at[turn],
            rs_zr.at[turn],
        )

        def side_copy(number):
            return remote(
                part.at[lower(ends[number], 1 - y0)],
                zhalf.at[number],
                rs_bs.at[turn, number],
                rs_br.at[turn, number],
                (left, right)[number],
            )

        before = (has_right, has_left)

        def side_add(number):
            side_copy(number).wait_recv()
            mine = lower(ends[number], 1 - y0)
            part[mine, :] = (part[mine, :].astype(f32) + zhalf[number].astype(f32)).astype(bf)

        def side_turn(number):
            @pl.when((p0 != ends[number]) & before[number])
            def _():
                side_add(number)

            @pl.when(p0 != ends[number])
            def _():
                side_copy(number).start()

        def y_add(p, carry=None):
            @pl.when(is_end(p) & (p != p0))
            def _():
                y_half(p).wait_recv()
                mine = upper(p, y0)
                part[mine, :] = (
                    part[mine, :].astype(f32)
                    + yrecv[pl.ds(pl.multiple_of(p * rows, half), half), :].astype(f32)
                ).astype(bf)

            @pl.when(~is_end(p) | (p == p0))
            def _():
                y_copy(p).wait_recv()
                mine = block(p, y0)
                part[mine, :] = (part[mine, :].astype(f32) + yrecv[at(p), :].astype(f32)).astype(bf)

        for number in range(2):

            @pl.when((p0 != ends[number]) & ~before[number])
            def _():
                side_copy(number).start()

        def start_y(j, carry):
            p = order(P - 1 - j)

            @pl.when(is_end(p))
            def _():
                y_half(p).start()

            @pl.when(~is_end(p))
            def _():
                y_copy(p).start()

            return carry

        lax.fori_loop(0, P - 1, start_y, 0)

        @pl.when(~is_end(p0))
        def _():
            y_copy(p0).start()

        if beside is not None:
            beside(0)

        @pl.when(p0 < P // 2)
        def _():
            for number in (1, 0):

                @pl.when((p0 != ends[number]) & before[number])
                def _():
                    side_turn(number)

        @pl.when(p0 >= P // 2)
        def _():
            for number in (0, 1):

                @pl.when((p0 != ends[number]) & before[number])
                def _():
                    side_turn(number)

        for j in range(P - 1):
            if beside is not None and j:
                beside(j)
            p = order(P - 1 - j)
            y_add(p)
            onward(p)
            if j == 1:
                for number in range(2):

                    @pl.when(p0 == ends[number])
                    def _():
                        side_add(number)
                        y_copy(p0).start()

        if beside is not None:
            beside(P - 1)
        y_add(p0)
        settle()
        ffn[...] = part[block(p0, y0), :].astype(f32)

        def drain(p, carry):
            @pl.when(is_end(p) & (p != p0))
            def _():
                y_half(p).wait_send()

            @pl.when(~is_end(p) | (p == p0))
            def _():
                y_copy(p).wait_send()

            drain_z(p)
            return carry

        lax.fori_loop(0, P, drain, 0)
        for number in range(2):

            @pl.when(p0 != ends[number])
            def _():
                side_copy(number).wait_send()

    def forward_down(p):
        for first, wide in spans(width, 768):
            cols = slice(first, first + wide)
            part[pair(p), cols] = mm(act[pair(p), :], w[2, :, cols], NN).astype(bf)

    class Forward:
        def before(s):
            @pl.when(s == 1)
            def _():
                for which in (0, 1, 3, 4):
                    local[which].wait()
                    pushes[which].wait_recv()

            @pl.when(s == 3)
            def _():
                local[2].wait()
                pushes[2].wait_recv()
                down_over.wait_recv()

                def early(q, carry):
                    @pl.when((q - p0 < 2) & (p0 - q < 2))
                    def _():
                        forward_down(q)

                    return carry

                lax.fori_loop(0, P, early, 0)

        def pair(p, s):
            feats = n2all[pair(p), :]
            for first, wide in spans(hidden, 256):
                cols = slice(first, first + wide)
                gates = mm(feats, w[0, cols, :], NT)
                ups = mm(feats, w[1, cols, :], NT)
                bent = jnp.tanh(GELU_A * (gates + GELU_B * gates * gates * gates))
                gate[pair(p), cols] = gates.astype(bf)
                up[pair(p), cols] = ups.astype(bf)
                act[pair(p), cols] = (0.5 * gates * (1.0 + bent) * ups).astype(bf)

            @pl.when(s >= 3)
            def _():
                forward_down(p)

        def after(s):
            @pl.when(s == 2)
            def _():
                down_across.wait_recv()
                down_over.start()

    gather(n2all, 0, Forward)
    scatter(0, None)
    gsum_ref[...] = jnp.zeros_like(gsum_ref)

    def leave(chunk):
        unit, inverse = unit_rows(ffn[chunk, :])
        out_ref[chunk, :] = (hidden_in[chunk, :] + unit * gain_ref[3:4, :]).astype(bf)
        upstream = dy_ref[chunk, :].astype(f32)
        gsum_ref[3:4, :] += jnp.sum(upstream * unit, axis=0, keepdims=True)
        pulled = upstream * gain_ref[3:4, :]
        dfall[inside(chunk), :] = (
            inverse * (pulled - unit * jnp.mean(pulled * unit, axis=-1, keepdims=True))
        ).astype(bf)

    some_rows(leave)

    class Backward:
        def before(s):
            return None

        def after(s):
            return None

        def pair(p, s):
            backward(p)

    def backward(p):
        grads = dfall[pair(p), :]
        for first, wide in spans(hidden, 256):
            cols = slice(first, first + wide)
            dact = mm(grads, w[2, cols, :], NT)
            gates = gate[pair(p), cols].astype(f32)
            ups = up[pair(p), cols].astype(f32)
            square = gates * gates
            bent = jnp.tanh(GELU_A * (gates + GELU_B * gates * square))
            half = 0.5 * (1.0 + bent)
            slope = half + 0.5 * gates * (1.0 - bent * bent) * (
                GELU_A * (1.0 + 3.0 * GELU_B * square)
            )
            gate[pair(p), cols] = (dact * ups * slope).astype(bf)
            up[pair(p), cols] = (dact * gates * half).astype(bf)
        for first, wide in spans(width, 768):
            cols = slice(first, first + wide)
            part[pair(p), cols] = (
                mm(gate[pair(p), :], w[0, :, cols], NN) + mm(up[pair(p), :], w[1, :, cols], NN)
            ).astype(bf)

    gather(dfall, 1, Backward)
    for copy in pushes:
        copy.wait_send()
    down_across.wait_send()
    down_over.wait_send()
    pl.semaphore_signal(ready, inc=1, device_id=core, device_id_type=MESH)
    pl.semaphore_wait(ready, 1)
    chunks = spans(width, 768)
    tasks = [(which, number) for which in (2, 0, 1) for number in range(len(chunks))]

    def dw_push(task):
        which, number = tasks[task]
        cols = pl.ds(*chunks[number])
        return remote(
            w.at[which, pl.ds(2 * slot, 2 * slot), cols],
            w.at[which, pl.ds(0, 2 * slot), cols],
            dw_s.at[task],
            dw_r.at[task],
            core,
        )

    def dw_out(which):
        return pltpu.make_async_copy(w.at[which, pl.ds(0, slot)], dwown_ref.at[which], store.at[which])

    def dw_side(which):
        return pltpu.make_async_copy(
            w.at[which, pl.ds(slot, slot)], dwside_ref.at[which], store.at[3 + which]
        )

    dw_down = remote(w.at[2, pl.ds(slot, slot)], dwdown_ref, down_s, down_r, xmate)

    def dw_finish(task):
        which, number = tasks[task]
        first, wide = chunks[number]
        cols = slice(first, first + wide)
        dw_push(task).wait_recv()
        w[which, : 2 * slot, cols] = (
            stage[task % 2].astype(f32) + w[which, : 2 * slot, cols].astype(f32)
        ).astype(bf)
        if number == len(chunks) - 1:
            dw_out(which).start()
            if which == 2:
                dw_down.start()
            else:
                dw_side(which).start()

    def weight_grad(task):
        which, number = tasks[task]
        first, wide = chunks[number]
        left_side = (gate, up, act)[which]
        right_side = (n2all, n2all, dfall)[which]
        summed = mm(left_side[...], right_side[:, first : first + wide], TN)
        w[which, 2 * slot :, first : first + wide] = summed[2 * slot :].astype(bf)
        stage[task % 2] = summed[: 2 * slot].astype(bf)
        dw_push(task).start()
        if task:
            dw_finish(task - 1)

    shares = [range(0, 4), range(4, 6), range(6, 8), range(8, 9)]

    def beside(j):
        if j < len(shares):
            for task in shares[j]:
                weight_grad(task)

    scatter(1, beside)

    def back(chunk):
        unit, inverse = unit_rows(hidden_in[chunk, :])
        grads = ffn[chunk, :]
        gsum_ref[2:3, :] += jnp.sum(grads * unit, axis=0, keepdims=True)
        pulled = grads * gain_ref[2:3, :]
        dres = dy_ref[chunk, :].astype(f32) + inverse * (
            pulled - unit * jnp.mean(pulled * unit, axis=-1, keepdims=True)
        )
        dh_ref[chunk, :] = dres
        unit, inverse = unit_rows(branch_ref[chunk, :])
        gsum_ref[1:2, :] += jnp.sum(dres * unit, axis=0, keepdims=True)
        pulled = dres * gain_ref[1:2, :]
        da_ref[chunk, :] = (
            inverse * (pulled - unit * jnp.mean(pulled * unit, axis=-1, keepdims=True))
        ).astype(bf)

    some_rows(back)
    dw_finish(len(tasks) - 1)
    for task in range(len(tasks)):
        dw_push(task).wait_send()
    for which in range(3):
        dw_out(which).wait()
    for which in range(2):
        dw_side(which).wait()
    dw_down.wait()


def ffn_call(mesh_shape, branch, x, dy, gain, own, across):
    fs = mesh_shape["fsdp"]
    planes = mesh_shape["ctx"] * fs // 8
    rows, width = x.shape
    slot = own.shape[1]
    hidden = 4 * slot
    tokens = planes * 2 * rows
    bf, f32 = jnp.bfloat16, jnp.float32
    vmem = pl.BlockSpec(memory_space=pltpu.VMEM)
    hbm = pl.BlockSpec(memory_space=pl.ANY)
    dma = pltpu.SemaphoreType.DMA
    shape = jax.ShapeDtypeStruct
    return pl.pallas_call(
        functools.partial(ffn_kernel, planes, fs),
        out_shape=(
            shape((rows, width), bf),
            shape((rows, width), f32),
            shape((rows, width), bf),
            shape((8, width), f32),
            shape((3, slot, width), bf),
            shape((2, slot, width), bf),
            shape((slot, width), bf),
        ),
        in_specs=[vmem, vmem, vmem, vmem, hbm, hbm],
        out_specs=(vmem, vmem, vmem, vmem, hbm, hbm, hbm),
        scratch_shapes=[
            pltpu.VMEM((3, hidden, width), bf),
            pltpu.VMEM((rows, width), f32),
            pltpu.VMEM((rows, width), f32),
            pltpu.VMEM((tokens, width), bf),
            pltpu.VMEM((tokens, width), bf),
            pltpu.VMEM((tokens, hidden), bf),
            pltpu.VMEM((tokens, hidden), bf),
            pltpu.VMEM((tokens, hidden), bf),
            pltpu.VMEM((tokens, width), bf),
            pltpu.VMEM((planes * rows, width), bf),
            pltpu.VMEM(((planes + 1) * rows, width), bf),
            pltpu.VMEM((2, rows // 2, width), bf),
            pltpu.VMEM((2, 2 * slot, 768), bf),
            dma((5,)),
            dma((7,)),
            dma((7,)),
            dma((2, planes)),
            dma((2, planes)),
            dma((2, 2, planes)),
            dma((2, planes)),
            dma((2, planes)),
            dma((2, planes)),
            dma((2, planes)),
            dma((2, planes + 1)),
            dma((2, 2)),
            dma((2, 2)),
            dma((2, 2)),
            dma((2, 2)),
            dma((9,)),
            dma((9,)),
            dma,
            dma,
            dma((5,)),
            pltpu.SemaphoreType.REGULAR,
        ],
        compiler_params=pltpu.CompilerParams(
            collective_id=1, has_side_effects=True, vmem_limit_bytes=62 * 2**20
        ),
        name="ffn",
    )(branch, x, dy, gain, own, across)


CONTRACT_ROWS = (((0,), (0,)), ((), ()))
CONTRACT_COLS = (((1,), (1,)), ((), ()))


def from_partner(array, axis, apart):
    return lax.ppermute(array, axis, [(i, i ^ 1 << apart) for i in range(lax.axis_size(axis))])


def normalize(values):
    inverse = lax.rsqrt(jnp.mean(values * values, axis=-1, keepdims=True) + NORM_EPS)
    return (values * inverse, inverse)


def norm_back(unit_values, inverse, grad_unit):
    return inverse * (
        grad_unit - unit_values * jnp.mean(grad_unit * unit_values, axis=-1, keepdims=True)
    )


def row_meta(blocks, prompt):
    offsets = jnp.arange(BLK, dtype=jnp.int32)
    natural = (blocks[:, None] * BLK + offsets[None, :]).reshape(-1)
    group_span = 2 * prompt
    inner_index = natural % group_span
    group_id = natural // group_span
    in_continuation = inner_index >= prompt
    segment = jnp.where(in_continuation, 1 + (inner_index - prompt) // CONT_LEN, 0)
    position = jnp.where(in_continuation, prompt + (inner_index - prompt) % CONT_LEN, inner_index)
    stride = prompt // CONT_LEN + 1
    return (position, group_id * stride + segment, group_id * stride)


def rope_tables(position):
    frequency = 10000.0 ** (-(jnp.arange(HD // 2, dtype=jnp.float32) * 2.0 / HD))
    angles = position.astype(jnp.float32)[:, None] * frequency[None, :]
    return (jnp.cos(angles), jnp.sin(angles))


def rotate(values, cosine, sine_table):
    half_width = values.shape[-1] // 2
    first_half, second_half = (values[..., :half_width], values[..., half_width:])
    cosine, sine_table = (cosine[:, None, :], sine_table[:, None, :])
    return jnp.concatenate(
        [
            first_half * cosine - second_half * sine_table,
            second_half * cosine + first_half * sine_table,
        ],
        axis=-1,
    )


def unrotate(grads, cosine, sine_table):
    half_width = grads.shape[-1] // 2
    first_half, second_half = (grads[..., :half_width], grads[..., half_width:])
    cosine, sine_table = (cosine[:, None, :], sine_table[:, None, :])
    return jnp.concatenate(
        [
            first_half * cosine + second_half * sine_table,
            second_half * cosine - first_half * sine_table,
        ],
        axis=-1,
    )


def pack_gains(gains, me, width):
    own = jnp.stack(gains).astype(jnp.bfloat16).astype(jnp.float32)
    wide = jnp.zeros((8, width), jnp.float32)
    return lax.dynamic_update_slice(wide, own, (0, me * own.shape[1]))


def visible(query_pos, query_doc, query_base, key_pos, key_doc):
    earlier = key_pos[None, :] <= query_pos[:, None]
    shared = (key_doc[None, :] == query_doc[:, None]) | (key_doc[None, :] == query_base[:, None])
    return earlier & shared


def gated(gate_values, up_values):
    return jax.nn.gelu(gate_values, approximate=True) * up_values


def ffn_gathered(hidden_res, normed_h, upstream, gain_four, w_gate, w_up, w_down):
    bfloat = jnp.bfloat16
    pair_weights = jnp.stack([w_gate, w_up]).astype(bfloat)
    down_local = w_down.astype(bfloat)
    gate_up = jnp.einsum(
        "rd,sdf->rsf",
        lax.all_gather(normed_h, ("ctx", "fsdp"), axis=0, tiled=True),
        pair_weights,
        preferred_element_type=jnp.float32,
    )
    activated = gated(gate_up[:, 0], gate_up[:, 1]).astype(bfloat)
    part_rows = activated
    ffn_raw = lax.psum_scatter(
        jnp.dot(part_rows, down_local, preferred_element_type=jnp.float32).astype(bfloat),
        ("ctx", "fsdp"),
        scatter_dimension=0,
        tiled=True,
    ).astype(jnp.float32)
    unit_f, inv_f = normalize(ffn_raw)
    layer_out = (hidden_res + unit_f * gain_four).astype(bfloat)
    grad_four = jnp.sum(upstream * unit_f, axis=0)
    grad_ffn = norm_back(unit_f, inv_f, upstream * gain_four).astype(bfloat)
    grad_piece = lax.all_gather(grad_ffn, ("ctx", "fsdp"), axis=0, tiled=True)
    normed_piece = lax.all_gather(normed_h, ("ctx", "fsdp"), axis=0, tiled=True)
    act_grad = lax.dot_general(
        grad_piece, down_local, CONTRACT_COLS, preferred_element_type=jnp.float32
    )
    pull_piece = jax.vjp(gated, gate_up[:, 0], gate_up[:, 1])[1]
    gate_grad, up_grad = pull_piece(act_grad)
    pair_low = jnp.stack([gate_grad, up_grad], axis=1).astype(bfloat)
    down_sum = lax.dot_general(
        activated, grad_piece, CONTRACT_ROWS, preferred_element_type=jnp.float32
    )
    pair_sum = jnp.einsum("nd,nsf->sdf", normed_piece, pair_low, preferred_element_type=jnp.float32)
    grad_gate = pair_sum[0]
    grad_up = pair_sum[1]
    part_rows = pair_low
    grad_normed_h = lax.psum_scatter(
        jnp.einsum("nsf,sdf->nd", part_rows, pair_weights, preferred_element_type=jnp.float32).astype(bfloat),
        ("ctx", "fsdp"),
        scatter_dimension=0,
        tiled=True,
    ).astype(jnp.float32)
    return (layer_out, grad_normed_h, grad_four, grad_gate, grad_up, down_sum)


def on_device(
    tokens_in,
    block_table,
    w_query,
    w_key,
    w_value,
    w_output,
    w_gate,
    w_up,
    w_down,
    gain_attn_in,
    gain_attn_out,
    gain_ffn_in,
    gain_ffn_out,
    cotangent,
):
    row_count, model_width = tokens_in.shape
    devices = lax.axis_size(("ctx", "fsdp"))
    slot_count = block_table.shape[0] // devices
    prompt = 2 * devices * BLK
    all_rows = row_count * devices
    device_here = lax.axis_index(("ctx", "fsdp"))
    head_count = w_query.shape[1] // HD
    kv_count = w_key.shape[1] // HD
    groups = head_count // kv_count
    score_scale = HD ** (-0.5)
    bfloat = jnp.bfloat16
    gathered = (
        lax.all_gather(w_query.astype(bfloat), ("ctx", "fsdp"), axis=0, tiled=True),
        lax.all_gather(w_key.astype(bfloat), ("ctx", "fsdp"), axis=0, tiled=True),
        lax.all_gather(w_value.astype(bfloat), ("ctx", "fsdp"), axis=0, tiled=True),
        lax.all_gather(w_output.astype(bfloat), ("ctx", "fsdp"), axis=1, tiled=True),
        lax.all_gather(gain_attn_in.astype(bfloat), ("ctx", "fsdp"), axis=0, tiled=True),
        lax.all_gather(gain_attn_out.astype(bfloat), ("ctx", "fsdp"), axis=0, tiled=True),
        lax.all_gather(gain_ffn_in.astype(bfloat), ("ctx", "fsdp"), axis=0, tiled=True),
        lax.all_gather(gain_ffn_out.astype(bfloat), ("ctx", "fsdp"), axis=0, tiled=True),
    )
    query_weight, key_weight, value_weight, output_weight = (
        gathered[0],
        gathered[1],
        gathered[2],
        gathered[3],
    )
    gain_one = gathered[4].astype(jnp.float32)
    gain_two = gathered[5].astype(jnp.float32)
    gain_three = gathered[6].astype(jnp.float32)
    gain_four = gathered[7].astype(jnp.float32)
    key_meta = row_meta(block_table, prompt)
    key_pos, key_doc = (key_meta[0], key_meta[1])
    my_blocks = lax.dynamic_slice_in_dim(block_table, device_here * slot_count, slot_count)
    query_pos, query_doc, query_base = row_meta(my_blocks, prompt)
    cosine, sine_table = rope_tables(query_pos)
    inputs = tokens_in.astype(jnp.float32)
    unit_x, inv_x = normalize(inputs)
    normed_x = (unit_x * gain_one).astype(bfloat)
    query_raw = jnp.dot(normed_x, query_weight, preferred_element_type=jnp.float32).reshape(
        row_count, head_count, HD
    )
    queries = (
        rotate(query_raw, cosine, sine_table)
        .astype(bfloat)
        .reshape(row_count, kv_count, groups, HD)
    )
    key_raw = jnp.dot(normed_x, key_weight, preferred_element_type=jnp.float32).reshape(
        row_count, kv_count, HD
    )
    keys = rotate(key_raw, cosine, sine_table).astype(bfloat)
    values = (
        jnp.dot(normed_x, value_weight, preferred_element_type=jnp.float32)
        .reshape(row_count, kv_count, HD)
        .astype(bfloat)
    )

    def key_block_meta(first_row, block_width):
        block_pos = lax.dynamic_slice_in_dim(key_pos, first_row, block_width)
        block_doc = lax.dynamic_slice_in_dim(key_doc, first_row, block_width)
        return visible(query_pos, query_doc, query_base, block_pos, block_doc)[:, None, None, :]

    def bent_scores(key_block):
        scores = jnp.einsum(
            "rgjd,kgd->rgjk", queries, key_block, preferred_element_type=jnp.float32
        )
        return jnp.tanh(scores * (score_scale / SOFT_CAP))

    start_state = (
        jnp.full((row_count, kv_count, groups), MASKED, jnp.float32),
        jnp.zeros((row_count, kv_count, groups), jnp.float32),
        jnp.zeros((row_count, kv_count, groups, HD), jnp.float32),
    )
    key_piece = lax.all_gather(keys, ("ctx", "fsdp"), axis=0, tiled=True)
    value_piece = lax.all_gather(values, ("ctx", "fsdp"), axis=0, tiled=True)
    piece_rows = key_piece.shape[0]
    block_width = math.gcd(piece_rows, KBLK)

    def attend_block_step(block_index, state):
        running_max, running_sum, running_out = state
        offset = block_index * block_width
        key_block = lax.dynamic_slice_in_dim(key_piece, offset, block_width, 0)
        value_block = lax.dynamic_slice_in_dim(value_piece, offset, block_width, 0)
        allowed = key_block_meta(offset, block_width)
        capped = jnp.where(allowed, SOFT_CAP * bent_scores(key_block), MASKED)
        fresh_max = jnp.maximum(running_max, jnp.max(capped, axis=-1))
        decay = jnp.exp(running_max - fresh_max)
        weights_soft = jnp.where(allowed, jnp.exp(capped - fresh_max[..., None]), 0.0)
        running_sum = running_sum * decay + jnp.sum(weights_soft, axis=-1)
        running_out = running_out * decay[..., None] + jnp.einsum(
            "rgjk,kgd->rgjd",
            weights_soft.astype(bfloat),
            value_block,
            preferred_element_type=jnp.float32,
        )
        return (fresh_max, running_sum, running_out)

    running_max, running_sum, running_out = lax.fori_loop(
        0, piece_rows // block_width, attend_block_step, start_state
    )
    log_total = running_max + jnp.log(running_sum)
    attended = (running_out / running_sum[..., None]).reshape(row_count, head_count * HD)
    attended_low = attended.astype(bfloat)
    branch_raw = jnp.dot(attended_low, output_weight, preferred_element_type=jnp.float32)
    unit_a, inv_a = normalize(branch_raw)
    hidden_res = inputs + unit_a * gain_two
    unit_h, inv_h = normalize(hidden_res)
    normed_h = (unit_h * gain_three).astype(bfloat)
    upstream = cotangent.astype(jnp.float32)
    layer_out, grad_normed_h, grad_four, grad_gate, grad_up, down_sum = ffn_gathered(
        hidden_res, normed_h, upstream, gain_four, w_gate, w_up, w_down
    )
    grad_three = jnp.sum(grad_normed_h * unit_h, axis=0)
    grad_res = upstream + norm_back(unit_h, inv_h, grad_normed_h * gain_three)
    grad_two = jnp.sum(grad_res * unit_a, axis=0)
    grad_branch = norm_back(unit_a, inv_a, grad_res * gain_two).astype(bfloat)
    grad_att = lax.dot_general(
        grad_branch, output_weight, CONTRACT_COLS, preferred_element_type=jnp.float32
    ).astype(bfloat)
    grad_heads = grad_att.reshape(row_count, kv_count, groups, HD)
    row_delta = jnp.sum(
        grad_heads.astype(jnp.float32) * attended.reshape(row_count, kv_count, groups, HD), axis=-1
    )
    begin_state = (
        jnp.zeros((row_count, kv_count, groups, HD), jnp.float32),
        jnp.zeros((all_rows, kv_count, HD), jnp.float32),
        jnp.zeros((all_rows, kv_count, HD), jnp.float32),
    )
    retrace_key_piece = lax.all_gather(keys, ("ctx", "fsdp"), axis=0, tiled=True)
    retrace_value_piece = lax.all_gather(values, ("ctx", "fsdp"), axis=0, tiled=True)
    piece_rows = retrace_key_piece.shape[0]
    retrace_block_width = math.gcd(piece_rows, KBLK)

    def retrace_block_step(block_index, state):
        query_sum, key_sums, value_sums = state
        offset = block_index * retrace_block_width
        key_block = lax.dynamic_slice_in_dim(retrace_key_piece, offset, retrace_block_width, 0)
        value_block = lax.dynamic_slice_in_dim(retrace_value_piece, offset, retrace_block_width, 0)
        allowed = key_block_meta(offset, retrace_block_width)
        bent = bent_scores(key_block)
        weights_soft = jnp.where(allowed, jnp.exp(SOFT_CAP * bent - log_total[..., None]), 0.0)
        value_dots = jnp.einsum(
            "rgjd,kgd->rgjk", grad_heads, value_block, preferred_element_type=jnp.float32
        )
        score_grad = (
            weights_soft * (value_dots - row_delta[..., None]) * (1.0 - bent * bent) * score_scale
        ).astype(bfloat)
        query_sum = query_sum + jnp.einsum(
            "rgjk,kgd->rgjd", score_grad, key_block, preferred_element_type=jnp.float32
        )
        key_part = jnp.einsum(
            "rgjk,rgjd->kgd", score_grad, queries, preferred_element_type=jnp.float32
        )
        value_part = jnp.einsum(
            "rgjk,rgjd->kgd",
            weights_soft.astype(bfloat),
            grad_heads,
            preferred_element_type=jnp.float32,
        )
        key_sums = lax.dynamic_update_slice_in_dim(key_sums, key_part, offset, 0)
        value_sums = lax.dynamic_update_slice_in_dim(value_sums, value_part, offset, 0)
        return (query_sum, key_sums, value_sums)

    query_sum, key_sums, value_sums = lax.fori_loop(
        0, piece_rows // retrace_block_width, retrace_block_step, begin_state
    )
    mate_count = CONT_LEN // (2 * BLK)
    tail_shape = key_sums.shape[1:]
    key_slots = key_sums.reshape((devices, slot_count, BLK) + tail_shape)
    value_slots = value_sums.reshape((devices, slot_count, BLK) + tail_shape)
    prompt_rows = 2 * BLK * devices
    key_head, value_head = (
        lax.psum_scatter(
            key_slots[:, :2].reshape((prompt_rows,) + tail_shape),
            ("ctx", "fsdp"),
            scatter_dimension=0,
            tiled=True,
        ),
        lax.psum_scatter(
            value_slots[:, :2].reshape((prompt_rows,) + tail_shape),
            ("ctx", "fsdp"),
            scatter_dimension=0,
            tiled=True,
        ),
    )
    group_start = device_here // mate_count * mate_count
    later_both = jnp.stack(
        [
            lax.dynamic_slice_in_dim(key_slots[:, 2:], group_start, mate_count, 0),
            lax.dynamic_slice_in_dim(value_slots[:, 2:], group_start, mate_count, 0),
        ],
        axis=1,
    )
    rank_inner = device_here % mate_count
    for level in reversed(range(mate_count.bit_length() - 1)):
        half_count = later_both.shape[0] // 2
        upper_side = rank_inner >> level & 1 == 1
        lower_half = later_both[:half_count]
        upper_half = later_both[half_count:]
        kept = jnp.where(upper_side, upper_half, lower_half)
        given = jnp.where(upper_side, lower_half, upper_half)
        later_both = kept + from_partner(given.astype(jnp.bfloat16), ("ctx", "fsdp"), level).astype(
            given.dtype
        )
    key_mine = jnp.concatenate(
        [key_head, later_both[0, 0].reshape((2 * BLK,) + tail_shape)], axis=0
    )
    value_mine = jnp.concatenate(
        [value_head, later_both[0, 1].reshape((2 * BLK,) + tail_shape)], axis=0
    )
    grad_q = (
        unrotate(query_sum.reshape(row_count, head_count, HD), cosine, sine_table)
        .reshape(row_count, head_count * HD)
        .astype(bfloat)
    )
    grad_k = unrotate(key_mine, cosine, sine_table).reshape(row_count, kv_count * HD).astype(bfloat)
    grad_v = value_mine.reshape(row_count, kv_count * HD).astype(bfloat)
    grad_normed_x = lax.dot_general(
        grad_q, query_weight, CONTRACT_COLS, preferred_element_type=jnp.float32
    )
    grad_normed_x = grad_normed_x + lax.dot_general(
        grad_k, key_weight, CONTRACT_COLS, preferred_element_type=jnp.float32
    )
    grad_normed_x = grad_normed_x + lax.dot_general(
        grad_v, value_weight, CONTRACT_COLS, preferred_element_type=jnp.float32
    )
    grad_one = jnp.sum(grad_normed_x * unit_x, axis=0)
    grad_in = (grad_res + norm_back(unit_x, inv_x, grad_normed_x * gain_one)).astype(bfloat)
    projection_grads = jnp.concatenate([grad_q, grad_k, grad_v], axis=1)
    input_term = lax.dot_general(
        normed_x, projection_grads, CONTRACT_ROWS, preferred_element_type=jnp.float32
    )
    output_term = lax.dot_general(
        grad_branch, attended_low, CONTRACT_ROWS, preferred_element_type=jnp.float32
    )
    input_share, output_share, share_one, share_two, share_three, share_four = (
        lax.psum_scatter(input_term, ("ctx", "fsdp"), scatter_dimension=0, tiled=True),
        lax.psum_scatter(output_term, ("ctx", "fsdp"), scatter_dimension=0, tiled=True),
        lax.psum_scatter(grad_one, ("ctx", "fsdp"), scatter_dimension=0, tiled=True),
        lax.psum_scatter(grad_two, ("ctx", "fsdp"), scatter_dimension=0, tiled=True),
        lax.psum_scatter(grad_three, ("ctx", "fsdp"), scatter_dimension=0, tiled=True),
        lax.psum_scatter(grad_four, ("ctx", "fsdp"), scatter_dimension=0, tiled=True),
    )
    query_cols = head_count * HD
    key_cols = kv_count * HD
    grad_query = input_share[:, :query_cols]
    grad_key = input_share[:, query_cols : query_cols + key_cols]
    grad_value = input_share[:, query_cols + key_cols :]
    grad_output = output_share.T
    return (
        layer_out,
        grad_in,
        grad_query,
        grad_key,
        grad_value,
        grad_output,
        grad_gate,
        grad_up,
        down_sum,
        share_one,
        share_two,
        share_three,
        share_four,
    )


def kernels_fit(mesh_shape, rows, width, slot):
    planes = mesh_shape["ctx"] * mesh_shape["fsdp"] // 8
    tokens, hidden = planes * 2 * rows, 4 * slot
    wide_rows = 3 * hidden + 3 * tokens + (2 * planes + 1) * rows
    held = 2 * width * wide_rows + 6 * tokens * hidden + 2 * 2 * 768 * hidden
    return rows == 128 and planes == 4 and slot % 16 == 0 and held < 48 * 2**20


def on_device_kernels(
    mesh_shape,
    tokens_in,
    block_table,
    w_query,
    w_key,
    w_value,
    w_output,
    w_gate,
    w_up,
    w_down,
    gain_attn_in,
    gain_attn_out,
    gain_ffn_in,
    gain_ffn_out,
    cotangent,
):
    axes = ("ctx", "fsdp")
    bf, f32 = jnp.bfloat16, jnp.float32
    rows, width = tokens_in.shape
    shard = w_query.shape[0]
    me = lax.axis_index(axes)
    gains = pack_gains((gain_attn_in, gain_attn_out, gain_ffn_in, gain_ffn_out), me, width)
    split = (2, rows // 2, width)
    x = tokens_in.reshape(split)
    across, branch, *saved, gains, own = attend_call(
        mesh_shape,
        x,
        w_query,
        w_key,
        w_value,
        w_output,
        gains,
        block_table,
        w_gate,
        w_up,
        w_down,
    )
    layer_out, grad_res, grad_branch, sums, mine, side, down = ffn_call(
        mesh_shape, branch.reshape(rows, width), tokens_in, cotangent, gains, own, across
    )
    grad_in, pieces, sums, side = retrace_call(
        mesh_shape,
        shard,
        grad_branch.reshape(split),
        grad_res.reshape(split),
        x,
        gains,
        sums,
        block_table,
        saved,
        side,
    )
    pieces = pieces[:, :, :shard].astype(f32).transpose(2, 1, 0, 3)
    pairs = pieces[:, 0].reshape(shard, -1, 2, HD)
    grad_key = pairs[:, :, 0].reshape(w_key.shape)
    grad_value = pairs[:, :, 1].reshape(w_value.shape)
    grad_query = pieces[:, 1].reshape(w_query.shape)
    grad_output = pieces[:, 2].reshape(shard, -1).T
    grad_one = (
        jnp.sum(w_query.astype(bf).astype(f32) * grad_query, axis=1)
        + jnp.sum(w_key.astype(bf).astype(f32) * grad_key, axis=1)
        + jnp.sum(w_value.astype(bf).astype(f32) * grad_value, axis=1)
    ) / gain_attn_in.astype(bf).astype(f32)
    shares = lax.dynamic_slice(sums, (1, me * shard), (3, shard))
    return (
        layer_out,
        grad_in.reshape(rows, width),
        grad_query,
        grad_key,
        grad_value,
        grad_output,
        (mine[0].astype(f32) + side[0].astype(f32)).T,
        (mine[1].astype(f32) + side[1].astype(f32)).T,
        mine[2].astype(f32) + down.astype(f32),
        grad_one,
        shares[0],
        shares[1],
        shares[2],
    )


def solution(mesh):
    placed = (
        P(("ctx", "fsdp"), None),
        P(),
        P(("ctx", "fsdp"), None),
        P(("ctx", "fsdp"), None),
        P(("ctx", "fsdp"), None),
        P(None, ("ctx", "fsdp")),
        P(None, ("ctx", "fsdp")),
        P(None, ("ctx", "fsdp")),
        P(("ctx", "fsdp"), None),
        P(("ctx", "fsdp")),
        P(("ctx", "fsdp")),
        P(("ctx", "fsdp")),
        P(("ctx", "fsdp")),
        P(("ctx", "fsdp"), None),
    )
    shape = dict(mesh.shape)

    def program(tokens_in, *others):
        devices = shape["ctx"] * shape["fsdp"]
        rows, width = tokens_in.shape
        slot = others[7].shape[0] // devices
        if kernels_fit(shape, rows // devices, width, slot):
            body = functools.partial(on_device_kernels, shape)
        else:
            body = on_device
        return placed_over(mesh, placed, body)(tokens_in, *others)

    return program


def placed_over(mesh, placed, body):
    return jax.shard_map(
        body,
        mesh=mesh,
        in_specs=placed,
        out_specs=(
            P(("ctx", "fsdp"), None),
            P(("ctx", "fsdp"), None),
            P(("ctx", "fsdp"), None),
            P(("ctx", "fsdp"), None),
            P(("ctx", "fsdp"), None),
            P(None, ("ctx", "fsdp")),
            P(None, ("ctx", "fsdp")),
            P(None, ("ctx", "fsdp")),
            P(("ctx", "fsdp"), None),
            P(("ctx", "fsdp")),
            P(("ctx", "fsdp")),
            P(("ctx", "fsdp")),
            P(("ctx", "fsdp")),
        ),
        check_vma=False,
    )
```
